256 devices in a mesh: row: 16 (over x, y), col: 16 (over z, core).
Axes of the slice: x: 4, y: 4, z: 8, core: 2. Of those that a mesh axis runs over, the one named last changes fastest.
Arguments:
- tokens: bfloat16 [512, 16384], P('col', 'row'), may hold values from -6 to 6
- weight: bfloat16 [16384, 53248], P('row', 'col')
- down_adapter: float32 [16384, 16], P('row'), may hold values from -0.046875 to 0.046875
- up_adapter: float32 [16, 53248], P(None, 'col'), may hold values from -0.75 to 0.75
- magnitude: float32 [53248], P('col'), may hold values from 0.5 to 2
- out_cotangent: bfloat16 [512, 53248], P('row', 'col')
Outputs:
- output: bfloat16 [512, 53248], P('row', 'col')
- grad_tokens: bfloat16 [512, 16384], P('col', 'row')
- grad_magnitude: float32 [53248], P('col')
- up_gradient: float32 [16, 53248], P(None, 'col')
- down_gradient: float32 [16384, 16], P('row')
The draws below stay inside these ranges and needn't reach their ends.
All inputs are finite; a program needn't handle non-finite values.
Results may differ from the reference program's by a relative error of at most 0.0058.
Values may be sent and summed in bfloat16 or wider, within the bound.
No kernel may reach another device: no remote copies, remote signals or barrier semaphores. Data moves between devices by JAX's collectives and lax.ppermute only.
A program may use at most 128 MiB of HBM per device.

```python
import math
import jax
import jax.numpy as jnp
from jax import lax

D = 16384
F = 53248
RANK = 16
TOKENS = 512


def draw_weight(key, part):
    key = jax.random.fold_in(key, 11)
    key_values, key_rows, key_cols = jax.random.split(key, 3)
    rising = jnp.power(3.0, jnp.arange(D, dtype=jnp.float32) / D)
    values = jnp.clip(jax.random.normal(key_values, (D, F), jnp.float32), -6.0, 6.0)
    row_scale = jnp.power(10.0, jax.random.uniform(key_rows, (D, 1), jnp.float32))
    col_scale = jnp.power(10.0, jax.random.uniform(key_cols, (1, F), jnp.float32))
    result = values * row_scale * rising[:, None] * col_scale / (10.0 * math.sqrt(D))
    return result.astype(jnp.bfloat16)


def draw_out_cotangent(key, part):
    key = jax.random.fold_in(key, 12)
    rising = jnp.power(3.0, jnp.arange(TOKENS, dtype=jnp.float32) / TOKENS)
    values = jnp.clip(jax.random.normal(key, (TOKENS, F), jnp.float32), -6.0, 6.0)
    return (0.05 * values * rising[:, None]).astype(jnp.bfloat16)


def strengthened(entries, own_key, source, target, shards_of, factor):
    owner, partner = [(jnp.arange(entries.shape[axis_at]) // (entries.shape[axis_at] // shards_of)).reshape([-1 if axis == axis_at else 1 for axis in range(entries.ndim)]) for axis_at in (source, target)]
    chosen = jax.random.permutation(own_key, shards_of)[partner]
    strong = (owner == chosen) | (owner == (partner + shards_of // 2) % shards_of)
    return jnp.where(strong, factor * entries, entries)


def shard_levels(own_key, dims, shards, smallest, top_value):
    loudness = 1.0
    for position, parts in shards:
        draws = jax.random.uniform(jax.random.fold_in(jax.random.fold_in(own_key, 6), position), (parts,), jnp.float32, smallest / len(shards), top_value / len(shards))
        loudness = loudness * jnp.repeat(jnp.exp(draws), dims[position] // parts).reshape((-1,) + (1,) * (len(dims) - 1 - position))
    return loudness


def scatter_about(stream_key, dims, deviation, bound, cuts=(), kind=jnp.bfloat16):
    gain = shard_levels(stream_key, dims, cuts, -0.22, 0.18) if cuts else 1.0
    values = jax.random.normal(stream_key, dims, jnp.float32) * deviation * gain
    return jnp.minimum(jnp.maximum(values, -bound), bound).astype(kind)


def bell_draw_with(key, extent, scale, most, shards, heavy, kind=jnp.bfloat16):
    values = scale * jax.random.normal(key, extent, jnp.float32)
    if shards:
        values = values * shard_levels(key, extent, shards, -0.22, 0.18)
    return jnp.clip(strengthened(values, jax.random.fold_in(key, 3), *heavy), -most, most).astype(kind)


def setup_inputs(seed: int = 0) -> dict:
    seeds = jax.random.split(jax.random.key(seed), 7)
    tokens = bell_draw_with(seeds[0], (TOKENS, D), 1.0, 6.0, ((0, 16), (1, 16)), (1, 0, 16, 2.0))
    weight = draw_weight(jax.random.fold_in(seeds[6], 71), 0)
    down_adapter = scatter_about(seeds[2], (D, RANK), D ** -0.5, 0.046875, ((0, 16),), jnp.float32)
    up_adapter = scatter_about(seeds[3], (RANK, F), (4 * RANK) ** -0.5, 0.75, ((1, 16),), jnp.float32)
    magnitude = jnp.clip(jnp.exp(math.log(2.0) - 1.3862944 * jax.random.uniform(seeds[4], (F,), jnp.float32) ** shard_levels(seeds[4], (F,), ((0, 16),), -0.2, 0.2)), 0.5, 2.0)
    out_cotangent = draw_out_cotangent(jax.random.fold_in(seeds[6], 71), 0)
    return {"tokens": tokens, "weight": weight, "down_adapter": down_adapter, "up_adapter": up_adapter, "magnitude": magnitude, "out_cotangent": out_cotangent}


adapter_scale = 2.0
epsilon = 1e-06
highest = lax.Precision.HIGHEST

def contract_last(left, right, precision=None, preferred_element_type=None):
    return lax.dot_general(left, right, (((1,), (1,)), ((), ())), precision=precision, preferred_element_type=preferred_element_type)

def reference(tokens, weight, down_adapter, up_adapter, magnitude, out_cotangent):
    blocks = 16
    width = F // blocks
    tokens_float = tokens.astype(jnp.float32)
    cotangent = out_cotangent.astype(jnp.float32)
    adapter_proj = jnp.dot(tokens_float, down_adapter, precision=highest)

    def step(carry, index):
        grad_total, low_total = carry
        start = (index * width).astype(jnp.int32)
        block_weight = lax.dynamic_slice_in_dim(weight, start, width, 1)
        block_up = lax.dynamic_slice_in_dim(up_adapter, start, width, 1)
        block_mag = lax.dynamic_slice_in_dim(magnitude, start, width, 0)
        block_cot = lax.dynamic_slice_in_dim(cotangent, start, width, 1)
        merged = block_weight.astype(jnp.float32) + adapter_scale * jnp.dot(down_adapter, block_up, precision=highest)
        column_norm = jnp.sqrt(lax.optimization_barrier(jnp.sum(merged * merged, axis=0)) + epsilon)
        merged_low = merged.astype(jnp.bfloat16)
        summed = jnp.dot(tokens, merged_low, preferred_element_type=jnp.float32)
        factor = block_mag / column_norm
        output = (summed * factor).astype(jnp.bfloat16)
        grad_rows = (block_cot * factor).astype(jnp.bfloat16)
        grad_total = grad_total + contract_last(grad_rows, merged_low, preferred_element_type=jnp.float32)
        grad_float = grad_rows.astype(jnp.float32)
        low_total = low_total + contract_last(grad_float, block_up, precision=highest)
        grad_mag = lax.optimization_barrier(jnp.sum(block_cot * summed, axis=0)) / column_norm
        up_grad = adapter_scale * lax.dot_general(adapter_proj, grad_float, (((0,), (0,)), ((), ())), precision=highest)
        return ((grad_total, low_total), (output, grad_mag, up_grad))
    start_carry = (jnp.zeros((TOKENS, D), jnp.float32), jnp.zeros((TOKENS, RANK), jnp.float32))
    indices = jnp.arange(blocks, dtype=jnp.int32)
    (grad_total, low_total), (outputs, grad_mags, up_grads) = lax.scan(step, start_carry, indices)
    output = jnp.transpose(outputs, (1, 0, 2)).reshape(TOKENS, F)
    grad_magnitude = grad_mags.reshape(F)
    up_gradient = jnp.transpose(up_grads, (1, 0, 2)).reshape(RANK, F)
    down_gradient = adapter_scale * lax.dot_general(tokens_float, low_total, (((0,), (0,)), ((), ())), precision=highest)
    return (output, grad_total.astype(jnp.bfloat16), grad_magnitude, up_gradient, down_gradient)
```

```python
import jax
import jax.numpy as jnp
from jax import lax
from jax.experimental import pallas as pl
from jax.experimental.pallas import tpu as pltpu
from jax.sharding import Mesh
from jax.sharding import PartitionSpec as P

adapter_scale = 2.0
epsilon = 1e-06
bf16 = jnp.bfloat16
f32 = jnp.float32
ROW = ("x", "y")
COL = ("z", "c")
TILE = 256
VMEM = 56 * 1024 * 1024


def pieces(value):
    high = value.astype(bf16)
    rest = value - high.astype(f32)
    mid = rest.astype(bf16)
    low = (rest - mid.astype(f32)).astype(bf16)
    return high, mid, low


def dot(left, right, left_dim, right_dim):
    return lax.dot_general(
        left, right, (((left_dim,), (right_dim,)), ((), ())), preferred_element_type=f32
    )


def params(semantics=("arbitrary",)):
    return pltpu.CompilerParams(dimension_semantics=semantics, vmem_limit_bytes=VMEM)


def merge_kernel(down_ref, up_ref, weight_ref, merged_ref, sums_ref, up_cat, totals):
    step = pl.program_id(0)
    rows, width = weight_ref.shape

    @pl.when(step == 0)
    def _():
        totals[...] = jnp.zeros_like(totals)
        for start in range(0, width, TILE):
            cols = slice(start, start + TILE)
            u1, u2, u3 = pieces(up_ref[:, cols])
            up_cat[:, cols] = jnp.concatenate([u1, u2, u1, u3, u1, u2], axis=0)

    d1, d2, d3 = pieces(down_ref[...] * adapter_scale)
    down_cat = jnp.concatenate([d1, d1, d2, d1, d3, d2], axis=0)
    for start in range(0, width, TILE):
        cols = slice(start, start + TILE)
        merged = weight_ref[:, cols].astype(f32) + dot(down_cat, up_cat[:, cols], 0, 0)
        merged_ref[:, cols] = merged.astype(bf16)
        totals[:, cols] += jnp.sum((merged * merged).reshape(rows // 8, 8, TILE), axis=0)

    @pl.when(step == pl.num_programs(0) - 1)
    def _():
        sums_ref[...] = jnp.sum(totals[...], axis=0, keepdims=True)


def merge(down_t, up, weight):
    depth, width = weight.shape
    rows = 256
    return pl.pallas_call(
        merge_kernel,
        grid=(depth // rows,),
        in_specs=[
            pl.BlockSpec((16, rows), lambda i: (0, i)),
            pl.BlockSpec((16, width), lambda i: (0, 0)),
            pl.BlockSpec((rows, width), lambda i: (i, 0)),
        ],
        out_specs=[
            pl.BlockSpec((rows, width), lambda i: (i, 0)),
            pl.BlockSpec((1, width), lambda i: (0, 0)),
        ],
        out_shape=[
            jax.ShapeDtypeStruct((depth, width), bf16),
            jax.ShapeDtypeStruct((1, width), f32),
        ],
        scratch_shapes=[pltpu.VMEM((96, width), bf16), pltpu.VMEM((8, width), f32)],
        compiler_params=params(),
        cost_estimate=pl.CostEstimate(
            flops=12 * depth * width, bytes_accessed=4 * depth * width, transcendentals=0
        ),
        name="merge",
    )(down_t, up, weight)


def forward_kernel(core_ref, own_ref, other_ref, down_ref, merged_ref, part_ref, tokens_ref, adapter_ref):
    core = core_ref[0]
    blocks = own_ref.shape[0]
    depth = own_ref.shape[2]

    @pl.when(pl.program_id(0) == 0)
    def _():
        d1, d2, d3 = pieces(down_ref[...])
        down_cat = jnp.concatenate([d1, d2, d3], axis=0)
        for source, parity in ((own_ref, core), (other_ref, 1 - core)):
            proj = dot(source[...].reshape(-1, depth), down_cat, 1, 1)
            proj = proj[:, :16] + proj[:, 16:32] + proj[:, 32:48]
            for z in range(blocks):
                tokens_ref[2 * z + parity] = source[z]
                adapter_ref[2 * z + parity] = proj[32 * z : 32 * z + 32]

    for source, parity in ((own_ref, core), (other_ref, 1 - core)):
        out = dot(source[...].reshape(-1, depth), merged_ref[...], 1, 0).astype(bf16)
        for z in range(blocks):
            part_ref[2 * z + parity] = out[32 * z : 32 * z + 32]


def forward(core, own, other, down_t, merged_low):
    blocks, size, depth = own.shape
    width = merged_low.shape[1]
    whole = lambda i, c: (0, 0, 0)
    return pl.pallas_call(
        forward_kernel,
        grid_spec=pltpu.PrefetchScalarGridSpec(
            num_scalar_prefetch=1,
            grid=(width // TILE,),
            in_specs=[
                pl.BlockSpec((blocks, size, depth), whole),
                pl.BlockSpec((blocks, size, depth), whole),
                pl.BlockSpec((16, depth), lambda i, c: (0, 0)),
                pl.BlockSpec((depth, TILE), lambda i, c: (0, i)),
            ],
            out_specs=[
                pl.BlockSpec((2 * blocks, size, TILE), lambda i, c: (0, 0, i)),
                pl.BlockSpec((2 * blocks, size, depth), whole),
                pl.BlockSpec((2 * blocks, size, 16), whole),
            ],
        ),
        out_shape=[
            jax.ShapeDtypeStruct((2 * blocks, size, width), bf16),
            jax.ShapeDtypeStruct((2 * blocks, size, depth), bf16),
            jax.ShapeDtypeStruct((2 * blocks, size, 16), f32),
        ],
        compiler_params=params(),
        cost_estimate=pl.CostEstimate(
            flops=2 * 512 * depth * width, bytes_accessed=12 * 1024 * 1024, transcendentals=0
        ),
        name="forward",
    )(core, own, other, down_t, merged_low)


def backward_kernel(
    core_ref, cot_ref, part_ref, factor_ref, up_ref, merged_ref,
    own_ref, other_ref, low_ref, mag_ref, total, low_total,
):
    core = core_ref[0]
    step = pl.program_id(0)

    @pl.when(step == 0)
    def _():
        total[...] = jnp.zeros_like(total)
        low_total[...] = jnp.zeros_like(low_total)

    cot = cot_ref[...].astype(f32)
    mag_ref[...] = jnp.sum(cot * part_ref[...].astype(f32), axis=0, keepdims=True)
    grad = (cot * factor_ref[...]).astype(bf16)
    total[...] += dot(grad, merged_ref[...], 1, 1)
    u1, u2, u3 = pieces(up_ref[...])
    low_total[...] += dot(grad, jnp.concatenate([u1, u2, u3], axis=0), 1, 1)

    @pl.when(step == pl.num_programs(0) - 1)
    def _():
        low_ref[...] = low_total[:, :16] + low_total[:, 16:32] + low_total[:, 32:48]
        for z in range(8):
            own = pl.ds(pl.multiple_of((2 * z + core) * 32, 32), 32)
            other = pl.ds(pl.multiple_of((2 * z + 1 - core) * 32, 32), 32)
            own_ref[z] = total[own, :]
            other_ref[z] = total[other, :].astype(bf16)


def backward(core, cot, part, factor, up, merged_low):
    depth, width = merged_low.shape
    tokens = cot.shape[0]
    return pl.pallas_call(
        backward_kernel,
        grid_spec=pltpu.PrefetchScalarGridSpec(
            num_scalar_prefetch=1,
            grid=(width // TILE,),
            in_specs=[
                pl.BlockSpec((tokens, TILE), lambda i, c: (0, i)),
                pl.BlockSpec((tokens, TILE), lambda i, c: (0, i)),
                pl.BlockSpec((1, TILE), lambda i, c: (0, i)),
                pl.BlockSpec((16, TILE), lambda i, c: (0, i)),
                pl.BlockSpec((depth, TILE), lambda i, c: (0, i)),
            ],
            out_specs=[
                pl.BlockSpec((8, 32, depth), lambda i, c: (0, 0, 0)),
                pl.BlockSpec((8, 32, depth), lambda i, c: (0, 0, 0)),
                pl.BlockSpec((tokens, 16), lambda i, c: (0, 0)),
                pl.BlockSpec((1, TILE), lambda i, c: (0, i)),
            ],
            scratch_shapes=[pltpu.VMEM((tokens, depth), f32), pltpu.VMEM((tokens, 48), f32)],
        ),
        out_shape=[
            jax.ShapeDtypeStruct((8, 32, depth), f32),
            jax.ShapeDtypeStruct((8, 32, depth), bf16),
            jax.ShapeDtypeStruct((tokens, 16), f32),
            jax.ShapeDtypeStruct((1, width), f32),
        ],
        compiler_params=params(),
        cost_estimate=pl.CostEstimate(
            flops=2 * 512 * depth * width, bytes_accessed=16 * 1024 * 1024, transcendentals=0
        ),
        name="backward",
    )(core, cot, part, factor, up, merged_low)


def up_kernel(proj_ref, cot_ref, factor_ref, out_ref):
    a1, a2, a3 = pieces(proj_ref[...] * adapter_scale)
    grad = (cot_ref[...].astype(f32) * factor_ref[...]).astype(bf16)
    out = dot(jnp.concatenate([a1, a2, a3], axis=1), grad, 0, 0)
    out_ref[...] = out[:16] + out[16:32] + out[32:48]


def up_gradient_of(proj, cot, factor):
    tokens, width = cot.shape
    tile = width // 2
    return pl.pallas_call(
        up_kernel,
        grid=(2,),
        in_specs=[
            pl.BlockSpec((tokens, 16), lambda i: (0, 0)),
            pl.BlockSpec((tokens, tile), lambda i: (0, i)),
            pl.BlockSpec((1, tile), lambda i: (0, i)),
        ],
        out_specs=pl.BlockSpec((16, tile), lambda i: (0, i)),
        out_shape=jax.ShapeDtypeStruct((16, width), f32),
        compiler_params=params(),
        cost_estimate=pl.CostEstimate(
            flops=2 * 512 * 256 * width, bytes_accessed=4 * 1024 * 1024, transcendentals=0
        ),
        name="up_gradient",
    )(proj, cot, factor)


def down_kernel(low_ref, tokens_ref, out_ref):
    a1, a2, a3 = pieces(low_ref[...] * adapter_scale)
    out = dot(jnp.concatenate([a1, a2, a3], axis=1), tokens_ref[...], 0, 0)
    out_ref[...] = out[:16] + out[16:32] + out[32:48]


def down_gradient_of(low, tokens):
    return pl.pallas_call(
        down_kernel,
        out_shape=jax.ShapeDtypeStruct((16, tokens.shape[1]), f32),
        compiler_params=pltpu.CompilerParams(vmem_limit_bytes=VMEM),
        cost_estimate=pl.CostEstimate(
            flops=2 * 512 * 256 * 1024, bytes_accessed=1024 * 1024, transcendentals=0
        ),
        name="down_gradient",
    )(low, tokens)


def exchange(blocks, axis):
    return lax.all_to_all(blocks, axis, 0, 0, tiled=False)


def add_up(part, axis):
    return jnp.sum(exchange(jnp.broadcast_to(part[None], (16,) + part.shape), axis), axis=0)


def on_device(tokens, weight, down_adapter, up_adapter, magnitude, out_cotangent):
    core = lax.axis_index("c")
    core_ref = core.astype(jnp.int32).reshape(1)
    swap = [(0, 1), (1, 0)]
    down_t = down_adapter.T
    cot_full = lax.all_gather(out_cotangent, ROW, axis=0, tiled=True)
    own_tokens = exchange(jnp.broadcast_to(tokens[None], (8,) + tokens.shape), "z")
    other_tokens = lax.ppermute(own_tokens, "c", swap)
    merged_low, square_sums = merge(down_t, up_adapter, weight)
    norm_squares = add_up(square_sums.reshape(26, 128), ROW).reshape(1, -1)
    column_norm = jnp.sqrt(norm_squares + epsilon)
    factor = magnitude.reshape(1, -1) / column_norm
    part, tokens_full, adapter_part = forward(core_ref, own_tokens, other_tokens, down_t, merged_low)
    out_parts = exchange(part, ROW)
    output = (jnp.sum(out_parts.astype(f32), axis=0) * factor).astype(bf16)
    own_grad, other_grad, low_part, magnitude_part = backward(
        core_ref, cot_full, part.reshape(512, -1), factor, up_adapter, merged_low
    )
    pair = (own_grad + lax.ppermute(other_grad, "c", swap).astype(f32)).astype(bf16)
    grad_tokens = jnp.sum(exchange(pair, "z").astype(f32), axis=0).astype(bf16)
    low_rank = add_up(low_part.reshape(64, 128), COL).reshape(512, 16)
    small = jnp.concatenate([magnitude_part.reshape(26, 128), adapter_part.reshape(64, 128)], axis=0)
    small = add_up(small, ROW)
    grad_magnitude = small[:26].reshape(-1) / column_norm.reshape(-1)
    adapter_proj = small[26:].reshape(512, 16)
    up_gradient = up_gradient_of(adapter_proj, cot_full, factor)
    down_gradient = down_gradient_of(low_rank, tokens_full.reshape(512, -1)).T
    return (output, grad_tokens, grad_magnitude, up_gradient, down_gradient)


def solution(mesh):
    split = Mesh(mesh.devices.reshape(4, 4, 8, 2), ROW + COL)
    return jax.shard_map(
        on_device,
        mesh=split,
        in_specs=(P(COL, ROW), P(ROW, COL), P(ROW, None), P(None, COL), P(COL), P(ROW, COL)),
        out_specs=(P(ROW, COL), P(COL, ROW), P(COL), P(None, COL), P(ROW, None)),
        check_vma=False,
    )
```

```python
import jax
import jax.numpy as jnp
from jax import lax
from jax.experimental import pallas as pl
from jax.experimental.pallas import tpu as pltpu
from jax.sharding import Mesh
from jax.sharding import PartitionSpec as P

adapter_scale = 2.0
epsilon = 1e-06
bf16 = jnp.bfloat16
f32 = jnp.float32
ROW = ("x", "y")
COL = ("z", "c")
CHUNK = 512
RANK = 16
MIB = 1024 * 1024
ANY = pl.BlockSpec(memory_space=pl.ANY)
VMEM = pl.BlockSpec(memory_space=pltpu.VMEM)
SMEM = pl.BlockSpec(memory_space=pltpu.SMEM)


def pieces(value):
    high = value.astype(bf16)
    rest = value - high.astype(f32)
    mid = rest.astype(bf16)
    low = (rest - mid.astype(f32)).astype(bf16)
    return high, mid, low


def dot(left, right, left_dim, right_dim):
    return lax.dot_general(
        left, right, (((left_dim,), (right_dim,)), ((), ())), preferred_element_type=f32
    )


def three(left, right, left_dim, right_dim):
    out = dot(jnp.concatenate(pieces(left), axis=0), right, left_dim, right_dim)
    return out[:RANK] + out[RANK : 2 * RANK] + out[2 * RANK :]


def chunks_of(width):
    return [(at, min(CHUNK, width - at)) for at in range(0, width, CHUNK)]


def call(body, flops, moved, limit, **options):
    return pl.pallas_call(
        body,
        compiler_params=pltpu.CompilerParams(vmem_limit_bytes=limit * MIB),
        cost_estimate=pl.CostEstimate(flops=flops, bytes_accessed=moved, transcendentals=0),
        **options,
    )


def merge_kernel(
    down_ref, up_ref, weight_hbm, merged_hbm, sums_ref, weight, merged, up_cat, totals, in_sem, out_sem
):
    depth, width = weight.shape
    rows, tile = 256, 256

    def fetch(j):
        part = pl.ds(j * rows, rows)
        return pltpu.make_async_copy(weight_hbm.at[part], weight.at[part], in_sem.at[j])

    def store(j):
        part = pl.ds(j * rows, rows)
        return pltpu.make_async_copy(merged.at[part], merged_hbm.at[part], out_sem.at[j])

    steps = range(depth // rows)
    for j in steps:
        fetch(j).start()
    totals[...] = jnp.zeros_like(totals)
    for at in range(0, width, tile):
        cols = slice(at, at + tile)
        u1, u2, u3 = pieces(up_ref[:, cols])
        up_cat[:, cols] = jnp.concatenate([u1, u2, u1, u3, u1, u2], axis=0)
    d1, d2, d3 = pieces(down_ref[...] * adapter_scale)
    down_cat = jnp.concatenate([d1, d1, d2, d1, d3, d2], axis=0)
    for j in steps:
        fetch(j).wait()
        part = slice(j * rows, (j + 1) * rows)
        for at in range(0, width, tile):
            cols = slice(at, at + tile)
            value = weight[part, cols].astype(f32) + dot(down_cat[:, part], up_cat[:, cols], 0, 0)
            merged[part, cols] = value.astype(bf16)
            totals[:, cols] += jnp.sum((value * value).reshape(rows // 8, 8, tile), axis=0)
        store(j).start()
    sums_ref[...] = jnp.sum(totals[...], axis=0, keepdims=True)
    for j in steps:
        store(j).wait()


def merge(down_t, up, weight):
    depth, width = weight.shape
    return call(
        merge_kernel,
        12 * depth * width,
        4 * depth * width,
        20,
        in_specs=[VMEM, VMEM, ANY],
        out_specs=[ANY, VMEM],
        out_shape=[
            jax.ShapeDtypeStruct((depth, width), bf16),
            jax.ShapeDtypeStruct((1, width), f32),
        ],
        scratch_shapes=[
            pltpu.VMEM((depth, width), bf16),
            pltpu.VMEM((depth, width), bf16),
            pltpu.VMEM((6 * RANK, width), bf16),
            pltpu.VMEM((8, width), f32),
            pltpu.SemaphoreType.DMA((4,)),
            pltpu.SemaphoreType.DMA((4,)),
        ],
        name="merge",
    )(down_t, up, weight)


def forward_kernel(
    core_ref, own_ref, other_ref, down_ref, sums_ref, merged_hbm,
    part_hbm, tokens_ref, small_ref, merged, part, in_sem, out_sem,
):
    core = core_ref[0]
    depth, width = merged.shape
    chunks = chunks_of(width)

    def fetch(j):
        cols = pl.ds(*chunks[j])
        return pltpu.make_async_copy(merged_hbm.at[:, cols], merged.at[:, cols], in_sem.at[j])

    def store(j):
        cols = pl.ds(*chunks[j])
        return pltpu.make_async_copy(part.at[:, :, cols], part_hbm.at[:, :, cols], out_sem.at[j])

    for j in range(len(chunks)):
        fetch(j).start()
    for z in range(8):
        tokens_ref[2 * z + core] = own_ref[z]
        tokens_ref[2 * z + 1 - core] = other_ref[z]
    tokens = tokens_ref[...].reshape(512, depth)
    small_ref[:RANK, :] = three(down_ref[...], tokens, 1, 1)
    small_ref[RANK:, :] = jnp.zeros((8, CHUNK), f32)
    for j, (at, size) in enumerate(chunks):
        small_ref[RANK + j : RANK + j + 1, :size] = sums_ref[:, at : at + size]
    for j, (at, size) in enumerate(chunks):
        fetch(j).wait()
        cols = slice(at, at + size)
        part[:, :, cols] = dot(tokens, merged[:, cols], 1, 0).astype(bf16).reshape(16, 32, size)
        store(j).start()
    for j in range(len(chunks)):
        store(j).wait()


def forward(core, own, other, down_t, sums, merged_low):
    depth, width = merged_low.shape
    count = len(chunks_of(width))
    return call(
        forward_kernel,
        2 * 512 * depth * width,
        12 * MIB,
        24,
        in_specs=[SMEM, VMEM, VMEM, VMEM, VMEM, ANY],
        out_specs=[ANY, VMEM, VMEM],
        out_shape=[
            jax.ShapeDtypeStruct((16, 32, width), bf16),
            jax.ShapeDtypeStruct((16, 32, depth), bf16),
            jax.ShapeDtypeStruct((RANK + 8, CHUNK), f32),
        ],
        scratch_shapes=[
            pltpu.VMEM((depth, width), bf16),
            pltpu.VMEM((16, 32, width), bf16),
            pltpu.SemaphoreType.DMA((count,)),
            pltpu.SemaphoreType.DMA((count,)),
        ],
        name="forward",
    )(core, own, other, down_t, sums, merged_low)


def pack(low, high_ref):
    high = low.astype(bf16)
    rest = (low - high.astype(f32)).astype(bf16)
    high_ref[:, :CHUNK] = high
    high_ref[:, CHUNK:] = rest
    return high.astype(f32) + rest.astype(f32)


def backward_kernel(
    core_ref, small_ref, magnitude_ref, up_ref, cot_hbm, part_hbm, merged_hbm,
    own_ref, send_ref, low_ref, mag_ref, factor_ref, cot, part, merged, total, sem,
):
    core = core_ref[0]
    width = merged.shape[1]
    chunks = chunks_of(width)

    def fetch(j):
        cols = pl.ds(*chunks[j])
        pairs = ((cot_hbm, cot), (merged_hbm, merged), (part_hbm, part))
        return [
            pltpu.make_async_copy(source.at[:, cols], target.at[:, cols], sem.at[i, j])
            for i, (source, target) in enumerate(pairs)
        ]

    for j in range(len(chunks)):
        for copy in fetch(j):
            copy.start()
    low = jnp.zeros((RANK, CHUNK), f32)
    for j, (at, size) in enumerate(chunks):
        for copy in fetch(j):
            copy.wait()
        cols = slice(at, at + size)
        norm = jnp.sqrt(small_ref[RANK + j : RANK + j + 1, :size] + epsilon)
        factor = magnitude_ref[:, cols] / norm
        factor_ref[:, cols] = factor
        given = cot[:, cols].astype(f32)
        mag_ref[:, cols] = jnp.sum(given * part[:, cols].astype(f32), axis=0, keepdims=True) / norm
        grad = (given * factor).astype(bf16)
        product = dot(grad, merged[:, cols], 1, 1)
        if j == 0:
            total[...] = product
        else:
            total[...] += product
        low += three(up_ref[:, cols], grad, 1, 1)
    low_ref[...] = pack(low, send_ref.at[256:272, :])
    for z in range(8):
        own = pl.ds(pl.multiple_of((2 * z + core) * 32, 32), 32)
        other = pl.ds(pl.multiple_of((2 * z + 1 - core) * 32, 32), 32)
        own_ref[32 * z : 32 * z + 32, :] = total[own, :]
        send_ref[32 * z : 32 * z + 32, :] = total[other, :].astype(bf16)


def backward(core, small, magnitude, up, cot, part, merged_low):
    depth, width = merged_low.shape
    count = len(chunks_of(width))
    return call(
        backward_kernel,
        2 * 512 * depth * width,
        16 * MIB,
        32,
        in_specs=[SMEM, VMEM, VMEM, VMEM, ANY, ANY, ANY],
        out_specs=[VMEM] * 5,
        out_shape=[
            jax.ShapeDtypeStruct((256, depth), f32),
            jax.ShapeDtypeStruct((272, depth), bf16),
            jax.ShapeDtypeStruct((RANK, CHUNK), f32),
            jax.ShapeDtypeStruct((1, width), f32),
            jax.ShapeDtypeStruct((1, width), f32),
        ],
        scratch_shapes=[
            pltpu.VMEM((512, width), bf16),
            pltpu.VMEM((512, width), bf16),
            pltpu.VMEM((depth, width), bf16),
            pltpu.VMEM((512, depth), f32),
            pltpu.SemaphoreType.DMA((3, count)),
        ],
        name="backward",
    )(core, small, magnitude, up, cot, part, merged_low)


def fold_kernel(bit_ref, keep_ref, low_ref, got_ref, keep_out, low_out, send_out):
    bit = bit_ref[0]
    rows = keep_ref.shape[0]
    for i in range(rows // 64):
        kept = pl.ds(pl.multiple_of((2 * i + bit) * 32, 32), 32)
        sent = pl.ds(pl.multiple_of((2 * i + 1 - bit) * 32, 32), 32)
        at = slice(32 * i, 32 * i + 32)
        keep_out[at, :] = keep_ref[kept, :] + got_ref[kept, :].astype(f32)
        send_out[at, :] = (keep_ref[sent, :] + got_ref[sent, :].astype(f32)).astype(bf16)
    got = got_ref[rows : rows + RANK, :].astype(f32)
    low = low_ref[...] + (got[:, :CHUNK] + got[:, CHUNK:])
    low_out[...] = pack(low, send_out.at[rows // 2 : rows // 2 + RANK, :])


def fold(bit, keep, low, got):
    rows, depth = keep.shape
    return call(
        fold_kernel,
        4 * rows * depth,
        12 * rows * depth,
        16,
        in_specs=[SMEM, VMEM, VMEM, VMEM],
        out_specs=[VMEM] * 3,
        out_shape=[
            jax.ShapeDtypeStruct((rows // 2, depth), f32),
            jax.ShapeDtypeStruct((RANK, CHUNK), f32),
            jax.ShapeDtypeStruct((rows // 2 + RANK, depth), bf16),
        ],
        name="fold",
    )(bit, keep, low, got)


def finish_kernel(keep_ref, low_ref, got_ref, tokens_ref, grad_ref, down_ref):
    grad_ref[...] = (keep_ref[...] + got_ref[:32, :].astype(f32)).astype(bf16)
    got = got_ref[32 : 32 + RANK, :].astype(f32)
    low = low_ref[...] + (got[:, :CHUNK] + got[:, CHUNK:])
    down_ref[...] = three(low * adapter_scale, tokens_ref[...], 1, 0)


def finish(keep, low, got, tokens):
    depth = tokens.shape[1]
    return call(
        finish_kernel,
        2 * 512 * 256 * depth,
        2 * MIB,
        16,
        in_specs=[VMEM] * 4,
        out_specs=[VMEM] * 2,
        out_shape=[
            jax.ShapeDtypeStruct((32, depth), bf16),
            jax.ShapeDtypeStruct((RANK, depth), f32),
        ],
        name="finish",
    )(keep, low, got, tokens)


def up_kernel(small_ref, cot_ref, factor_ref, out_ref):
    grad = (cot_ref[...].astype(f32) * factor_ref[...]).astype(bf16)
    out_ref[...] = three(small_ref[:RANK, :] * adapter_scale, grad, 1, 0)


def up_gradient_of(small, cot, factor):
    tokens, width = cot.shape
    tile = width // 2
    return call(
        up_kernel,
        2 * 512 * 256 * width,
        4 * MIB,
        16,
        grid=(2,),
        in_specs=[
            pl.BlockSpec((RANK + 8, CHUNK), lambda i: (0, 0)),
            pl.BlockSpec((tokens, tile), lambda i: (0, i)),
            pl.BlockSpec((1, tile), lambda i: (0, i)),
        ],
        out_specs=pl.BlockSpec((RANK, tile), lambda i: (0, i)),
        out_shape=jax.ShapeDtypeStruct((RANK, width), f32),
        name="up_gradient",
    )(small, cot, factor)


def exchange(blocks, axis):
    return lax.all_to_all(blocks, axis, 0, 0, tiled=False)


def around(value, axis):
    one, two, other = [
        lax.ppermute(value, axis, [(i, (i + k) % 4) for i in range(4)]) for k in (1, 2, 3)
    ]
    return (value + two) + (one + other)


def add_row(value):
    return around(around(value, "x"), "y")


def on_device(tokens, weight, down_adapter, up_adapter, magnitude, out_cotangent):
    core = lax.axis_index("c").astype(jnp.int32).reshape(1)
    z = lax.axis_index("z").astype(jnp.int32)
    swap = [(0, 1), (1, 0)]
    down_t = down_adapter.T
    cot_full = lax.all_gather(out_cotangent, ROW, axis=0, tiled=True)
    own_tokens = exchange(jnp.broadcast_to(tokens[None], (8,) + tokens.shape), "z")
    merged_low, sums = merge(down_t, up_adapter, weight)
    own_tokens, merged_low, sums = lax.optimization_barrier((own_tokens, merged_low, sums))
    other_tokens = lax.ppermute(own_tokens, "c", swap)
    part, tokens_full, small = forward(core, own_tokens, other_tokens, down_t, sums, merged_low)
    out_parts = exchange(part, ROW)
    small = add_row(small)
    keep, send, low, magnitude_part, factor = backward(
        core, small, magnitude.reshape(1, -1), up_adapter, cot_full, part.reshape(512, -1), merged_low
    )
    got = lax.ppermute(send, "c", swap)
    for k in range(3):
        keep, low, send = fold(((z >> k) & 1).reshape(1), keep, low, got)
        got = lax.ppermute(send, "z", [(i, i ^ (1 << k)) for i in range(8)])
    grad_tokens, down_gradient = finish(keep, low, got, tokens_full.reshape(512, -1))
    grad_magnitude = add_row(magnitude_part).reshape(-1)
    up_gradient = up_gradient_of(small, cot_full, factor)
    output = (jnp.sum(out_parts.astype(f32), axis=0) * factor).astype(bf16)
    return (output, grad_tokens, grad_magnitude, up_gradient, down_gradient.T)


def solution(mesh):
    split = Mesh(mesh.devices.reshape(4, 4, 8, 2), ROW + COL)
    return jax.shard_map(
        on_device,
        mesh=split,
        in_specs=(P(COL, ROW), P(ROW, COL), P(ROW, None), P(None, COL), P(COL), P(ROW, COL)),
        out_specs=(P(ROW, COL), P(COL, ROW), P(COL), P(None, COL), P(ROW, None)),
        check_vma=False,
    )
```

```python
import jax
import jax.numpy as jnp
from jax import lax
from jax.experimental import pallas as pl
from jax.experimental.pallas import tpu as pltpu
from jax.sharding import Mesh
from jax.sharding import PartitionSpec as P

adapter_scale = 2.0
epsilon = 1e-06
bf16 = jnp.bfloat16
f32 = jnp.float32
ROW = ("x", "y")
COL = ("z", "c")
CHUNK = 512
RANK = 16
EXTRA = 256
MIB = 1024 * 1024
ANY = pl.BlockSpec(memory_space=pl.ANY)
VMEM = pl.BlockSpec(memory_space=pltpu.VMEM)
SMEM = pl.BlockSpec(memory_space=pltpu.SMEM)


def pieces(value):
    high = value.astype(bf16)
    rest = value - high.astype(f32)
    mid = rest.astype(bf16)
    low = (rest - mid.astype(f32)).astype(bf16)
    return high, mid, low


def dot(left, right, left_dim, right_dim):
    return lax.dot_general(
        left, right, (((left_dim,), (right_dim,)), ((), ())), preferred_element_type=f32
    )


def three(left, right, left_dim, right_dim):
    out = dot(jnp.concatenate(pieces(left), axis=0), right, left_dim, right_dim)
    return out[:RANK] + out[RANK : 2 * RANK] + out[2 * RANK :]


def chunks_of(width):
    return [(at, min(CHUNK, width - at)) for at in range(0, width, CHUNK)]


def call(body, flops, moved, limit, **options):
    return pl.pallas_call(
        body,
        compiler_params=pltpu.CompilerParams(vmem_limit_bytes=limit * MIB),
        cost_estimate=pl.CostEstimate(flops=flops, bytes_accessed=moved, transcendentals=0),
        **options,
    )


def begin(source, target, sem):
    copy = pltpu.make_async_copy(source, target, sem)
    copy.start()
    return copy


def merge_kernel(
    down_hbm, up_hbm, weight_hbm, merged_hbm, sums_ref,
    down, up, weight, merged, up_cat, totals, small_sem, in_sem, out_sem,
):
    depth, width = weight.shape
    rows, tile = 256, 256
    steps = [slice(at, at + rows) for at in range(0, depth, rows)]
    first = begin(up_hbm, up, small_sem.at[0]), begin(down_hbm, down, small_sem.at[1])
    fetches = [begin(weight_hbm.at[p], weight.at[p], in_sem.at[j]) for j, p in enumerate(steps)]
    totals[...] = jnp.zeros_like(totals)
    for copy in first:
        copy.wait()
    for at in range(0, width, tile):
        cols = slice(at, at + tile)
        u1, u2, u3 = pieces(up[:, cols])
        up_cat[:, cols] = jnp.concatenate([u1, u2, u1, u3, u1, u2], axis=0)
    d1, d2, d3 = pieces(down[...] * adapter_scale)
    down_cat = jnp.concatenate([d1, d1, d2, d1, d3, d2], axis=0)
    stores = []
    for j, part in enumerate(steps):
        fetches[j].wait()
        for at in range(0, width, tile):
            cols = slice(at, at + tile)
            value = weight[part, cols].astype(f32) + dot(down_cat[:, part], up_cat[:, cols], 0, 0)
            merged[part, cols] = value.astype(bf16)
            totals[:, cols] += jnp.sum((value * value).reshape(rows // 8, 8, tile), axis=0)
        stores.append(begin(merged.at[part], merged_hbm.at[part], out_sem.at[j]))
    sums_ref[...] = jnp.sum(totals[...], axis=0, keepdims=True)
    for copy in stores:
        copy.wait()


def merge(down_t, up, weight):
    depth, width = weight.shape
    return call(
        merge_kernel,
        12 * depth * width,
        4 * depth * width,
        20,
        in_specs=[ANY, ANY, ANY],
        out_specs=[ANY, VMEM],
        out_shape=[
            jax.ShapeDtypeStruct((depth, width), bf16),
            jax.ShapeDtypeStruct((1, width), f32),
        ],
        scratch_shapes=[
            pltpu.VMEM((RANK, depth), f32),
            pltpu.VMEM((RANK, width), f32),
            pltpu.VMEM((depth, width), bf16),
            pltpu.VMEM((depth, width), bf16),
            pltpu.VMEM((6 * RANK, width), bf16),
            pltpu.VMEM((8, width), f32),
            pltpu.SemaphoreType.DMA((2,)),
            pltpu.SemaphoreType.DMA((4,)),
            pltpu.SemaphoreType.DMA((4,)),
        ],
        name="merge",
    )(down_t, up, weight)


def forward_kernel(
    core_ref, own_hbm, other_hbm, down_hbm, sums_ref, merged_hbm,
    part_hbm, tokens_hbm, small_hbm,
    tokens, down, small, merged, part, small_sem, in_sem, out_sem,
):
    core = core_ref[0]
    depth, width = merged.shape
    chunks = chunks_of(width)
    first = (
        begin(own_hbm, tokens.at[:, core], small_sem.at[0]),
        begin(other_hbm, tokens.at[:, 1 - core], small_sem.at[1]),
        begin(down_hbm, down, small_sem.at[2]),
    )
    fetches, stores = [], []
    for j, (at, size) in enumerate(chunks):
        cols = slice(at, at + size)
        fetches.append(begin(merged_hbm.at[:, cols], merged.at[:, cols], in_sem.at[j]))
    for j, (at, size) in enumerate(chunks):
        small[RANK + j : RANK + j + 1, :size] = sums_ref[:, at : at + size]
    at, size = chunks[-1]
    small[RANK + len(chunks) - 1 : RANK + len(chunks), size:] = jnp.zeros((1, CHUNK - size), f32)
    small[RANK + len(chunks) :, :] = jnp.zeros((8 - len(chunks), CHUNK), f32)
    for copy in first:
        copy.wait()
    all_tokens = tokens[...].reshape(512, depth)
    small[:RANK, :] = three(down[...], all_tokens, 1, 1)
    stores.append(begin(small, small_hbm, small_sem.at[0]))
    stores.append(begin(tokens, tokens_hbm, small_sem.at[1]))
    for j, (at, size) in enumerate(chunks):
        fetches[j].wait()
        cols = slice(at, at + size)
        product = dot(all_tokens, merged[:, cols], 1, 0).astype(bf16)
        part[:, :, cols] = product.reshape(16, 32, size)
        stores.append(begin(part.at[:, :, cols], part_hbm.at[:, :, cols], out_sem.at[j]))
    for copy in stores:
        copy.wait()


def forward(core, own, other, down_t, sums, merged_low):
    depth, width = merged_low.shape
    count = len(chunks_of(width))
    return call(
        forward_kernel,
        2 * 512 * depth * width,
        12 * MIB,
        24,
        in_specs=[SMEM, ANY, ANY, ANY, VMEM, ANY],
        out_specs=[ANY, ANY, ANY],
        out_shape=[
            jax.ShapeDtypeStruct((16, 32, width + EXTRA), bf16),
            jax.ShapeDtypeStruct((8, 2, 32, depth), bf16),
            jax.ShapeDtypeStruct((RANK + 8, CHUNK), f32),
        ],
        scratch_shapes=[
            pltpu.VMEM((8, 2, 32, depth), bf16),
            pltpu.VMEM((RANK, depth), f32),
            pltpu.VMEM((RANK + 8, CHUNK), f32),
            pltpu.VMEM((depth, width), bf16),
            pltpu.VMEM((16, 32, width), bf16),
            pltpu.SemaphoreType.DMA((3,)),
            pltpu.SemaphoreType.DMA((count,)),
            pltpu.SemaphoreType.DMA((count,)),
        ],
        name="forward",
    )(core, own, other, down_t, sums, merged_low)


def magnitude_kernel(cot_hbm, part_hbm, out_hbm, cot, part, extra, sem, out_sem):
    width = cot.shape[1]
    chunks = chunks_of(width)
    fetches = []
    for j, (at, size) in enumerate(chunks):
        cols = slice(at, at + size)
        fetches.append(
            (
                begin(cot_hbm.at[:, cols], cot.at[:, cols], sem.at[0, j]),
                begin(part_hbm.at[:, :, cols], part.at[:, :, cols], sem.at[1, j]),
            )
        )
    rows = []
    for j, (at, size) in enumerate(chunks):
        for copy in fetches[j]:
            copy.wait()
        cols = slice(at, at + size)
        product = cot[:, cols].astype(f32) * part[:, :, cols].reshape(512, size).astype(f32)
        total = jnp.sum(product, axis=0, keepdims=True)
        rows += [total[:, k : k + EXTRA] for k in range(0, size, EXTRA)]
    rows += [jnp.zeros((1, EXTRA), f32)] * (16 - len(rows))
    value = jnp.concatenate(rows, axis=0)
    high = value.astype(bf16)
    extra[:16, :] = high
    extra[16:, :] = (value - high.astype(f32)).astype(bf16)
    stores = [
        begin(extra, out_hbm.at[r, :, width : width + EXTRA], out_sem.at[r]) for r in range(16)
    ]
    for copy in stores:
        copy.wait()


def add_magnitude(cot, part):
    tokens, width = cot.shape
    return call(
        magnitude_kernel,
        4 * tokens * width,
        7 * MIB,
        16,
        in_specs=[ANY, ANY],
        out_specs=ANY,
        out_shape=jax.ShapeDtypeStruct(part.shape, bf16),
        scratch_shapes=[
            pltpu.VMEM((tokens, width), bf16),
            pltpu.VMEM((16, 32, width), bf16),
            pltpu.VMEM((32, EXTRA), bf16),
            pltpu.SemaphoreType.DMA((2, len(chunks_of(width)))),
            pltpu.SemaphoreType.DMA((16,)),
        ],
        input_output_aliases={1: 0},
        name="magnitude",
    )(cot, part)


def output_kernel(small_ref, magnitude_ref, parts_hbm, out_hbm, mag_hbm, parts, out, mag, sem, out_sem):
    width = out.shape[1]
    chunks = chunks_of(width)
    tail = begin(parts_hbm.at[:, :, width:], parts.at[:, :, width:], sem.at[len(chunks)])
    fetches, stores = [], []
    for j, (at, size) in enumerate(chunks):
        cols = slice(at, at + size)
        fetches.append(begin(parts_hbm.at[:, :, cols], parts.at[:, :, cols], sem.at[j]))

    def added(cols):
        total = parts[0, :, cols].astype(f32)
        for r in range(1, 16):
            total += parts[r, :, cols].astype(f32)
        return total

    tail.wait()
    extra = added(slice(width, width + EXTRA))
    extra = extra[:16] + extra[16:]
    for j, (at, size) in enumerate(chunks):
        fetches[j].wait()
        cols = slice(at, at + size)
        norm = jnp.sqrt(small_ref[RANK + j : RANK + j + 1, :size] + epsilon)
        out[:, cols] = (added(cols) * (magnitude_ref[:, cols] / norm)).astype(bf16)
        stores.append(begin(out.at[:, cols], out_hbm.at[:, cols], out_sem.at[j]))
        for k in range(0, size, EXTRA):
            row = (at + k) // EXTRA
            mag[:, at + k : at + k + EXTRA] = extra[row : row + 1] / norm[:, k : k + EXTRA]
    stores.append(begin(mag, mag_hbm, out_sem.at[len(chunks)]))
    for copy in stores:
        copy.wait()


def output_of(small, magnitude, parts):
    width = magnitude.shape[1]
    count = len(chunks_of(width)) + 1
    return call(
        output_kernel,
        16 * 32 * width,
        4 * MIB,
        16,
        in_specs=[VMEM, VMEM, ANY],
        out_specs=[ANY, ANY],
        out_shape=[
            jax.ShapeDtypeStruct((32, width), bf16),
            jax.ShapeDtypeStruct((1, width), f32),
        ],
        scratch_shapes=[
            pltpu.VMEM(parts.shape, bf16),
            pltpu.VMEM((32, width), bf16),
            pltpu.VMEM((1, width), f32),
            pltpu.SemaphoreType.DMA((count,)),
            pltpu.SemaphoreType.DMA((count,)),
        ],
        name="output",
    )(small, magnitude, parts)


def pack(low, out):
    high = low.astype(bf16)
    rest = (low - high.astype(f32)).astype(bf16)
    out[:, :CHUNK] = high
    out[:, CHUNK:] = rest
    return high.astype(f32) + rest.astype(f32)


def unpack(got):
    got = got.astype(f32)
    return got[:, :CHUNK] + got[:, CHUNK:]


def backward_kernel(
    core_ref, small_hbm, magnitude_ref, up_hbm, cot_hbm, merged_hbm,
    own_ref, send_hbm, low_ref, small, up, cot, merged, total, send, first_sem, sem,
):
    core = core_ref[0]
    width = merged.shape[1]
    chunks = chunks_of(width)
    first = begin(small_hbm, small, first_sem.at[0]), begin(up_hbm, up, first_sem.at[1])
    fetches = []
    for j, (at, size) in enumerate(chunks):
        cols = slice(at, at + size)
        fetches.append(
            (
                begin(cot_hbm.at[:, cols], cot.at[:, cols], sem.at[0, j]),
                begin(merged_hbm.at[:, cols], merged.at[:, cols], sem.at[1, j]),
            )
        )
    for copy in first:
        copy.wait()
    low = jnp.zeros((RANK, CHUNK), f32)
    for j, (at, size) in enumerate(chunks):
        for copy in fetches[j]:
            copy.wait()
        cols = slice(at, at + size)
        norm = jnp.sqrt(small[RANK + j : RANK + j + 1, :size] + epsilon)
        grad = (cot[:, cols].astype(f32) * (magnitude_ref[:, cols] / norm)).astype(bf16)
        product = dot(grad, merged[:, cols], 1, 1)
        if j == 0:
            total[...] = product
        else:
            total[...] += product
        low += three(up[:, cols], grad, 1, 1)
    low_ref[...] = pack(low, send.at[256:272, :])
    for z in range(8):
        own = pl.ds(pl.multiple_of((2 * z + core) * 32, 32), 32)
        other = pl.ds(pl.multiple_of((2 * z + 1 - core) * 32, 32), 32)
        send[32 * z : 32 * z + 32, :] = total[other, :].astype(bf16)
        own_ref[32 * z : 32 * z + 32, :] = total[own, :]
    copy = begin(send, send_hbm, first_sem.at[0])
    copy.wait()


def backward(core, small, magnitude, up, cot, merged_low):
    depth, width = merged_low.shape
    count = len(chunks_of(width))
    return call(
        backward_kernel,
        2 * 512 * depth * width,
        12 * MIB,
        28,
        in_specs=[SMEM, ANY, VMEM, ANY, ANY, ANY],
        out_specs=[VMEM, ANY, VMEM],
        out_shape=[
            jax.ShapeDtypeStruct((256, depth), f32),
            jax.ShapeDtypeStruct((272, depth), bf16),
            jax.ShapeDtypeStruct((RANK, CHUNK), f32),
        ],
        scratch_shapes=[
            pltpu.VMEM((RANK + 8, CHUNK), f32),
            pltpu.VMEM((RANK, width), f32),
            pltpu.VMEM((512, width), bf16),
            pltpu.VMEM((depth, width), bf16),
            pltpu.VMEM((512, depth), f32),
            pltpu.VMEM((272, depth), bf16),
            pltpu.SemaphoreType.DMA((2,)),
            pltpu.SemaphoreType.DMA((2, count)),
        ],
        name="backward",
    )(core, small, magnitude, up, cot, merged_low)


def fold_kernel(bit_ref, keep_ref, low_ref, got_hbm, keep_out, low_out, send_hbm, got_ref, send_out, sem):
    bit = bit_ref[0]
    rows = keep_ref.shape[0]
    begin(got_hbm, got_ref, sem.at[0]).wait()
    for i in range(rows // 64):
        kept = pl.ds(pl.multiple_of((2 * i + bit) * 32, 32), 32)
        sent = pl.ds(pl.multiple_of((2 * i + 1 - bit) * 32, 32), 32)
        at = slice(32 * i, 32 * i + 32)
        keep_out[at, :] = keep_ref[kept, :] + got_ref[kept, :].astype(f32)
        send_out[at, :] = (keep_ref[sent, :] + got_ref[sent, :].astype(f32)).astype(bf16)
    low = low_ref[...] + unpack(got_ref[rows : rows + RANK, :])
    low_out[...] = pack(low, send_out.at[rows // 2 : rows // 2 + RANK, :])
    begin(send_out, send_hbm, sem.at[0]).wait()


def fold(bit, keep, low, got):
    rows, depth = keep.shape
    return call(
        fold_kernel,
        4 * rows * depth,
        12 * rows * depth,
        16,
        in_specs=[SMEM, VMEM, VMEM, ANY],
        out_specs=[VMEM, VMEM, ANY],
        out_shape=[
            jax.ShapeDtypeStruct((rows // 2, depth), f32),
            jax.ShapeDtypeStruct((RANK, CHUNK), f32),
            jax.ShapeDtypeStruct((rows // 2 + RANK, depth), bf16),
        ],
        scratch_shapes=[
            pltpu.VMEM((rows + RANK, depth), bf16),
            pltpu.VMEM((rows // 2 + RANK, depth), bf16),
            pltpu.SemaphoreType.DMA((1,)),
        ],
        name="fold",
    )(bit, keep, low, got)


def finish_kernel(
    keep_ref, low_ref, got_hbm, tokens_hbm, grad_hbm, down_hbm, got, tokens, grad, down, sem
):
    later = begin(tokens_hbm, tokens, sem.at[1])
    begin(got_hbm, got, sem.at[0]).wait()
    grad[...] = (keep_ref[...] + got[:32, :].astype(f32)).astype(bf16)
    first = begin(grad, grad_hbm, sem.at[0])
    low = low_ref[...] + unpack(got[32 : 32 + RANK, :])
    later.wait()
    down[...] = three(low * adapter_scale, tokens[...], 1, 0)
    begin(down, down_hbm, sem.at[1]).wait()
    first.wait()


def finish(keep, low, got, tokens):
    depth = tokens.shape[1]
    return call(
        finish_kernel,
        2 * 512 * 256 * depth,
        2 * MIB,
        16,
        in_specs=[VMEM, VMEM, ANY, ANY],
        out_specs=[ANY, ANY],
        out_shape=[
            jax.ShapeDtypeStruct((32, depth), bf16),
            jax.ShapeDtypeStruct((RANK, depth), f32),
        ],
        scratch_shapes=[
            pltpu.VMEM(got.shape, bf16),
            pltpu.VMEM(tokens.shape, bf16),
            pltpu.VMEM((32, depth), bf16),
            pltpu.VMEM((RANK, depth), f32),
            pltpu.SemaphoreType.DMA((2,)),
        ],
        name="finish",
    )(keep, low, got, tokens)


def up_kernel(small_hbm, magnitude_ref, cot_hbm, out_hbm, small, cot, out, sem, out_sem):
    width = cot.shape[1]
    chunks = chunks_of(width)
    first = begin(small_hbm, small, sem.at[len(chunks)])
    fetches, stores = [], []
    for j, (at, size) in enumerate(chunks):
        cols = slice(at, at + size)
        fetches.append(begin(cot_hbm.at[:, cols], cot.at[:, cols], sem.at[j]))
    first.wait()
    for j, (at, size) in enumerate(chunks):
        fetches[j].wait()
        cols = slice(at, at + size)
        norm = jnp.sqrt(small[RANK + j : RANK + j + 1, :size] + epsilon)
        grad = (cot[:, cols].astype(f32) * (magnitude_ref[:, cols] / norm)).astype(bf16)
        out[:, cols] = three(small[:RANK, :] * adapter_scale, grad, 1, 0)
        stores.append(begin(out.at[:, cols], out_hbm.at[:, cols], out_sem.at[j]))
    for copy in stores:
        copy.wait()


def up_gradient_of(small, magnitude, cot):
    tokens, width = cot.shape
    count = len(chunks_of(width)) + 1
    return call(
        up_kernel,
        2 * 512 * 256 * width,
        4 * MIB,
        16,
        in_specs=[ANY, VMEM, ANY],
        out_specs=ANY,
        out_shape=jax.ShapeDtypeStruct((RANK, width), f32),
        scratch_shapes=[
            pltpu.VMEM(small.shape, f32),
            pltpu.VMEM(cot.shape, bf16),
            pltpu.VMEM((RANK, width), f32),
            pltpu.SemaphoreType.DMA((count,)),
            pltpu.SemaphoreType.DMA((count,)),
        ],
        name="up_gradient",
    )(small, magnitude, cot)


def exchange(blocks, axis):
    return lax.all_to_all(blocks, axis, 0, 0, tiled=False)


def around(value, axis):
    one, two, other = [
        lax.ppermute(value, axis, [(i, (i + k) % 4) for i in range(4)]) for k in (1, 2, 3)
    ]
    return (value + two) + (one + other)


def add_row(value):
    return around(around(value, "x"), "y")


def on_device(tokens, weight, down_adapter, up_adapter, magnitude, out_cotangent):
    core = lax.axis_index("c").astype(jnp.int32).reshape(1)
    z = lax.axis_index("z").astype(jnp.int32)
    swap = [(0, 1), (1, 0)]
    down_t = down_adapter.T
    magnitude = magnitude.reshape(1, -1)
    cot_full = lax.all_gather(out_cotangent, ROW, axis=0, tiled=True)
    own_tokens = exchange(jnp.broadcast_to(tokens[None], (8,) + tokens.shape), "z")
    merged_low, sums = merge(down_t, up_adapter, weight)
    own_tokens, merged_low, sums = lax.optimization_barrier((own_tokens, merged_low, sums))
    other_tokens = lax.ppermute(own_tokens, "c", swap)
    part, tokens_full, small = forward(core, own_tokens, other_tokens, down_t, sums, merged_low)
    small = add_row(small)
    small, part, cot_full = lax.optimization_barrier((small, part, cot_full))
    part = add_magnitude(cot_full, part)
    out_parts = exchange(part, ROW)
    keep, send, low = backward(core, small, magnitude, up_adapter, cot_full, merged_low)
    got = lax.ppermute(send, "c", swap)
    for k in range(3):
        keep, low, send = fold(((z >> k) & 1).reshape(1), keep, low, got)
        got = lax.ppermute(send, "z", [(i, i ^ (1 << k)) for i in range(8)])
    grad_tokens, down_gradient = finish(keep, low, got, tokens_full.reshape(512, -1))
    up_gradient = up_gradient_of(small, magnitude, cot_full)
    output, grad_magnitude = output_of(small, magnitude, out_parts)
    return (output, grad_tokens, grad_magnitude.reshape(-1), up_gradient, down_gradient.T)


def solution(mesh):
    split = Mesh(mesh.devices.reshape(4, 4, 8, 2), ROW + COL)
    return jax.shard_map(
        on_device,
        mesh=split,
        in_specs=(P(COL, ROW), P(ROW, COL), P(ROW, None), P(None, COL), P(COL), P(ROW, COL)),
        out_specs=(P(ROW, COL), P(COL, ROW), P(COL), P(None, COL), P(ROW, None)),
        check_vma=False,
    )
```

```python
import jax
import jax.numpy as jnp
from jax import lax
from jax.experimental import pallas as pl
from jax.experimental.pallas import tpu as pltpu
from jax.sharding import Mesh
from jax.sharding import PartitionSpec as P

adapter_scale = 2.0
epsilon = 1e-06
bf16 = jnp.bfloat16
f32 = jnp.float32
ROW = ("x", "y")
COL = ("z", "c")
CHUNK = 512
RANK = 16
EXTRA = 256
MIB = 1024 * 1024
LIMIT = 62 * MIB
ANY = pl.BlockSpec(memory_space=pl.ANY)
SMEM = pl.BlockSpec(memory_space=pltpu.SMEM)


def pieces(value):
    high = value.astype(bf16)
    rest = value - high.astype(f32)
    mid = rest.astype(bf16)
    low = (rest - mid.astype(f32)).astype(bf16)
    return high, mid, low


def dot(left, right, left_dim, right_dim):
    return lax.dot_general(
        left, right, (((left_dim,), (right_dim,)), ((), ())), preferred_element_type=f32
    )


def three(left, right, left_dim, right_dim):
    out = dot(jnp.concatenate(pieces(left), axis=0), right, left_dim, right_dim)
    return out[:RANK] + out[RANK : 2 * RANK] + out[2 * RANK :]


def chunks_of(width):
    return [(at, min(CHUNK, width - at)) for at in range(0, width, CHUNK)]


def call(body, flops, moved, **options):
    return pl.pallas_call(
        body,
        compiler_params=pltpu.CompilerParams(vmem_limit_bytes=LIMIT),
        cost_estimate=pl.CostEstimate(flops=flops, bytes_accessed=moved, transcendentals=0),
        **options,
    )


def begin(source, target, sem):
    copy = pltpu.make_async_copy(source, target, sem)
    copy.start()
    return copy


def merge_kernel(
    shard_ref, tokens_hbm, down_hbm, up_hbm, weight_hbm, merged_hbm, small_hbm,
    tokens, down, up, weight, merged, small, up_cat, totals, small_sem, in_sem, out_sem,
):
    depth, width = weight.shape
    rows, tile = 256, 256
    chunks = chunks_of(width)
    steps = [slice(at, at + rows) for at in range(0, depth, rows)]
    first = begin(up_hbm, up, small_sem.at[0]), begin(down_hbm, down, small_sem.at[1])
    later = begin(tokens_hbm, tokens, small_sem.at[2])
    fetches = [begin(weight_hbm.at[p], weight.at[p], in_sem.at[j]) for j, p in enumerate(steps)]
    totals[...] = jnp.zeros_like(totals)
    for copy in first:
        copy.wait()
    for at in range(0, width, tile):
        cols = slice(at, at + tile)
        u1, u2, u3 = pieces(up[:, cols])
        up_cat[:, cols] = jnp.concatenate([u1, u2, u1, u3, u1, u2], axis=0)
    d1, d2, d3 = pieces(down[...] * adapter_scale)
    down_cat = jnp.concatenate([d1, d1, d2, d1, d3, d2], axis=0)
    stores = []
    for j, part in enumerate(steps):
        fetches[j].wait()
        for at in range(0, width, tile):
            cols = slice(at, at + tile)
            value = weight[part, cols].astype(f32) + dot(down_cat[:, part], up_cat[:, cols], 0, 0)
            merged[part, cols] = value.astype(bf16)
            totals[:, cols] += jnp.sum((value * value).reshape(rows // 8, 8, tile), axis=0)
        stores.append(begin(merged.at[part], merged_hbm.at[part], out_sem.at[j]))
    later.wait()
    proj = three(down[...], tokens[...], 1, 1)
    owner = lax.broadcasted_iota(jnp.int32, (RANK, CHUNK), 1) // 32
    small[:RANK, :] = jnp.where(owner == shard_ref[0], jnp.concatenate([proj] * 16, axis=1), 0.0)
    small[RANK:, :] = jnp.zeros((8, CHUNK), f32)
    for j, (at, size) in enumerate(chunks):
        sums = jnp.sum(totals[:, at : at + size], axis=0, keepdims=True)
        small[RANK + j : RANK + j + 1, :size] = sums
    stores.append(begin(small, small_hbm, small_sem.at[0]))
    for copy in stores:
        copy.wait()


def merge(shard, tokens, down_t, up, weight):
    depth, width = weight.shape
    return call(
        merge_kernel,
        12 * depth * width,
        4 * depth * width,
        in_specs=[SMEM, ANY, ANY, ANY, ANY],
        out_specs=[ANY, ANY],
        out_shape=[
            jax.ShapeDtypeStruct((depth, width), bf16),
            jax.ShapeDtypeStruct((RANK + 8, CHUNK), f32),
        ],
        scratch_shapes=[
            pltpu.VMEM(tokens.shape, bf16),
            pltpu.VMEM((RANK, depth), f32),
            pltpu.VMEM((RANK, width), f32),
            pltpu.VMEM((depth, width), bf16),
            pltpu.VMEM((depth, width), bf16),
            pltpu.VMEM((RANK + 8, CHUNK), f32),
            pltpu.VMEM((6 * RANK, width), bf16),
            pltpu.VMEM((8, width), f32),
            pltpu.SemaphoreType.DMA((3,)),
            pltpu.SemaphoreType.DMA((4,)),
            pltpu.SemaphoreType.DMA((4,)),
        ],
        name="merge",
    )(shard, tokens, down_t, up, weight)


def forward_kernel(*refs):
    place_ref, tokens_hbm, merged_hbm = refs[:3]
    halves = refs[3:7], refs[7:11]
    part_hbm, cot_hbm = refs[11:13]
    tokens, merged, cot, part, extra, cot_sem, in_sem, out_sem = refs[13:]
    x, y = place_ref[0], place_ref[1]
    depth, width = merged.shape
    chunks = chunks_of(width)
    first = begin(tokens_hbm, tokens, in_sem.at[len(chunks)])
    fetches, stores, arrived = [], [], []
    for j, (at, size) in enumerate(chunks):
        cols = slice(at, at + size)
        fetches.append(begin(merged_hbm.at[:, cols], merged.at[:, cols], in_sem.at[j]))
    for half, arrays in enumerate(halves):
        rows = slice(16 * half, 16 * half + 16)
        for j, array in enumerate(arrays):
            for k in range(4):
                near, far = (k, j) if half == 0 else (j, k)
                target = cot.at[lax.rem(x + 4 - near, 4), lax.rem(y + 4 - far, 4), rows]
                source = array.at[16 * k : 16 * k + 16]
                arrived.append(begin(source, target, cot_sem.at[16 * half + 4 * j + k]))
    first.wait()
    all_tokens = tokens[...].reshape(512, depth)
    rows = []
    for j, (at, size) in enumerate(chunks):
        fetches[j].wait()
        cols = slice(at, at + size)
        product = dot(all_tokens, merged[:, cols], 1, 0)
        part[:, :, cols] = product.astype(bf16).reshape(16, 32, size)
        stores.append(begin(part.at[:, :, cols], part_hbm.at[:, :, cols], out_sem.at[j]))
        if j == 0:
            for copy in arrived:
                copy.wait()
            stores.append(begin(cot, cot_hbm, cot_sem.at[0]))
        weighted = product * cot[:, :, :, cols].reshape(512, size).astype(f32)
        total = jnp.sum(weighted, axis=0, keepdims=True)
        rows += [total[:, k : k + EXTRA] for k in range(0, size, EXTRA)]
    rows += [jnp.zeros((1, EXTRA), f32)] * (16 - len(rows))
    value = jnp.concatenate(rows, axis=0)
    high = value.astype(bf16)
    rest = (value - high.astype(f32)).astype(bf16)
    extra[...] = jnp.broadcast_to(jnp.concatenate([high, rest], axis=0)[None], extra.shape)
    stores.append(begin(extra, part_hbm.at[:, :, width:], out_sem.at[len(chunks)]))
    for copy in stores:
        copy.wait()


def forward(place, tokens, merged_low, first_half, second_half):
    depth, width = merged_low.shape
    count = len(chunks_of(width)) + 1
    return call(
        forward_kernel,
        2 * 512 * depth * width,
        16 * MIB,
        in_specs=[SMEM] + [ANY] * 10,
        out_specs=[ANY, ANY],
        out_shape=[
            jax.ShapeDtypeStruct((16, 32, width + EXTRA), bf16),
            jax.ShapeDtypeStruct((4, 4, 32, width), bf16),
        ],
        scratch_shapes=[
            pltpu.VMEM((16, 32, depth), bf16),
            pltpu.VMEM((depth, width), bf16),
            pltpu.VMEM((4, 4, 32, width), bf16),
            pltpu.VMEM((16, 32, width), bf16),
            pltpu.VMEM((16, 32, EXTRA), bf16),
            pltpu.SemaphoreType.DMA((32,)),
            pltpu.SemaphoreType.DMA((count,)),
            pltpu.SemaphoreType.DMA((count,)),
        ],
        name="forward",
    )(place, tokens, merged_low, *first_half, *second_half)


def output_kernel(
    small_hbm, magnitude_hbm, parts_hbm, out_hbm, mag_hbm,
    small, magnitude, parts, out, mag, small_sem, sem, out_sem,
):
    width = out.shape[1]
    chunks = chunks_of(width)
    first = (
        begin(small_hbm, small, small_sem.at[0]),
        begin(magnitude_hbm, magnitude, small_sem.at[1]),
        begin(parts_hbm.at[:, :, width:], parts.at[:, :, width:], sem.at[len(chunks)]),
    )
    fetches, stores = [], []
    for j, (at, size) in enumerate(chunks):
        cols = slice(at, at + size)
        fetches.append(begin(parts_hbm.at[:, :, cols], parts.at[:, :, cols], sem.at[j]))

    def added(cols):
        total = parts[0, :, cols].astype(f32)
        for r in range(1, 16):
            total += parts[r, :, cols].astype(f32)
        return total

    for copy in first:
        copy.wait()
    extra = added(slice(width, width + EXTRA))
    extra = extra[:16] + extra[16:]
    for j, (at, size) in enumerate(chunks):
        fetches[j].wait()
        cols = slice(at, at + size)
        norm = jnp.sqrt(small[RANK + j : RANK + j + 1, :size] + epsilon)
        out[:, cols] = (added(cols) * (magnitude[:, cols] / norm)).astype(bf16)
        stores.append(begin(out.at[:, cols], out_hbm.at[:, cols], out_sem.at[j]))
        for k in range(0, size, EXTRA):
            row = (at + k) // EXTRA
            mag[:, at + k : at + k + EXTRA] = extra[row : row + 1] / norm[:, k : k + EXTRA]
    stores.append(begin(mag, mag_hbm, out_sem.at[len(chunks)]))
    for copy in stores:
        copy.wait()


def output_of(small, magnitude, parts):
    width = magnitude.shape[1]
    count = len(chunks_of(width)) + 1
    return call(
        output_kernel,
        16 * 32 * width,
        4 * MIB,
        in_specs=[ANY, ANY, ANY],
        out_specs=[ANY, ANY],
        out_shape=[
            jax.ShapeDtypeStruct((32, width), bf16),
            jax.ShapeDtypeStruct((1, width), f32),
        ],
        scratch_shapes=[
            pltpu.VMEM(small.shape, f32),
            pltpu.VMEM((1, width), f32),
            pltpu.VMEM(parts.shape, bf16),
            pltpu.VMEM((32, width), bf16),
            pltpu.VMEM((1, width), f32),
            pltpu.SemaphoreType.DMA((2,)),
            pltpu.SemaphoreType.DMA((count,)),
            pltpu.SemaphoreType.DMA((count,)),
        ],
        name="output",
    )(small, magnitude, parts)


def pack(low, out):
    high = low.astype(bf16)
    rest = (low - high.astype(f32)).astype(bf16)
    out[:, :CHUNK] = high
    out[:, CHUNK:] = rest
    return high.astype(f32) + rest.astype(f32)


def unpack(got):
    got = got.astype(f32)
    return got[:, :CHUNK] + got[:, CHUNK:]


def backward_kernel(
    core_ref, small_hbm, magnitude_hbm, up_hbm, cot_hbm, merged_hbm,
    own_hbm, send_hbm, small, magnitude, up, cot, merged, total, own, send, first_sem, sem,
):
    core = core_ref[0]
    width = merged.shape[1]
    chunks = chunks_of(width)
    first = (
        begin(small_hbm, small, first_sem.at[0]),
        begin(up_hbm, up, first_sem.at[1]),
        begin(magnitude_hbm, magnitude, first_sem.at[2]),
    )
    fetches = []
    for j, (at, size) in enumerate(chunks):
        cols = slice(at, at + size)
        fetches.append(
            (
                begin(cot_hbm.at[:, cols], cot.at[:, cols], sem.at[0, j]),
                begin(merged_hbm.at[:, cols], merged.at[:, cols], sem.at[1, j]),
            )
        )
    for copy in first:
        copy.wait()
    low = jnp.zeros((RANK, CHUNK), f32)
    for j, (at, size) in enumerate(chunks):
        for copy in fetches[j]:
            copy.wait()
        cols = slice(at, at + size)
        norm = jnp.sqrt(small[RANK + j : RANK + j + 1, :size] + epsilon)
        grad = (cot[:, cols].astype(f32) * (magnitude[:, cols] / norm)).astype(bf16)
        product = dot(grad, merged[:, cols], 1, 1)
        if j == 0:
            total[...] = product
        else:
            total[...] += product
        low += three(up[:, cols], grad, 1, 1)
    for z in range(8):
        theirs = pl.ds(pl.multiple_of((2 * z + 1 - core) * 32, 32), 32)
        send[32 * z : 32 * z + 32, :] = total[theirs, :].astype(bf16)
    pack(low, send.at[256:272, :])
    first = begin(send, send_hbm, first_sem.at[0])
    for z in range(8):
        mine = pl.ds(pl.multiple_of((2 * z + core) * 32, 32), 32)
        own[32 * z : 32 * z + 32, :] = total[mine, :].astype(bf16)
    own[256:272, :] = send[256:272, :]
    begin(own, own_hbm, first_sem.at[1]).wait()
    first.wait()


def backward(core, small, magnitude, up, cot, merged_low):
    depth, width = merged_low.shape
    count = len(chunks_of(width))
    return call(
        backward_kernel,
        2 * 512 * depth * width,
        12 * MIB,
        in_specs=[SMEM] + [ANY] * 5,
        out_specs=[ANY, ANY],
        out_shape=[jax.ShapeDtypeStruct((272, depth), bf16)] * 2,
        scratch_shapes=[
            pltpu.VMEM(small.shape, f32),
            pltpu.VMEM((1, width), f32),
            pltpu.VMEM((RANK, width), f32),
            pltpu.VMEM((512, width), bf16),
            pltpu.VMEM((depth, width), bf16),
            pltpu.VMEM((512, depth), f32),
            pltpu.VMEM((272, depth), bf16),
            pltpu.VMEM((272, depth), bf16),
            pltpu.SemaphoreType.DMA((3,)),
            pltpu.SemaphoreType.DMA((2, count)),
        ],
        name="backward",
    )(core, small, magnitude, up, cot, merged_low)


def pair_kernel(z_ref, own_hbm, got_hbm, *refs):
    out_hbm = refs[:8]
    own, got, send, sem, out_sem = refs[8:]
    z = z_ref[0]
    copies = begin(own_hbm, own, sem.at[0]), begin(got_hbm, got, sem.at[1])
    for copy in copies:
        copy.wait()
    low = unpack(own[256:272, :]) + unpack(got[256:272, :])
    pack(low, send.at[0, 32:48, :])
    stores = []
    for k in [1, 7, 2, 6, 3, 5, 4, 0]:
        block = pl.ds(pl.multiple_of(lax.rem(z + k, 8) * 32, 32), 32)
        send[k, :32, :] = (own[block, :].astype(f32) + got[block, :].astype(f32)).astype(bf16)
        if k:
            send[k, 32:48, :] = send[0, 32:48, :]
        stores.append(begin(send.at[k], out_hbm[k], out_sem.at[k]))
    for copy in stores:
        copy.wait()


def pair(z, own, got):
    rows, depth = own.shape
    return call(
        pair_kernel,
        4 * rows * depth,
        6 * rows * depth,
        in_specs=[SMEM, ANY, ANY],
        out_specs=[ANY] * 8,
        out_shape=[jax.ShapeDtypeStruct((48, depth), bf16)] * 8,
        scratch_shapes=[
            pltpu.VMEM((rows, depth), bf16),
            pltpu.VMEM((rows, depth), bf16),
            pltpu.VMEM((8, 48, depth), bf16),
            pltpu.SemaphoreType.DMA((2,)),
            pltpu.SemaphoreType.DMA((8,)),
        ],
        name="pair",
    )(z, own, got)


def finish_kernel(z_ref, tokens_hbm, *refs):
    parts_hbm = refs[:8]
    grad_hbm, down_hbm, parts, tokens, lows, grad, down, sem, out_sem = refs[8:]
    z = z_ref[0]
    later = begin(tokens_hbm, tokens, sem.at[8])
    copies = [begin(parts_hbm[k], parts.at[k], sem.at[k]) for k in range(8)]
    for copy in copies:
        copy.wait()
    total = parts[0, :32, :].astype(f32)
    for k in range(1, 8):
        total += parts[k, :32, :].astype(f32)
    grad[...] = total.astype(bf16)
    first = begin(grad, grad_hbm, out_sem.at[0])
    for k in range(8):
        lows[lax.rem(z + 8 - k, 8)] = unpack(parts[k, 32:48, :])
    low = lows[0]
    for k in range(1, 8):
        low += lows[k]
    later.wait()
    down[...] = three(low * adapter_scale, tokens[...], 1, 0)
    begin(down, down_hbm, out_sem.at[1]).wait()
    first.wait()


def finish(z, tokens, parts):
    depth = tokens.shape[1]
    return call(
        finish_kernel,
        2 * 512 * 256 * depth,
        2 * MIB,
        in_specs=[SMEM] + [ANY] * 9,
        out_specs=[ANY, ANY],
        out_shape=[
            jax.ShapeDtypeStruct((32, depth), bf16),
            jax.ShapeDtypeStruct((RANK, depth), f32),
        ],
        scratch_shapes=[
            pltpu.VMEM((8, 48, depth), bf16),
            pltpu.VMEM(tokens.shape, bf16),
            pltpu.VMEM((8, RANK, CHUNK), f32),
            pltpu.VMEM((32, depth), bf16),
            pltpu.VMEM((RANK, depth), f32),
            pltpu.SemaphoreType.DMA((9,)),
            pltpu.SemaphoreType.DMA((2,)),
        ],
        name="finish",
    )(z, tokens, *parts)


def up_kernel(
    proj_hbm, small_hbm, magnitude_hbm, cot_hbm, out_hbm,
    proj, small, magnitude, cot, out, first_sem, sem, out_sem,
):
    width = cot.shape[1]
    chunks = chunks_of(width)
    first = (
        begin(proj_hbm, proj, first_sem.at[0]),
        begin(small_hbm, small, first_sem.at[1]),
        begin(magnitude_hbm, magnitude, first_sem.at[2]),
    )
    fetches, stores = [], []
    for j, (at, size) in enumerate(chunks):
        cols = slice(at, at + size)
        fetches.append(begin(cot_hbm.at[:, cols], cot.at[:, cols], sem.at[j]))
    for copy in first:
        copy.wait()
    for j, (at, size) in enumerate(chunks):
        fetches[j].wait()
        cols = slice(at, at + size)
        norm = jnp.sqrt(small[RANK + j : RANK + j + 1, :size] + epsilon)
        grad = (cot[:, cols].astype(f32) * (magnitude[:, cols] / norm)).astype(bf16)
        out[:, cols] = three(proj[...] * adapter_scale, grad, 1, 0)
        stores.append(begin(out.at[:, cols], out_hbm.at[:, cols], out_sem.at[j]))
    for copy in stores:
        copy.wait()


def up_gradient_of(proj, small, magnitude, cot):
    tokens, width = cot.shape
    count = len(chunks_of(width))
    return call(
        up_kernel,
        2 * 512 * 256 * width,
        4 * MIB,
        in_specs=[ANY] * 4,
        out_specs=ANY,
        out_shape=jax.ShapeDtypeStruct((RANK, width), f32),
        scratch_shapes=[
            pltpu.VMEM(proj.shape, f32),
            pltpu.VMEM(small.shape, f32),
            pltpu.VMEM((1, width), f32),
            pltpu.VMEM(cot.shape, bf16),
            pltpu.VMEM((RANK, width), f32),
            pltpu.SemaphoreType.DMA((3,)),
            pltpu.SemaphoreType.DMA((count,)),
            pltpu.SemaphoreType.DMA((count,)),
        ],
        name="up_gradient",
    )(proj, small, magnitude, cot)


def shifted(value, axis, size):
    return [
        lax.ppermute(value, axis, [(i, (i + k) % size) for i in range(size)])
        for k in range(1, size)
    ]


def around(value, axis):
    one, two, other = shifted(value, axis, 4)
    return (value + two) + (one + other)


def add_col(value):
    value = value + lax.ppermute(value, "c", [(0, 1), (1, 0)])
    for k in (1, 2, 4):
        value = value + lax.ppermute(value, "z", [(i, i ^ k) for i in range(8)])
    return value


def on_device(tokens, weight, down_adapter, up_adapter, magnitude, out_cotangent):
    x, y, z, core = [lax.axis_index(name).astype(jnp.int32) for name in ROW + COL]
    shard = (2 * z + core).reshape(1)
    place = jnp.stack([x, y])
    down_t = down_adapter.T
    magnitude = magnitude.reshape(1, -1)
    tokens_full = lax.all_gather(tokens, COL, axis=0)
    first, second = out_cotangent[:16], out_cotangent[16:]
    first = [first] + shifted(first, "x", 4)
    second = [second] + shifted(second, "y", 4)
    merged_low, small = merge(shard, tokens, down_t, up_adapter, weight)
    small = around(small, "x")
    first = jnp.concatenate(first, axis=0)
    second = jnp.concatenate(second, axis=0)
    first, second, small = lax.optimization_barrier((first, second, small))
    first = [first] + shifted(first, "y", 4)
    second = [second] + shifted(second, "x", 4)
    small = around(small, "y")
    first, second, small = lax.optimization_barrier((first, second, small))
    part, cot_full = forward(place, tokens_full, merged_low, first, second)
    cot_full = cot_full.reshape(512, -1)
    parts = lax.all_to_all(part, ROW, 0, 0, tiled=False)
    own, send = backward(core.reshape(1), small, magnitude, up_adapter, cot_full, merged_low)
    got = lax.ppermute(send, "c", [(0, 1), (1, 0)])
    blocks = list(pair(z.reshape(1), own, got))
    for k in range(1, 8):
        blocks[k] = lax.ppermute(blocks[k], "z", [(i, (i + k) % 8) for i in range(8)])
    grad_tokens, down_gradient = finish(z.reshape(1), tokens_full.reshape(512, -1), blocks)
    proj = add_col(small[:RANK])
    up_gradient = up_gradient_of(proj, small, magnitude, cot_full)
    output, grad_magnitude = output_of(small, magnitude, parts)
    return (output, grad_tokens, grad_magnitude.reshape(-1), up_gradient, down_gradient.T)


def solution(mesh):
    split = Mesh(mesh.devices.reshape(4, 4, 8, 2), ROW + COL)
    return jax.shard_map(
        on_device,
        mesh=split,
        in_specs=(P(COL, ROW), P(ROW, COL), P(ROW, None), P(None, COL), P(COL), P(ROW, COL)),
        out_specs=(P(ROW, COL), P(COL, ROW), P(COL), P(None, COL), P(ROW, None)),
        check_vma=False,
    )
```

```python
import jax
import jax.numpy as jnp
from jax import lax
from jax.experimental import pallas as pl
from jax.experimental.pallas import tpu as pltpu
from jax.sharding import Mesh
from jax.sharding import PartitionSpec as P

adapter_scale = 2.0
epsilon = 1e-06
bf16 = jnp.bfloat16
f32 = jnp.float32
ROW = ("x", "y")
COL = ("z", "c")
CHUNK = 512
RANK = 16
LANES = 128
MIB = 1024 * 1024
LIMIT = 62 * MIB
ANY = pl.BlockSpec(memory_space=pl.ANY)
SMEM = pl.BlockSpec(memory_space=pltpu.SMEM)


def pieces(value):
    high = value.astype(bf16)
    rest = value - high.astype(f32)
    mid = rest.astype(bf16)
    low = (rest - mid.astype(f32)).astype(bf16)
    return high, mid, low


def dot(left, right, left_dim, right_dim):
    return lax.dot_general(
        left, right, (((left_dim,), (right_dim,)), ((), ())), preferred_element_type=f32
    )


def three(left, right, left_dim, right_dim):
    out = dot(jnp.concatenate(pieces(left), axis=0), right, left_dim, right_dim)
    return out[:RANK] + out[RANK : 2 * RANK] + out[2 * RANK :]


def chunks_of(width):
    return [(at, min(CHUNK, width - at)) for at in range(0, width, CHUNK)]


def call(body, flops, moved, **options):
    return pl.pallas_call(
        body,
        compiler_params=pltpu.CompilerParams(vmem_limit_bytes=LIMIT),
        cost_estimate=pl.CostEstimate(flops=flops, bytes_accessed=moved, transcendentals=0),
        **options,
    )


def begin(source, target, sem):
    copy = pltpu.make_async_copy(source, target, sem)
    copy.start()
    return copy


def stream(pairs, sem, chunks):
    def copies(j):
        for i, (source, target) in enumerate(pairs):
            index = (slice(None),) * (len(target.shape) - 1) + (pl.ds(*chunks[j]),)
            yield pltpu.make_async_copy(source.at[index], target.at[index], sem.at[i, j])

    def start(j):
        if j < len(chunks):
            for copy in copies(j):
                copy.start()

    def ready(j):
        for copy in copies(j):
            copy.wait()
        start(j + 2)

    start(0)
    start(1)
    return ready


def in_rows(row):
    return [row[:, at : at + LANES] for at in range(0, row.shape[1], LANES)]


def in_line(rows, at, size):
    return jnp.concatenate(
        [rows[k : k + 1, :] for k in range(at // LANES, (at + size) // LANES)], axis=1
    )


def merge_kernel(
    down_hbm, up_hbm, weight_hbm, cot_hbm, merged_hbm, message_hbm,
    down, up, weight, cot, merged, extra, up_cat, totals, small_sem, in_sem, out_sem, copy_sem,
):
    depth, width = weight.shape
    rows, tile = 256, 256
    steps = [slice(at, at + rows) for at in range(0, depth, rows)]
    first = begin(up_hbm, up, small_sem.at[0]), begin(down_hbm, down, small_sem.at[1])
    fetches = [begin(weight_hbm.at[p], weight.at[p], in_sem.at[j]) for j, p in enumerate(steps)]
    later = begin(cot_hbm, cot, small_sem.at[2])
    totals[...] = jnp.zeros_like(totals)
    for copy in first:
        copy.wait()
    for at in range(0, width, tile):
        cols = slice(at, at + tile)
        u1, u2, u3 = pieces(up[:, cols])
        up_cat[:, cols] = jnp.concatenate([u1, u2, u1, u3, u1, u2], axis=0)
    d1, d2, d3 = pieces(down[...] * adapter_scale)
    down_cat = jnp.concatenate([d1, d1, d2, d1, d3, d2], axis=0)
    stores = []
    for j, part in enumerate(steps):
        fetches[j].wait()
        if j == len(steps) - 1:
            later.wait()
            for r in range(16):
                stores.append(begin(cot, message_hbm.at[r, :, :width], copy_sem.at[r]))
        for at in range(0, width, tile):
            cols = slice(at, at + tile)
            value = weight[part, cols].astype(f32) + dot(down_cat[:, part], up_cat[:, cols], 0, 0)
            merged[part, cols] = value.astype(bf16)
            totals[:, cols] += jnp.sum((value * value).reshape(rows // 8, 8, tile), axis=0)
        stores.append(begin(merged.at[part], merged_hbm.at[part], out_sem.at[j]))
    sums = in_rows(jnp.sum(totals[...], axis=0, keepdims=True))
    sums = jnp.concatenate(sums + [jnp.zeros((32 - len(sums), LANES), f32)], axis=0)
    high = sums.astype(bf16)
    rest = (sums - high.astype(f32)).astype(bf16)
    both = jnp.concatenate([high, rest], axis=1)
    extra[...] = jnp.broadcast_to(both[None], extra.shape)
    stores.append(begin(extra, message_hbm.at[:, :, width:], small_sem.at[0]))
    for copy in stores:
        copy.wait()


def merge(down_t, up, weight, cot):
    depth, width = weight.shape
    return call(
        merge_kernel,
        16 * 512 * depth * width,
        18 * MIB,
        in_specs=[ANY] * 4,
        out_specs=[ANY] * 2,
        out_shape=[
            jax.ShapeDtypeStruct((depth, width), bf16),
            jax.ShapeDtypeStruct((16, 32, width + 2 * LANES), bf16),
        ],
        scratch_shapes=[
            pltpu.VMEM((RANK, depth), f32),
            pltpu.VMEM((RANK, width), f32),
            pltpu.VMEM((depth, width), bf16),
            pltpu.VMEM((32, width), bf16),
            pltpu.VMEM((depth, width), bf16),
            pltpu.VMEM((16, 32, 2 * LANES), bf16),
            pltpu.VMEM((6 * RANK, width), bf16),
            pltpu.VMEM((8, width), f32),
            pltpu.SemaphoreType.DMA((3,)),
            pltpu.SemaphoreType.DMA((4,)),
            pltpu.SemaphoreType.DMA((4,)),
            pltpu.SemaphoreType.DMA((16,)),
        ],
        name="merge",
    )(down_t, up, weight, cot)


def forward_kernel(
    tokens_hbm, down_hbm, merged_hbm, part_hbm,
    tokens, down, merged, part, extra, first_sem, sem, out_sem,
):
    depth, width = merged.shape
    chunks = chunks_of(width)
    first = begin(tokens_hbm, tokens, first_sem.at[0]), begin(down_hbm, down, first_sem.at[1])
    ready = stream([(merged_hbm, merged)], sem, chunks)
    for copy in first:
        copy.wait()
    all_tokens = tokens[...].reshape(512, depth)
    proj = three(down[...], all_tokens, 1, 1).astype(bf16)
    proj = jnp.concatenate([proj[:, : 2 * LANES], proj[:, 2 * LANES :]], axis=0)
    extra[...] = jnp.broadcast_to(proj[None], extra.shape)
    beside = part_hbm.at[:, :, width : width + 2 * LANES]
    stores = [begin(extra, beside, first_sem.at[0])]
    for j, (at, size) in enumerate(chunks):
        ready(j)
        cols = slice(at, at + size)
        product = dot(all_tokens, merged[:, cols], 1, 0).astype(bf16)
        part[:, :, cols] = product.reshape(16, 32, size)
        stores.append(begin(part.at[:, :, cols], part_hbm.at[:, :, cols], out_sem.at[j]))
    for copy in stores:
        copy.wait()


def forward(tokens, down_t, merged_low):
    depth, width = merged_low.shape
    count = len(chunks_of(width))
    return call(
        forward_kernel,
        32 * 512 * depth * width,
        12 * MIB,
        in_specs=[ANY] * 3,
        out_specs=ANY,
        out_shape=jax.ShapeDtypeStruct((16, 32, width + 3 * LANES), bf16),
        scratch_shapes=[
            pltpu.VMEM((16, 32, depth), bf16),
            pltpu.VMEM((RANK, depth), f32),
            pltpu.VMEM((depth, width), bf16),
            pltpu.VMEM((16, 32, width), bf16),
            pltpu.VMEM((16, 32, 2 * LANES), bf16),
            pltpu.SemaphoreType.DMA((2,)),
            pltpu.SemaphoreType.DMA((1, count)),
            pltpu.SemaphoreType.DMA((count,)),
        ],
        name="forward",
    )(tokens, down_t, merged_low)


def magnitude_kernel(given_hbm, part_hbm, out_hbm, cot, part, extra, sem, out_sem):
    width = cot.shape[2]
    chunks = chunks_of(width)
    ready = stream([(given_hbm, cot), (part_hbm, part)], sem, chunks)
    rows = []
    for j, (at, size) in enumerate(chunks):
        ready(j)
        cols = slice(at, at + size)
        product = cot[:, :, cols].astype(f32) * part[:, :, cols].astype(f32)
        total = jnp.sum(product.reshape(64, 8, size), axis=0)
        rows += in_rows(jnp.sum(total, axis=0, keepdims=True))
    rows.append(jnp.zeros((32 - len(rows), LANES), f32))
    sums = jnp.concatenate(rows, axis=0).astype(bf16)
    extra[...] = jnp.broadcast_to(sums[None], extra.shape)
    begin(extra, out_hbm.at[:, :, width + 2 * LANES :], out_sem.at[0]).wait()


def add_magnitude(given, part):
    blocks, rows, width = given.shape
    width -= 2 * LANES
    return call(
        magnitude_kernel,
        4 * 512 * width,
        7 * MIB,
        in_specs=[ANY, ANY],
        out_specs=ANY,
        out_shape=jax.ShapeDtypeStruct(part.shape, bf16),
        scratch_shapes=[
            pltpu.VMEM((blocks, rows, width), bf16),
            pltpu.VMEM((blocks, rows, width), bf16),
            pltpu.VMEM((blocks, rows, LANES), bf16),
            pltpu.SemaphoreType.DMA((2, len(chunks_of(width)))),
            pltpu.SemaphoreType.DMA((1,)),
        ],
        input_output_aliases={1: 0},
        name="magnitude",
    )(given, part)


def pack(low, out):
    high = low.astype(bf16)
    rest = (low - high.astype(f32)).astype(bf16)
    out[:, :CHUNK] = high
    out[:, CHUNK:] = rest
    return high.astype(f32) + rest.astype(f32)


def unpack(got):
    got = got.astype(f32)
    return got[:, :CHUNK] + got[:, CHUNK:]


def backward_kernel(
    core_ref, magnitude_hbm, up_hbm, given_hbm, merged_hbm, own_hbm, send_hbm, scale_hbm,
    magnitude, squares, up, cot, merged, total, own, send, scale, first_sem, sem,
):
    core = core_ref[0]
    depth, width = merged.shape
    chunks = chunks_of(width)
    count = width // LANES
    first = (
        begin(given_hbm.at[:, :, width:], squares, first_sem.at[0]),
        begin(up_hbm, up, first_sem.at[1]),
        begin(magnitude_hbm, magnitude, first_sem.at[2]),
    )
    ready = stream([(given_hbm, cot), (merged_hbm, merged)], sem, chunks)
    for copy in first:
        copy.wait()
    sums = squares[0].astype(f32)
    for r in range(1, 16):
        sums += squares[r].astype(f32)
    norm = jnp.sqrt(sums[:, :LANES] + sums[:, LANES:] + epsilon)
    factors = magnitude[...] / norm[:count]
    scale[...] = jnp.zeros_like(scale)
    scale[:count, :] = factors
    scale[32:, :] = norm
    last = begin(scale, scale_hbm, first_sem.at[0])
    low = jnp.zeros((RANK, CHUNK), f32)
    for j, (at, size) in enumerate(chunks):
        ready(j)
        cols = slice(at, at + size)
        value = cot[:, :, cols].reshape(512, size).astype(f32)
        grad = (value * in_line(factors, at, size)).astype(bf16)
        product = dot(grad, merged[:, cols], 1, 1)
        if j == 0:
            total[...] = product
        else:
            total[...] += product
        low += three(up[:, cols], grad, 1, 1)
    for z in range(8):
        theirs = pl.ds(pl.multiple_of((2 * z + 1 - core) * 32, 32), 32)
        send[32 * z : 32 * z + 32, :] = total[theirs, :].astype(bf16)
    pack(low, send.at[256:272, :])
    first = begin(send, send_hbm, first_sem.at[1])
    for z in range(8):
        mine = pl.ds(pl.multiple_of((2 * z + core) * 32, 32), 32)
        own[32 * z : 32 * z + 32, :] = total[mine, :].astype(bf16)
    own[256:272, :] = send[256:272, :]
    begin(own, own_hbm, first_sem.at[2]).wait()
    first.wait()
    last.wait()


def backward(core, magnitude, up, given, merged_low):
    depth, width = merged_low.shape
    count = len(chunks_of(width))
    return call(
        backward_kernel,
        2 * 512 * depth * width,
        12 * MIB,
        in_specs=[SMEM] + [ANY] * 4,
        out_specs=[ANY] * 3,
        out_shape=[jax.ShapeDtypeStruct((272, depth), bf16)] * 2
        + [jax.ShapeDtypeStruct((64, LANES), f32)],
        scratch_shapes=[
            pltpu.VMEM(magnitude.shape, f32),
            pltpu.VMEM((16, 32, 2 * LANES), bf16),
            pltpu.VMEM((RANK, width), f32),
            pltpu.VMEM((16, 32, width), bf16),
            pltpu.VMEM((depth, width), bf16),
            pltpu.VMEM((512, depth), f32),
            pltpu.VMEM((272, depth), bf16),
            pltpu.VMEM((272, depth), bf16),
            pltpu.VMEM((64, LANES), f32),
            pltpu.SemaphoreType.DMA((3,)),
            pltpu.SemaphoreType.DMA((2, count)),
        ],
        name="backward",
    )(core, magnitude, up, given, merged_low)


def pair_kernel(z_ref, own_hbm, got_hbm, *refs):
    out_hbm = refs[:8]
    own, got, send, sem, out_sem = refs[8:]
    z = z_ref[0]
    copies = begin(own_hbm, own, sem.at[0]), begin(got_hbm, got, sem.at[1])
    for copy in copies:
        copy.wait()
    low = unpack(own[256:272, :]) + unpack(got[256:272, :])
    pack(low, send.at[0, 32:48, :])
    stores = []
    for k in [1, 7, 2, 6, 3, 5, 4, 0]:
        block = pl.ds(pl.multiple_of(lax.rem(z + k, 8) * 32, 32), 32)
        send[k, :32, :] = (own[block, :].astype(f32) + got[block, :].astype(f32)).astype(bf16)
        if k:
            send[k, 32:48, :] = send[0, 32:48, :]
        stores.append(begin(send.at[k], out_hbm[k], out_sem.at[k]))
    for copy in stores:
        copy.wait()


def pair(z, own, got):
    rows, depth = own.shape
    return call(
        pair_kernel,
        4 * rows * depth,
        6 * rows * depth,
        in_specs=[SMEM, ANY, ANY],
        out_specs=[ANY] * 8,
        out_shape=[jax.ShapeDtypeStruct((48, depth), bf16)] * 8,
        scratch_shapes=[
            pltpu.VMEM((rows, depth), bf16),
            pltpu.VMEM((rows, depth), bf16),
            pltpu.VMEM((8, 48, depth), bf16),
            pltpu.SemaphoreType.DMA((2,)),
            pltpu.SemaphoreType.DMA((8,)),
        ],
        name="pair",
    )(z, own, got)


def finish_kernel(z_ref, tokens_hbm, *refs):
    parts_hbm = refs[:8]
    grad_hbm, down_hbm, parts, tokens, lows, grad, down, sem, out_sem = refs[8:]
    z = z_ref[0]
    later = begin(tokens_hbm, tokens, sem.at[8])
    copies = [begin(parts_hbm[k], parts.at[k], sem.at[k]) for k in range(8)]
    for copy in copies:
        copy.wait()
    total = parts[0, :32, :].astype(f32)
    for k in range(1, 8):
        total += parts[k, :32, :].astype(f32)
    grad[...] = total.astype(bf16)
    first = begin(grad, grad_hbm, out_sem.at[0])
    for k in range(8):
        lows[lax.rem(z + 8 - k, 8)] = unpack(parts[k, 32:48, :])
    low = lows[0]
    for k in range(1, 8):
        low += lows[k]
    later.wait()
    down[...] = three(low * adapter_scale, tokens[...], 1, 0)
    begin(down, down_hbm, out_sem.at[1]).wait()
    first.wait()


def finish(z, tokens, parts):
    depth = tokens.shape[1]
    return call(
        finish_kernel,
        2 * 512 * 256 * depth,
        2 * MIB,
        in_specs=[SMEM] + [ANY] * 9,
        out_specs=[ANY, ANY],
        out_shape=[
            jax.ShapeDtypeStruct((32, depth), bf16),
            jax.ShapeDtypeStruct((RANK, depth), f32),
        ],
        scratch_shapes=[
            pltpu.VMEM((8, 48, depth), bf16),
            pltpu.VMEM(tokens.shape, bf16),
            pltpu.VMEM((8, RANK, CHUNK), f32),
            pltpu.VMEM((32, depth), bf16),
            pltpu.VMEM((RANK, depth), f32),
            pltpu.SemaphoreType.DMA((9,)),
            pltpu.SemaphoreType.DMA((2,)),
        ],
        name="finish",
    )(z, tokens, *parts)


def output_kernel(
    scale_hbm, given_hbm, parts_hbm, out_hbm, mag_hbm, up_hbm,
    scale, cot, parts, out, mag, up, first_sem, sem, out_sem,
):
    width = out.shape[1]
    chunks = chunks_of(width)
    count = width // LANES
    first = (
        begin(scale_hbm, scale, first_sem.at[0]),
        begin(parts_hbm.at[:, :, width:], parts.at[:, :, width:], first_sem.at[1]),
    )
    ready = stream([(given_hbm, cot), (parts_hbm, parts.at[:, :, :width])], sem, chunks)
    for copy in first:
        copy.wait()

    def added(cols):
        total = parts[0, :, cols].astype(f32)
        for r in range(1, 16):
            total += parts[r, :, cols].astype(f32)
        return total

    extra = added(slice(width, width + 3 * LANES))
    proj = jnp.concatenate([extra[:16, : 2 * LANES], extra[16:, : 2 * LANES]], axis=1)
    proj = proj * adapter_scale
    mag[...] = extra[:count, 2 * LANES :] / scale[32 : 32 + count, :]
    stores = [begin(mag, mag_hbm, first_sem.at[0])]
    factors = scale[:32, :]
    for j, (at, size) in enumerate(chunks):
        ready(j)
        cols = slice(at, at + size)
        factor = in_line(factors, at, size)
        out[:, cols] = (added(cols) * factor).astype(bf16)
        stores.append(begin(out.at[:, cols], out_hbm.at[:, cols], out_sem.at[0, j]))
        value = cot[:, :, cols].reshape(512, size).astype(f32)
        up[:, cols] = three(proj, (value * factor).astype(bf16), 1, 0)
        stores.append(begin(up.at[:, cols], up_hbm.at[:, cols], out_sem.at[1, j]))
    for copy in stores:
        copy.wait()


def output_of(scale, given, parts):
    width = given.shape[2] - 2 * LANES
    count = len(chunks_of(width))
    return call(
        output_kernel,
        2 * 512 * 256 * width,
        8 * MIB,
        in_specs=[ANY] * 3,
        out_specs=[ANY] * 3,
        out_shape=[
            jax.ShapeDtypeStruct((32, width), bf16),
            jax.ShapeDtypeStruct((width // LANES, LANES), f32),
            jax.ShapeDtypeStruct((RANK, width), f32),
        ],
        scratch_shapes=[
            pltpu.VMEM(scale.shape, f32),
            pltpu.VMEM((16, 32, width), bf16),
            pltpu.VMEM(parts.shape, bf16),
            pltpu.VMEM((32, width), bf16),
            pltpu.VMEM((width // LANES, LANES), f32),
            pltpu.VMEM((RANK, width), f32),
            pltpu.SemaphoreType.DMA((2,)),
            pltpu.SemaphoreType.DMA((2, count)),
            pltpu.SemaphoreType.DMA((2, count)),
        ],
        name="output",
    )(scale, given, parts)


def exchange(blocks):
    return lax.all_to_all(blocks, ROW, 0, 0, tiled=False)


def on_device(tokens, weight, down_adapter, up_adapter, magnitude, out_cotangent):
    z, core = [lax.axis_index(name).astype(jnp.int32).reshape(1) for name in COL]
    down_t = down_adapter.T
    magnitude = magnitude.reshape(-1, LANES)
    tokens_full = lax.all_gather(tokens, COL, axis=0)
    merged_low, message = merge(down_t, up_adapter, weight, out_cotangent)
    given = exchange(message)
    part = forward(tokens_full, down_t, merged_low)
    part = add_magnitude(given, part)
    parts = exchange(part)
    own, send, scale = backward(core, magnitude, up_adapter, given, merged_low)
    got = lax.ppermute(send, "c", [(0, 1), (1, 0)])
    blocks = list(pair(z, own, got))
    for k in range(1, 8):
        blocks[k] = lax.ppermute(blocks[k], "z", [(i, (i + k) % 8) for i in range(8)])
    grad_tokens, down_gradient = finish(z, tokens_full.reshape(512, -1), blocks)
    output, grad_magnitude, up_gradient = output_of(scale, given, parts)
    return (output, grad_tokens, grad_magnitude.reshape(-1), up_gradient, down_gradient.T)


def solution(mesh):
    split = Mesh(mesh.devices.reshape(4, 4, 8, 2), ROW + COL)
    return jax.shard_map(
        on_device,
        mesh=split,
        in_specs=(P(COL, ROW), P(ROW, COL), P(ROW, None), P(None, COL), P(COL), P(ROW, COL)),
        out_specs=(P(ROW, COL), P(COL, ROW), P(COL), P(None, COL), P(ROW, None)),
        check_vma=False,
    )
```

```python
import jax
import jax.numpy as jnp
from jax import lax
from jax.experimental import pallas as pl
from jax.experimental.pallas import tpu as pltpu
from jax.sharding import Mesh
from jax.sharding import PartitionSpec as P

adapter_scale = 2.0
epsilon = 1e-06
bf16 = jnp.bfloat16
f32 = jnp.float32
ROW = ("x", "y")
COL = ("z", "c")
CHUNK = 512
RANK = 16
LANES = 128
MIB = 1024 * 1024
LIMIT = 62 * MIB
ANY = pl.BlockSpec(memory_space=pl.ANY)
SMEM = pl.BlockSpec(memory_space=pltpu.SMEM)


def pieces(value):
    high = value.astype(bf16)
    rest = value - high.astype(f32)
    mid = rest.astype(bf16)
    low = (rest - mid.astype(f32)).astype(bf16)
    return high, mid, low


def dot(left, right, left_dim, right_dim):
    return lax.dot_general(
        left, right, (((left_dim,), (right_dim,)), ((), ())), preferred_element_type=f32
    )


def three(left, right, left_dim, right_dim):
    out = dot(jnp.concatenate(pieces(left), axis=0), right, left_dim, right_dim)
    return out[:RANK] + out[RANK : 2 * RANK] + out[2 * RANK :]


def chunks_of(width):
    return [(at, min(CHUNK, width - at)) for at in range(0, width, CHUNK)]


def call(body, flops, moved, **options):
    return pl.pallas_call(
        body,
        compiler_params=pltpu.CompilerParams(vmem_limit_bytes=LIMIT),
        cost_estimate=pl.CostEstimate(flops=flops, bytes_accessed=moved, transcendentals=0),
        **options,
    )


def begin(source, target, sem):
    copy = pltpu.make_async_copy(source, target, sem)
    copy.start()
    return copy


def stream(pairs, sem, chunks, depth=2):
    def copies(j):
        for i, (source, target) in enumerate(pairs):
            index = (slice(None),) * (len(target.shape) - 1) + (pl.ds(*chunks[j]),)
            yield pltpu.make_async_copy(source.at[index], target.at[index], sem.at[i, j])

    def start(j):
        if j < len(chunks):
            for copy in copies(j):
                copy.start()

    def ready(j):
        for copy in copies(j):
            copy.wait()
        start(j + depth)

    for j in range(depth):
        start(j)
    return ready


def in_rows(row):
    return [row[:, at : at + LANES] for at in range(0, row.shape[1], LANES)]


def in_line(rows, at, size):
    return jnp.concatenate(
        [rows[k : k + 1, :] for k in range(at // LANES, (at + size) // LANES)], axis=1
    )


def merge_kernel(
    down_hbm, up_hbm, weight_hbm, merged_hbm, sums_hbm,
    down, up, weight, merged, sums, up_cat, totals, small_sem, in_sem, out_sem,
):
    depth, width = weight.shape
    rows, tile = 256, 256
    steps = [slice(at, at + rows) for at in range(0, depth, rows)]
    first = begin(up_hbm, up, small_sem.at[0]), begin(down_hbm, down, small_sem.at[1])
    fetches = [begin(weight_hbm.at[p], weight.at[p], in_sem.at[j]) for j, p in enumerate(steps)]
    totals[...] = jnp.zeros_like(totals)
    for copy in first:
        copy.wait()
    for at in range(0, width, tile):
        cols = slice(at, at + tile)
        u1, u2, u3 = pieces(up[:, cols])
        up_cat[:, cols] = jnp.concatenate([u1, u2, u1, u3, u1, u2], axis=0)
    d1, d2, d3 = pieces(down[...] * adapter_scale)
    down_cat = jnp.concatenate([d1, d1, d2, d1, d3, d2], axis=0)
    stores = []
    for j, part in enumerate(steps):
        fetches[j].wait()
        for at in range(0, width, tile):
            cols = slice(at, at + tile)
            value = weight[part, cols].astype(f32) + dot(down_cat[:, part], up_cat[:, cols], 0, 0)
            merged[part, cols] = value.astype(bf16)
            totals[:, cols] += jnp.sum((value * value).reshape(rows // 8, 8, tile), axis=0)
        stores.append(begin(merged.at[part], merged_hbm.at[part], out_sem.at[j]))
    lines = in_rows(jnp.sum(totals[...], axis=0, keepdims=True))
    sums[...] = jnp.concatenate(lines + [jnp.zeros((32 - len(lines), LANES), f32)], axis=0)
    stores.append(begin(sums, sums_hbm, small_sem.at[0]))
    for copy in stores:
        copy.wait()


def merge(down_t, up, weight):
    depth, width = weight.shape
    return call(
        merge_kernel,
        12 * depth * width,
        4 * depth * width,
        in_specs=[ANY] * 3,
        out_specs=[ANY] * 2,
        out_shape=[
            jax.ShapeDtypeStruct((depth, width), bf16),
            jax.ShapeDtypeStruct((32, LANES), f32),
        ],
        scratch_shapes=[
            pltpu.VMEM((RANK, depth), f32),
            pltpu.VMEM((RANK, width), f32),
            pltpu.VMEM((depth, width), bf16),
            pltpu.VMEM((depth, width), bf16),
            pltpu.VMEM((32, LANES), f32),
            pltpu.VMEM((6 * RANK, width), bf16),
            pltpu.VMEM((8, width), f32),
            pltpu.SemaphoreType.DMA((2,)),
            pltpu.SemaphoreType.DMA((4,)),
            pltpu.SemaphoreType.DMA((4,)),
        ],
        name="merge",
    )(down_t, up, weight)


def forward_kernel(
    core_ref, own_hbm, other_hbm, down_hbm, sums_hbm, merged_hbm, part_hbm, tokens_hbm, small_hbm,
    tokens, down, small, merged, part, first_sem, sem, out_sem,
):
    core = core_ref[0]
    depth, width = merged.shape
    chunks = chunks_of(width)
    first = (
        begin(own_hbm, tokens.at[:, core], first_sem.at[0]),
        begin(other_hbm, tokens.at[:, 1 - core], first_sem.at[1]),
        begin(down_hbm, down, first_sem.at[2]),
        begin(sums_hbm, small.at[64:], first_sem.at[3]),
    )
    ready = stream([(merged_hbm, merged)], sem, chunks)
    for copy in first:
        copy.wait()
    all_tokens = tokens[...].reshape(512, depth)
    proj = three(down[...], all_tokens, 1, 1)
    for k in range(4):
        small[RANK * k : RANK * k + RANK, :] = proj[:, LANES * k : LANES * k + LANES]
    stores = [
        begin(small, small_hbm, first_sem.at[0]),
        begin(tokens, tokens_hbm, first_sem.at[1]),
    ]
    for j, (at, size) in enumerate(chunks):
        ready(j)
        cols = slice(at, at + size)
        product = dot(all_tokens, merged[:, cols], 1, 0).astype(bf16)
        part[:, :, cols] = product.reshape(16, 32, size)
        stores.append(begin(part.at[:, :, cols], part_hbm.at[:, :, cols], out_sem.at[j]))
    for copy in stores:
        copy.wait()


def forward(core, own, other, down_t, sums, merged_low):
    depth, width = merged_low.shape
    count = len(chunks_of(width))
    return call(
        forward_kernel,
        2 * 512 * depth * width,
        12 * MIB,
        in_specs=[SMEM] + [ANY] * 5,
        out_specs=[ANY] * 3,
        out_shape=[
            jax.ShapeDtypeStruct((16, 32, width + LANES), bf16),
            jax.ShapeDtypeStruct((8, 2, 32, depth), bf16),
            jax.ShapeDtypeStruct((96, LANES), f32),
        ],
        scratch_shapes=[
            pltpu.VMEM((8, 2, 32, depth), bf16),
            pltpu.VMEM((RANK, depth), f32),
            pltpu.VMEM((96, LANES), f32),
            pltpu.VMEM((depth, width), bf16),
            pltpu.VMEM((16, 32, width), bf16),
            pltpu.SemaphoreType.DMA((4,)),
            pltpu.SemaphoreType.DMA((1, count)),
            pltpu.SemaphoreType.DMA((count,)),
        ],
        name="forward",
    )(core, own, other, down_t, sums, merged_low)


def magnitude_kernel(given_hbm, part_hbm, out_hbm, cot, part, extra, sem, out_sem):
    width = cot.shape[2]
    chunks = chunks_of(width)
    ready = stream([(given_hbm, cot), (part_hbm, part)], sem, chunks, len(chunks))
    rows = []
    for j, (at, size) in enumerate(chunks):
        ready(j)
        cols = slice(at, at + size)
        product = cot[:, :, cols].astype(f32) * part[:, :, cols].astype(f32)
        total = jnp.sum(product.reshape(64, 8, size), axis=0)
        rows += in_rows(jnp.sum(total, axis=0, keepdims=True))
    rows.append(jnp.zeros((32 - len(rows), LANES), f32))
    sums = jnp.concatenate(rows, axis=0).astype(bf16)
    extra[...] = jnp.broadcast_to(sums[None], extra.shape)
    begin(extra, out_hbm.at[:, :, width:], out_sem.at[0]).wait()


def add_magnitude(given, part):
    blocks, rows, width = given.shape
    return call(
        magnitude_kernel,
        4 * 512 * width,
        7 * MIB,
        in_specs=[ANY, ANY],
        out_specs=ANY,
        out_shape=jax.ShapeDtypeStruct(part.shape, bf16),
        scratch_shapes=[
            pltpu.VMEM((blocks, rows, width), bf16),
            pltpu.VMEM((blocks, rows, width), bf16),
            pltpu.VMEM((blocks, rows, LANES), bf16),
            pltpu.SemaphoreType.DMA((2, len(chunks_of(width)))),
            pltpu.SemaphoreType.DMA((1,)),
        ],
        input_output_aliases={1: 0},
        name="magnitude",
    )(given, part)


def pack(low, out):
    high = low.astype(bf16)
    rest = (low - high.astype(f32)).astype(bf16)
    out[:, :CHUNK] = high
    out[:, CHUNK:] = rest
    return high.astype(f32) + rest.astype(f32)


def unpack(got):
    got = got.astype(f32)
    return got[:, :CHUNK] + got[:, CHUNK:]


def backward_kernel(
    core_ref, small_hbm, magnitude_hbm, up_hbm, given_hbm, merged_hbm, own_hbm, send_hbm, scale_hbm,
    squares, magnitude, up, cot, merged, total, low_total, own, send, scale, first_sem, sem,
):
    core = core_ref[0]
    depth, width = merged.shape
    chunks = chunks_of(width)
    count = width // LANES
    first = (
        begin(small_hbm.at[64:], squares, first_sem.at[0]),
        begin(up_hbm, up, first_sem.at[1]),
        begin(magnitude_hbm, magnitude, first_sem.at[2]),
    )
    ready = stream([(given_hbm, cot), (merged_hbm, merged)], sem, chunks)
    for copy in first:
        copy.wait()
    norm = jnp.sqrt(squares[...] + epsilon)
    factors = magnitude[...] / norm[:count]
    scale[...] = jnp.zeros_like(scale)
    scale[:count, :] = factors
    scale[32:, :] = norm
    last = begin(scale, scale_hbm, first_sem.at[0])
    blank = jnp.zeros((LANES - 3 * RANK, CHUNK), bf16)
    for j, (at, size) in enumerate(chunks):
        ready(j)
        cols = slice(at, at + size)
        value = cot[:, :, cols].reshape(512, size).astype(f32)
        grad = (value * in_line(factors, at, size)).astype(bf16)
        product = dot(grad, merged[:, cols], 1, 1)
        up_cat = jnp.concatenate([*pieces(up[:, cols]), blank[:, :size]], axis=0)
        low = dot(grad, up_cat, 1, 1)
        if j == 0:
            total[...] = product
            low_total[...] = low
        else:
            total[...] += product
            low_total[...] += low
    for z in range(8):
        theirs = pl.ds(pl.multiple_of((2 * z + 1 - core) * 32, 32), 32)
        send[32 * z : 32 * z + 32, :] = total[theirs, :].astype(bf16)
    low = low_total[...].T
    low = low[:RANK] + low[RANK : 2 * RANK] + low[2 * RANK : 3 * RANK]
    pack(low, send.at[256:272, :])
    first = begin(send, send_hbm, first_sem.at[1])
    for z in range(8):
        mine = pl.ds(pl.multiple_of((2 * z + core) * 32, 32), 32)
        own[32 * z : 32 * z + 32, :] = total[mine, :].astype(bf16)
    own[256:272, :] = send[256:272, :]
    begin(own, own_hbm, first_sem.at[2]).wait()
    first.wait()
    last.wait()


def backward(core, small, magnitude, up, given, merged_low):
    depth, width = merged_low.shape
    count = len(chunks_of(width))
    return call(
        backward_kernel,
        2 * 512 * depth * width,
        12 * MIB,
        in_specs=[SMEM] + [ANY] * 5,
        out_specs=[ANY] * 3,
        out_shape=[jax.ShapeDtypeStruct((272, depth), bf16)] * 2
        + [jax.ShapeDtypeStruct((64, LANES), f32)],
        scratch_shapes=[
            pltpu.VMEM((32, LANES), f32),
            pltpu.VMEM(magnitude.shape, f32),
            pltpu.VMEM((RANK, width), f32),
            pltpu.VMEM((16, 32, width), bf16),
            pltpu.VMEM((depth, width), bf16),
            pltpu.VMEM((512, depth), f32),
            pltpu.VMEM((512, LANES), f32),
            pltpu.VMEM((272, depth), bf16),
            pltpu.VMEM((272, depth), bf16),
            pltpu.VMEM((64, LANES), f32),
            pltpu.SemaphoreType.DMA((3,)),
            pltpu.SemaphoreType.DMA((2, count)),
        ],
        name="backward",
    )(core, small, magnitude, up, given, merged_low)


def pair_kernel(z_ref, own_hbm, got_hbm, keep_hbm, send_hbm, own, got, keep, send, sem, out_sem):
    bit = lax.rem(z_ref[0], 2)
    copies = begin(own_hbm, own, sem.at[0]), begin(got_hbm, got, sem.at[1])
    for copy in copies:
        copy.wait()
    low = unpack(own[256:272, :]) + unpack(got[256:272, :])
    pack(low, send.at[128:144, :])
    keep[128:144, :] = send[128:144, :]
    stores = []
    for target, other, out in ((send, 1 - bit, send_hbm), (keep, bit, keep_hbm)):
        for i in range(4):
            block = pl.ds(pl.multiple_of((2 * i + other) * 32, 32), 32)
            value = own[block, :].astype(f32) + got[block, :].astype(f32)
            target[32 * i : 32 * i + 32, :] = value.astype(bf16)
        stores.append(begin(target, out, out_sem.at[len(stores)]))
    for copy in stores:
        copy.wait()


def pair(z, own, got):
    rows, depth = own.shape
    return call(
        pair_kernel,
        4 * rows * depth,
        6 * rows * depth,
        in_specs=[SMEM, ANY, ANY],
        out_specs=[ANY] * 2,
        out_shape=[jax.ShapeDtypeStruct((144, depth), bf16)] * 2,
        scratch_shapes=[pltpu.VMEM((rows, depth), bf16)] * 2
        + [pltpu.VMEM((144, depth), bf16)] * 2
        + [pltpu.SemaphoreType.DMA((2,))] * 2,
        name="pair",
    )(z, own, got)


def quad_kernel(z_ref, keep_hbm, got_hbm, *refs):
    out_hbm = refs[:4]
    keep, got, send, sem, out_sem = refs[4:]
    half = z_ref[0] // 2
    copies = begin(keep_hbm, keep, sem.at[0]), begin(got_hbm, got, sem.at[1])
    for copy in copies:
        copy.wait()
    low = unpack(keep[128:144, :]) + unpack(got[128:144, :])
    pack(low, send.at[0, 32:48, :])
    stores = []
    for k in [2, 1, 3, 0]:
        block = pl.ds(pl.multiple_of(lax.rem(half + k, 4) * 32, 32), 32)
        send[k, :32, :] = (keep[block, :].astype(f32) + got[block, :].astype(f32)).astype(bf16)
        if k:
            send[k, 32:48, :] = send[0, 32:48, :]
        stores.append(begin(send.at[k], out_hbm[k], out_sem.at[k]))
    for copy in stores:
        copy.wait()


def quad(z, keep, got):
    rows, depth = keep.shape
    return call(
        quad_kernel,
        4 * rows * depth,
        6 * rows * depth,
        in_specs=[SMEM, ANY, ANY],
        out_specs=[ANY] * 4,
        out_shape=[jax.ShapeDtypeStruct((48, depth), bf16)] * 4,
        scratch_shapes=[pltpu.VMEM((rows, depth), bf16)] * 2
        + [pltpu.VMEM((4, 48, depth), bf16)]
        + [pltpu.SemaphoreType.DMA((2,)), pltpu.SemaphoreType.DMA((4,))],
        name="quad",
    )(z, keep, got)


def finish_kernel(z_ref, tokens_hbm, *refs):
    parts_hbm = refs[:4]
    grad_hbm, down_hbm, parts, tokens, lows, grad, down, sem, out_sem = refs[4:]
    half = z_ref[0] // 2
    copies = [begin(parts_hbm[k], parts.at[k], sem.at[k]) for k in range(4)]
    later = begin(tokens_hbm, tokens, sem.at[4])
    for copy in copies:
        copy.wait()
    total = parts[0, :32, :].astype(f32)
    for k in range(1, 4):
        total += parts[k, :32, :].astype(f32)
    grad[...] = total.astype(bf16)
    first = begin(grad, grad_hbm, out_sem.at[0])
    for k in range(4):
        lows[lax.rem(half + 4 - k, 4)] = unpack(parts[k, 32:48, :])
    low = (lows[0] + lows[1]) + (lows[2] + lows[3])
    later.wait()
    down[...] = three(low * adapter_scale, tokens[...], 1, 0)
    begin(down, down_hbm, out_sem.at[1]).wait()
    first.wait()


def finish(z, tokens, parts):
    depth = tokens.shape[1]
    return call(
        finish_kernel,
        2 * 512 * 256 * depth,
        2 * MIB,
        in_specs=[SMEM] + [ANY] * 5,
        out_specs=[ANY, ANY],
        out_shape=[
            jax.ShapeDtypeStruct((32, depth), bf16),
            jax.ShapeDtypeStruct((RANK, depth), f32),
        ],
        scratch_shapes=[
            pltpu.VMEM((4, 48, depth), bf16),
            pltpu.VMEM(tokens.shape, bf16),
            pltpu.VMEM((4, RANK, CHUNK), f32),
            pltpu.VMEM((32, depth), bf16),
            pltpu.VMEM((RANK, depth), f32),
            pltpu.SemaphoreType.DMA((5,)),
            pltpu.SemaphoreType.DMA((2,)),
        ],
        name="finish",
    )(z, tokens, *parts)


def up_kernel(
    small_hbm, scale_hbm, given_hbm, out_hbm, small, scale, cot, out, first_sem, sem, out_sem
):
    width = cot.shape[2]
    chunks = chunks_of(width)
    first = begin(small_hbm, small, first_sem.at[0]), begin(scale_hbm, scale, first_sem.at[1])
    ready = stream([(given_hbm, cot)], sem, chunks, 3)
    for copy in first:
        copy.wait()
    proj = [small[RANK * k : RANK * k + RANK, :] for k in range(4)]
    proj = jnp.concatenate(proj, axis=1) * adapter_scale
    factors = scale[:32, :]
    stores = []
    for j, (at, size) in enumerate(chunks):
        ready(j)
        cols = slice(at, at + size)
        value = cot[:, :, cols].reshape(512, size).astype(f32)
        grad = (value * in_line(factors, at, size)).astype(bf16)
        out[:, cols] = three(proj, grad, 1, 0)
        stores.append(begin(out.at[:, cols], out_hbm.at[:, cols], out_sem.at[j]))
    for copy in stores:
        copy.wait()


def up_gradient_of(small, scale, given):
    width = given.shape[2]
    count = len(chunks_of(width))
    return call(
        up_kernel,
        2 * 512 * 256 * width,
        4 * MIB,
        in_specs=[ANY] * 3,
        out_specs=ANY,
        out_shape=jax.ShapeDtypeStruct((RANK, width), f32),
        scratch_shapes=[
            pltpu.VMEM(small.shape, f32),
            pltpu.VMEM(scale.shape, f32),
            pltpu.VMEM(given.shape, bf16),
            pltpu.VMEM((RANK, width), f32),
            pltpu.SemaphoreType.DMA((2,)),
            pltpu.SemaphoreType.DMA((1, count)),
            pltpu.SemaphoreType.DMA((count,)),
        ],
        name="up_gradient",
    )(small, scale, given)


def output_kernel(
    scale_hbm, parts_hbm, out_hbm, mag_hbm, scale, parts, out, mag, first_sem, sem, out_sem
):
    width = out.shape[1]
    chunks = chunks_of(width)
    count = width // LANES
    first = (
        begin(scale_hbm, scale, first_sem.at[0]),
        begin(parts_hbm.at[:, :, width:], parts.at[:, :, width:], first_sem.at[1]),
    )
    ready = stream([(parts_hbm, parts.at[:, :, :width])], sem, chunks, 4)
    for copy in first:
        copy.wait()

    def added(cols):
        total = parts[0, :, cols].astype(f32)
        for r in range(1, 16):
            total += parts[r, :, cols].astype(f32)
        return total

    mag[...] = added(slice(width, width + LANES))[:count] / scale[32 : 32 + count, :]
    stores = [begin(mag, mag_hbm, first_sem.at[0])]
    factors = scale[:32, :]
    for j, (at, size) in enumerate(chunks):
        ready(j)
        cols = slice(at, at + size)
        out[:, cols] = (added(cols) * in_line(factors, at, size)).astype(bf16)
        stores.append(begin(out.at[:, cols], out_hbm.at[:, cols], out_sem.at[j]))
    for copy in stores:
        copy.wait()


def output_of(scale, parts):
    width = parts.shape[2] - LANES
    count = len(chunks_of(width))
    return call(
        output_kernel,
        16 * 32 * width,
        4 * MIB,
        in_specs=[ANY] * 2,
        out_specs=[ANY] * 2,
        out_shape=[
            jax.ShapeDtypeStruct((32, width), bf16),
            jax.ShapeDtypeStruct((width // LANES, LANES), f32),
        ],
        scratch_shapes=[
            pltpu.VMEM(scale.shape, f32),
            pltpu.VMEM(parts.shape, bf16),
            pltpu.VMEM((32, width), bf16),
            pltpu.VMEM((width // LANES, LANES), f32),
            pltpu.SemaphoreType.DMA((2,)),
            pltpu.SemaphoreType.DMA((1, count)),
            pltpu.SemaphoreType.DMA((count,)),
        ],
        name="output",
    )(scale, parts)


def exchange(blocks, axis):
    return lax.all_to_all(blocks, axis, 0, 0, tiled=False)


def around(value, axis):
    one, two, other = [
        lax.ppermute(value, axis, [(i, (i + k) % 4) for i in range(4)]) for k in (1, 2, 3)
    ]
    return (value + two) + (one + other)


def on_device(tokens, weight, down_adapter, up_adapter, magnitude, out_cotangent):
    z, core = [lax.axis_index(name).astype(jnp.int32).reshape(1) for name in COL]
    swap = [(0, 1), (1, 0)]
    down_t = down_adapter.T
    magnitude = magnitude.reshape(-1, LANES)
    given = lax.all_gather(out_cotangent, ROW, axis=0)
    own_tokens = exchange(jnp.broadcast_to(tokens[None], (8,) + tokens.shape), "z")
    merged_low, sums = merge(down_t, up_adapter, weight)
    own_tokens, merged_low, sums = lax.optimization_barrier((own_tokens, merged_low, sums))
    other_tokens = lax.ppermute(own_tokens, "c", swap)
    part, tokens_full, small = forward(core, own_tokens, other_tokens, down_t, sums, merged_low)
    small = around(around(small, "x"), "y")
    small, part, given = lax.optimization_barrier((small, part, given))
    part = add_magnitude(given, part)
    parts = exchange(part, ROW)
    own, send, scale = backward(core, small, magnitude, up_adapter, given, merged_low)
    got = lax.ppermute(send, "c", swap)
    keep, send = pair(z, own, got)
    got = lax.ppermute(send, "z", [(i, i ^ 1) for i in range(8)])
    blocks = list(quad(z, keep, got))
    for k in range(1, 4):
        blocks[k] = lax.ppermute(blocks[k], "z", [(i, (i + 2 * k) % 8) for i in range(8)])
    up_gradient = up_gradient_of(small, scale, given)
    grad_tokens, down_gradient = finish(z, tokens_full.reshape(512, -1), blocks)
    output, grad_magnitude = output_of(scale, parts)
    return (output, grad_tokens, grad_magnitude.reshape(-1), up_gradient, down_gradient.T)


def solution(mesh):
    split = Mesh(mesh.devices.reshape(4, 4, 8, 2), ROW + COL)
    return jax.shard_map(
        on_device,
        mesh=split,
        in_specs=(P(COL, ROW), P(ROW, COL), P(ROW, None), P(None, COL), P(COL), P(ROW, COL)),
        out_specs=(P(ROW, COL), P(COL, ROW), P(COL), P(None, COL), P(ROW, None)),
        check_vma=False,
    )
```

```python
import jax
import jax.numpy as jnp
from jax import lax
from jax.experimental import pallas as pl
from jax.experimental.pallas import tpu as pltpu
from jax.sharding import Mesh
from jax.sharding import PartitionSpec as P

adapter_scale = 2.0
epsilon = 1e-06
bf16 = jnp.bfloat16
f32 = jnp.float32
ROW = ("x", "y")
COL = ("z", "c")
CHUNK = 512
RANK = 16
LANES = 128
MIB = 1024 * 1024
LIMIT = 62 * MIB
ANY = pl.BlockSpec(memory_space=pl.ANY)
SMEM = pl.BlockSpec(memory_space=pltpu.SMEM)


def pieces(value):
    high = value.astype(bf16)
    rest = value - high.astype(f32)
    mid = rest.astype(bf16)
    low = (rest - mid.astype(f32)).astype(bf16)
    return high, mid, low


def dot(left, right, left_dim, right_dim):
    return lax.dot_general(
        left, right, (((left_dim,), (right_dim,)), ((), ())), preferred_element_type=f32
    )


def three(left, right, left_dim, right_dim):
    out = dot(jnp.concatenate(pieces(left), axis=0), right, left_dim, right_dim)
    return out[:RANK] + out[RANK : 2 * RANK] + out[2 * RANK :]


def chunks_of(width):
    return [(at, min(CHUNK, width - at)) for at in range(0, width, CHUNK)]


def call(body, flops, moved, **options):
    return pl.pallas_call(
        body,
        compiler_params=pltpu.CompilerParams(vmem_limit_bytes=LIMIT),
        cost_estimate=pl.CostEstimate(flops=flops, bytes_accessed=moved, transcendentals=0),
        **options,
    )


def begin(source, target, sem):
    copy = pltpu.make_async_copy(source, target, sem)
    copy.start()
    return copy


def stream(pairs, sem, chunks, depth=2):
    def copies(j):
        for i, (source, target) in enumerate(pairs):
            index = (slice(None),) * (len(target.shape) - 1) + (pl.ds(*chunks[j]),)
            yield pltpu.make_async_copy(source.at[index], target.at[index], sem.at[i, j])

    def start(j):
        if j < len(chunks):
            for copy in copies(j):
                copy.start()

    def ready(j):
        for copy in copies(j):
            copy.wait()
        start(j + depth)

    for j in range(depth):
        start(j)
    return ready


def in_rows(row):
    return [row[:, at : at + LANES] for at in range(0, row.shape[1], LANES)]


def in_line(rows, at, size):
    return jnp.concatenate(
        [rows[k : k + 1, :] for k in range(at // LANES, (at + size) // LANES)], axis=1
    )


def merge_kernel(
    after_hbm, down_hbm, up_hbm, weight_hbm, merged_hbm, sums_hbm,
    down, up, weight, merged, sums, up_cat, totals, small_sem, in_sem, out_sem,
):
    depth, width = weight.shape
    rows, tile = 256, 256
    steps = [slice(at, at + rows) for at in range(0, depth, rows)]
    first = begin(up_hbm, up, small_sem.at[0]), begin(down_hbm, down, small_sem.at[1])
    fetches = [begin(weight_hbm.at[p], weight.at[p], in_sem.at[j]) for j, p in enumerate(steps)]
    totals[...] = jnp.zeros_like(totals)
    for copy in first:
        copy.wait()
    for at in range(0, width, tile):
        cols = slice(at, at + tile)
        u1, u2, u3 = pieces(up[:, cols])
        up_cat[:, cols] = jnp.concatenate([u1, u2, u1, u3, u1, u2], axis=0)
    d1, d2, d3 = pieces(down[...] * adapter_scale)
    down_cat = jnp.concatenate([d1, d1, d2, d1, d3, d2], axis=0)
    stores = []
    for j, part in enumerate(steps):
        fetches[j].wait()
        for at in range(0, width, tile):
            cols = slice(at, at + tile)
            value = weight[part, cols].astype(f32) + dot(down_cat[:, part], up_cat[:, cols], 0, 0)
            merged[part, cols] = value.astype(bf16)
            totals[:, cols] += jnp.sum((value * value).reshape(rows // 8, 8, tile), axis=0)
        stores.append(begin(merged.at[part], merged_hbm.at[part], out_sem.at[j]))
    lines = in_rows(jnp.sum(totals[...], axis=0, keepdims=True))
    sums[...] = jnp.concatenate(lines + [jnp.zeros((32 - len(lines), LANES), f32)], axis=0)
    stores.append(begin(sums, sums_hbm, small_sem.at[0]))
    for copy in stores:
        copy.wait()


def merge(after, down_t, up, weight):
    depth, width = weight.shape
    return call(
        merge_kernel,
        12 * depth * width,
        4 * depth * width,
        in_specs=[ANY] * 4,
        out_specs=[ANY] * 2,
        out_shape=[
            jax.ShapeDtypeStruct((depth, width), bf16),
            jax.ShapeDtypeStruct((32, LANES), f32),
        ],
        scratch_shapes=[
            pltpu.VMEM((RANK, depth), f32),
            pltpu.VMEM((RANK, width), f32),
            pltpu.VMEM((depth, width), bf16),
            pltpu.VMEM((depth, width), bf16),
            pltpu.VMEM((32, LANES), f32),
            pltpu.VMEM((6 * RANK, width), bf16),
            pltpu.VMEM((8, width), f32),
            pltpu.SemaphoreType.DMA((2,)),
            pltpu.SemaphoreType.DMA((4,)),
            pltpu.SemaphoreType.DMA((4,)),
        ],
        name="merge",
    )(after, down_t, up, weight)


def spread_kernel(cot_hbm, out_hbm, cot, in_sem, out_sem):
    begin(cot_hbm, cot, in_sem.at[0]).wait()
    copies = [begin(cot, out_hbm.at[r], out_sem.at[r]) for r in range(16)]
    for copy in copies:
        copy.wait()


def spread(cot):
    return call(
        spread_kernel,
        cot.size,
        4 * MIB,
        in_specs=[ANY],
        out_specs=ANY,
        out_shape=jax.ShapeDtypeStruct((16,) + cot.shape, bf16),
        scratch_shapes=[
            pltpu.VMEM(cot.shape, bf16),
            pltpu.SemaphoreType.DMA((1,)),
            pltpu.SemaphoreType.DMA((16,)),
        ],
        name="spread",
    )(cot)


def project_kernel(
    place_ref, own_hbm, other_hbm, down_hbm, sums_hbm, small_hbm, tokens_hbm,
    tokens, down, small, first_sem, sem,
):
    z, core = place_ref[0], place_ref[1]
    copies = [
        begin(down_hbm, down, first_sem.at[0]),
        begin(sums_hbm, small.at[64:], first_sem.at[1]),
    ]
    for k in range(8):
        back = lax.rem(z + 8 - k, 8)
        rows = slice(32 * k, 32 * k + 32)
        copies.append(begin(own_hbm.at[rows], tokens.at[back, core], sem.at[0, k]))
        copies.append(begin(other_hbm.at[rows], tokens.at[back, 1 - core], sem.at[1, k]))
    for copy in copies:
        copy.wait()
    stores = [begin(tokens, tokens_hbm, first_sem.at[0])]
    proj = three(down[...], tokens[...].reshape(512, down.shape[1]), 1, 1)
    for k in range(4):
        small[RANK * k : RANK * k + RANK, :] = proj[:, LANES * k : LANES * k + LANES]
    stores.append(begin(small, small_hbm, first_sem.at[1]))
    for copy in stores:
        copy.wait()


def project(place, own, other, down_t, sums):
    depth = down_t.shape[1]
    return call(
        project_kernel,
        2 * 512 * 256 * depth,
        3 * MIB,
        in_specs=[SMEM] + [ANY] * 4,
        out_specs=[ANY] * 2,
        out_shape=[
            jax.ShapeDtypeStruct((96, LANES), f32),
            jax.ShapeDtypeStruct((8, 2, 32, depth), bf16),
        ],
        scratch_shapes=[
            pltpu.VMEM((8, 2, 32, depth), bf16),
            pltpu.VMEM((RANK, depth), f32),
            pltpu.VMEM((96, LANES), f32),
            pltpu.SemaphoreType.DMA((2,)),
            pltpu.SemaphoreType.DMA((2, 8)),
        ],
        name="project",
    )(place, own, other, down_t, sums)


def forward_kernel(tokens_hbm, merged_hbm, part_hbm, tokens, merged, part, first_sem, sem, out_sem):
    depth, width = merged.shape
    chunks = chunks_of(width)
    first = begin(tokens_hbm, tokens, first_sem.at[0])
    ready = stream([(merged_hbm, merged)], sem, chunks)
    first.wait()
    stores = []
    for j, (at, size) in enumerate(chunks):
        ready(j)
        cols = slice(at, at + size)
        product = dot(tokens[...], merged[:, cols], 1, 0).astype(bf16)
        part[:, :, cols] = product.reshape(16, 32, size)
        stores.append(begin(part.at[:, :, cols], part_hbm.at[:, :, cols], out_sem.at[j]))
    for copy in stores:
        copy.wait()


def forward(tokens, merged_low):
    depth, width = merged_low.shape
    count = len(chunks_of(width))
    return call(
        forward_kernel,
        2 * 512 * depth * width,
        12 * MIB,
        in_specs=[ANY] * 2,
        out_specs=ANY,
        out_shape=jax.ShapeDtypeStruct((16, 32, width + LANES), bf16),
        scratch_shapes=[
            pltpu.VMEM((512, depth), bf16),
            pltpu.VMEM((depth, width), bf16),
            pltpu.VMEM((16, 32, width), bf16),
            pltpu.SemaphoreType.DMA((1,)),
            pltpu.SemaphoreType.DMA((1, count)),
            pltpu.SemaphoreType.DMA((count,)),
        ],
        name="forward",
    )(tokens, merged_low)


def magnitude_kernel(given_hbm, part_hbm, out_hbm, cot, part, extra, sem, out_sem):
    width = cot.shape[2]
    chunks = chunks_of(width)
    ready = stream([(given_hbm, cot), (part_hbm, part)], sem, chunks, len(chunks))
    rows = []
    for j, (at, size) in enumerate(chunks):
        ready(j)
        cols = slice(at, at + size)
        product = cot[:, :, cols].astype(f32) * part[:, :, cols].astype(f32)
        total = jnp.sum(product.reshape(64, 8, size), axis=0)
        rows += in_rows(jnp.sum(total, axis=0, keepdims=True))
    rows.append(jnp.zeros((32 - len(rows), LANES), f32))
    sums = jnp.concatenate(rows, axis=0).astype(bf16)
    extra[...] = jnp.broadcast_to(sums[None], extra.shape)
    begin(extra, out_hbm.at[:, :, width:], out_sem.at[0]).wait()


def add_magnitude(given, part):
    blocks, rows, width = given.shape
    return call(
        magnitude_kernel,
        4 * 512 * width,
        7 * MIB,
        in_specs=[ANY, ANY],
        out_specs=ANY,
        out_shape=jax.ShapeDtypeStruct(part.shape, bf16),
        scratch_shapes=[
            pltpu.VMEM((blocks, rows, width), bf16),
            pltpu.VMEM((blocks, rows, width), bf16),
            pltpu.VMEM((blocks, rows, LANES), bf16),
            pltpu.SemaphoreType.DMA((2, len(chunks_of(width)))),
            pltpu.SemaphoreType.DMA((1,)),
        ],
        input_output_aliases={1: 0},
        name="magnitude",
    )(given, part)


def pack(low, out):
    high = low.astype(bf16)
    rest = (low - high.astype(f32)).astype(bf16)
    out[:, :CHUNK] = high
    out[:, CHUNK:] = rest
    return high.astype(f32) + rest.astype(f32)


def unpack(got):
    got = got.astype(f32)
    return got[:, :CHUNK] + got[:, CHUNK:]


def backward_kernel(
    core_ref, small_hbm, magnitude_hbm, up_hbm, given_hbm, merged_hbm, own_hbm, send_hbm, scale_hbm,
    squares, magnitude, up, cot, merged, total, own, send, scale, first_sem, sem,
):
    core = core_ref[0]
    depth, width = merged.shape
    chunks = chunks_of(width)
    count = width // LANES
    first = (
        begin(small_hbm.at[64:], squares, first_sem.at[0]),
        begin(up_hbm, up, first_sem.at[1]),
        begin(magnitude_hbm, magnitude, first_sem.at[2]),
    )
    ready = stream([(given_hbm, cot), (merged_hbm, merged)], sem, chunks)
    for copy in first:
        copy.wait()
    norm = jnp.sqrt(squares[...] + epsilon)
    factors = magnitude[...] / norm[:count]
    scale[...] = jnp.zeros_like(scale)
    scale[:count, :] = factors
    scale[32:, :] = norm
    last = begin(scale, scale_hbm, first_sem.at[0])
    low = jnp.zeros((RANK, CHUNK), f32)
    for j, (at, size) in enumerate(chunks):
        ready(j)
        cols = slice(at, at + size)
        value = cot[:, :, cols].reshape(512, size).astype(f32)
        grad = (value * in_line(factors, at, size)).astype(bf16)
        product = dot(grad, merged[:, cols], 1, 1)
        if j == 0:
            total[...] = product
        else:
            total[...] += product
        low += three(up[:, cols], grad, 1, 1)
    for z in range(8):
        theirs = pl.ds(pl.multiple_of((2 * z + 1 - core) * 32, 32), 32)
        send[32 * z : 32 * z + 32, :] = total[theirs, :].astype(bf16)
    pack(low, send.at[256:272, :])
    first = begin(send, send_hbm, first_sem.at[1])
    for z in range(8):
        mine = pl.ds(pl.multiple_of((2 * z + core) * 32, 32), 32)
        own[32 * z : 32 * z + 32, :] = total[mine, :].astype(bf16)
    own[256:272, :] = send[256:272, :]
    begin(own, own_hbm, first_sem.at[2]).wait()
    first.wait()
    last.wait()


def backward(core, small, magnitude, up, given, merged_low):
    depth, width = merged_low.shape
    count = len(chunks_of(width))
    return call(
        backward_kernel,
        2 * 512 * depth * width,
        12 * MIB,
        in_specs=[SMEM] + [ANY] * 5,
        out_specs=[ANY] * 3,
        out_shape=[jax.ShapeDtypeStruct((272, depth), bf16)] * 2
        + [jax.ShapeDtypeStruct((64, LANES), f32)],
        scratch_shapes=[
            pltpu.VMEM((32, LANES), f32),
            pltpu.VMEM(magnitude.shape, f32),
            pltpu.VMEM((RANK, width), f32),
            pltpu.VMEM((16, 32, width), bf16),
            pltpu.VMEM((depth, width), bf16),
            pltpu.VMEM((512, depth), f32),
            pltpu.VMEM((272, depth), bf16),
            pltpu.VMEM((272, depth), bf16),
            pltpu.VMEM((64, LANES), f32),
            pltpu.SemaphoreType.DMA((3,)),
            pltpu.SemaphoreType.DMA((2, count)),
        ],
        name="backward",
    )(core, small, magnitude, up, given, merged_low)


def pair_kernel(z_ref, own_hbm, got_hbm, keep_hbm, send_hbm, own, got, keep, send, sem, out_sem):
    bit = lax.rem(z_ref[0], 2)
    copies = begin(own_hbm, own, sem.at[0]), begin(got_hbm, got, sem.at[1])
    for copy in copies:
        copy.wait()
    low = unpack(own[256:272, :]) + unpack(got[256:272, :])
    pack(low, send.at[128:144, :])
    keep[128:144, :] = send[128:144, :]
    stores = []
    for target, other, out in ((send, 1 - bit, send_hbm), (keep, bit, keep_hbm)):
        for i in range(4):
            block = pl.ds(pl.multiple_of((2 * i + other) * 32, 32), 32)
            value = own[block, :].astype(f32) + got[block, :].astype(f32)
            target[32 * i : 32 * i + 32, :] = value.astype(bf16)
        stores.append(begin(target, out, out_sem.at[len(stores)]))
    for copy in stores:
        copy.wait()


def pair(z, own, got):
    rows, depth = own.shape
    return call(
        pair_kernel,
        4 * rows * depth,
        6 * rows * depth,
        in_specs=[SMEM, ANY, ANY],
        out_specs=[ANY] * 2,
        out_shape=[jax.ShapeDtypeStruct((144, depth), bf16)] * 2,
        scratch_shapes=[pltpu.VMEM((rows, depth), bf16)] * 2
        + [pltpu.VMEM((144, depth), bf16)] * 2
        + [pltpu.SemaphoreType.DMA((2,))] * 2,
        name="pair",
    )(z, own, got)


def quad_kernel(z_ref, keep_hbm, got_hbm, *refs):
    out_hbm = refs[:4]
    keep, got, send, sem, out_sem = refs[4:]
    half = z_ref[0] // 2
    copies = begin(keep_hbm, keep, sem.at[0]), begin(got_hbm, got, sem.at[1])
    for copy in copies:
        copy.wait()
    low = unpack(keep[128:144, :]) + unpack(got[128:144, :])
    pack(low, send.at[0, 32:48, :])
    stores = []
    for k in [2, 1, 3, 0]:
        block = pl.ds(pl.multiple_of(lax.rem(half + k, 4) * 32, 32), 32)
        send[k, :32, :] = (keep[block, :].astype(f32) + got[block, :].astype(f32)).astype(bf16)
        if k:
            send[k, 32:48, :] = send[0, 32:48, :]
        stores.append(begin(send.at[k], out_hbm[k], out_sem.at[k]))
    for copy in stores:
        copy.wait()


def quad(z, keep, got):
    rows, depth = keep.shape
    return call(
        quad_kernel,
        4 * rows * depth,
        6 * rows * depth,
        in_specs=[SMEM, ANY, ANY],
        out_specs=[ANY] * 4,
        out_shape=[jax.ShapeDtypeStruct((48, depth), bf16)] * 4,
        scratch_shapes=[pltpu.VMEM((rows, depth), bf16)] * 2
        + [pltpu.VMEM((4, 48, depth), bf16)]
        + [pltpu.SemaphoreType.DMA((2,)), pltpu.SemaphoreType.DMA((4,))],
        name="quad",
    )(z, keep, got)


def finish_kernel(z_ref, tokens_hbm, *refs):
    parts_hbm = refs[:4]
    grad_hbm, down_hbm, parts, tokens, lows, grad, down, sem, out_sem = refs[4:]
    half = z_ref[0] // 2
    copies = [begin(parts_hbm[k], parts.at[k], sem.at[k]) for k in range(4)]
    later = begin(tokens_hbm, tokens, sem.at[4])
    for copy in copies:
        copy.wait()
    total = parts[0, :32, :].astype(f32)
    for k in range(1, 4):
        total += parts[k, :32, :].astype(f32)
    grad[...] = total.astype(bf16)
    first = begin(grad, grad_hbm, out_sem.at[0])
    for k in range(4):
        lows[lax.rem(half + 4 - k, 4)] = unpack(parts[k, 32:48, :])
    low = (lows[0] + lows[1]) + (lows[2] + lows[3])
    later.wait()
    down[...] = three(low * adapter_scale, tokens[...], 1, 0)
    begin(down, down_hbm, out_sem.at[1]).wait()
    first.wait()


def finish(z, tokens, parts):
    depth = tokens.shape[1]
    return call(
        finish_kernel,
        2 * 512 * 256 * depth,
        2 * MIB,
        in_specs=[SMEM] + [ANY] * 5,
        out_specs=[ANY, ANY],
        out_shape=[
            jax.ShapeDtypeStruct((32, depth), bf16),
            jax.ShapeDtypeStruct((RANK, depth), f32),
        ],
        scratch_shapes=[
            pltpu.VMEM((4, 48, depth), bf16),
            pltpu.VMEM(tokens.shape, bf16),
            pltpu.VMEM((4, RANK, CHUNK), f32),
            pltpu.VMEM((32, depth), bf16),
            pltpu.VMEM((RANK, depth), f32),
            pltpu.SemaphoreType.DMA((5,)),
            pltpu.SemaphoreType.DMA((2,)),
        ],
        name="finish",
    )(z, tokens, *parts)


def up_kernel(
    small_hbm, scale_hbm, given_hbm, out_hbm, small, scale, cot, out, first_sem, sem, out_sem
):
    width = cot.shape[2]
    chunks = chunks_of(width)
    first = begin(small_hbm, small, first_sem.at[0]), begin(scale_hbm, scale, first_sem.at[1])
    ready = stream([(given_hbm, cot)], sem, chunks, 3)
    for copy in first:
        copy.wait()
    proj = [small[RANK * k : RANK * k + RANK, :] for k in range(4)]
    proj = jnp.concatenate(proj, axis=1) * adapter_scale
    factors = scale[:32, :]
    stores = []
    for j, (at, size) in enumerate(chunks):
        ready(j)
        cols = slice(at, at + size)
        value = cot[:, :, cols].reshape(512, size).astype(f32)
        grad = (value * in_line(factors, at, size)).astype(bf16)
        out[:, cols] = three(proj, grad, 1, 0)
        stores.append(begin(out.at[:, cols], out_hbm.at[:, cols], out_sem.at[j]))
    for copy in stores:
        copy.wait()


def up_gradient_of(small, scale, given):
    width = given.shape[2]
    count = len(chunks_of(width))
    return call(
        up_kernel,
        2 * 512 * 256 * width,
        4 * MIB,
        in_specs=[ANY] * 3,
        out_specs=ANY,
        out_shape=jax.ShapeDtypeStruct((RANK, width), f32),
        scratch_shapes=[
            pltpu.VMEM(small.shape, f32),
            pltpu.VMEM(scale.shape, f32),
            pltpu.VMEM(given.shape, bf16),
            pltpu.VMEM((RANK, width), f32),
            pltpu.SemaphoreType.DMA((2,)),
            pltpu.SemaphoreType.DMA((1, count)),
            pltpu.SemaphoreType.DMA((count,)),
        ],
        name="up_gradient",
    )(small, scale, given)


def output_kernel(
    scale_hbm, parts_hbm, out_hbm, mag_hbm, scale, parts, out, mag, first_sem, sem, out_sem
):
    width = out.shape[1]
    chunks = chunks_of(width)
    count = width // LANES
    first = (
        begin(scale_hbm, scale, first_sem.at[0]),
        begin(parts_hbm.at[:, :, width:], parts.at[:, :, width:], first_sem.at[1]),
    )
    ready = stream([(parts_hbm, parts.at[:, :, :width])], sem, chunks, 4)
    for copy in first:
        copy.wait()

    def added(cols):
        total = parts[0, :, cols].astype(f32)
        for r in range(1, 16):
            total += parts[r, :, cols].astype(f32)
        return total

    mag[...] = added(slice(width, width + LANES))[:count] / scale[32 : 32 + count, :]
    stores = [begin(mag, mag_hbm, first_sem.at[0])]
    factors = scale[:32, :]
    for j, (at, size) in enumerate(chunks):
        ready(j)
        cols = slice(at, at + size)
        out[:, cols] = (added(cols) * in_line(factors, at, size)).astype(bf16)
        stores.append(begin(out.at[:, cols], out_hbm.at[:, cols], out_sem.at[j]))
    for copy in stores:
        copy.wait()


def output_of(scale, parts):
    width = parts.shape[2] - LANES
    count = len(chunks_of(width))
    return call(
        output_kernel,
        16 * 32 * width,
        4 * MIB,
        in_specs=[ANY] * 2,
        out_specs=[ANY] * 2,
        out_shape=[
            jax.ShapeDtypeStruct((32, width), bf16),
            jax.ShapeDtypeStruct((width // LANES, LANES), f32),
        ],
        scratch_shapes=[
            pltpu.VMEM(scale.shape, f32),
            pltpu.VMEM(parts.shape, bf16),
            pltpu.VMEM((32, width), bf16),
            pltpu.VMEM((width // LANES, LANES), f32),
            pltpu.SemaphoreType.DMA((2,)),
            pltpu.SemaphoreType.DMA((1, count)),
            pltpu.SemaphoreType.DMA((count,)),
        ],
        name="output",
    )(scale, parts)


def exchange(blocks):
    return lax.all_to_all(blocks, ROW, 0, 0, tiled=False)


def further(value, axis, k, size):
    return lax.ppermute(value, axis, [(i, (i + k) % size) for i in range(size)])


def shifted(value, axis):
    return [further(value, axis, k, 4) for k in (1, 2, 3)]


def added(value, arrived):
    one, two, other = arrived
    return (value + two) + (one + other)


def on_device(tokens, weight, down_adapter, up_adapter, magnitude, out_cotangent):
    z, core = [lax.axis_index(name).astype(jnp.int32).reshape(1) for name in COL]
    swap = [(0, 1), (1, 0)]
    down_t = down_adapter.T
    magnitude = magnitude.reshape(-1, LANES)
    message = spread(out_cotangent)
    given = exchange(message)
    blocks = [tokens] * 8
    for k in (4, 3, 5, 2):
        blocks[k] = further(tokens, "z", k, 8)
    merged_low, sums = merge(message, down_t, up_adapter, weight)
    later, sums, merged_low = lax.optimization_barrier((tokens, sums, merged_low))
    for k in (6, 1, 7):
        blocks[k] = further(later, "z", k, 8)
    own = jnp.concatenate(blocks, axis=0)
    other = lax.ppermute(own, "c", swap)
    place = jnp.concatenate([z, core])
    small, tokens_full = project(place, own, other, down_t, sums)
    tokens_full = tokens_full.reshape(512, -1)
    part = forward(tokens_full, merged_low)
    arrived = shifted(small, "x")
    arrived, part = lax.optimization_barrier((arrived, part))
    small = added(small, arrived)
    part = add_magnitude(given, part)
    arrived = shifted(small, "y")
    arrived, part = lax.optimization_barrier((arrived, part))
    small = added(small, arrived)
    small, part = lax.optimization_barrier((small, part))
    parts = exchange(part)
    own, send, scale = backward(core, small, magnitude, up_adapter, given, merged_low)
    got = lax.ppermute(send, "c", swap)
    keep, send = pair(z, own, got)
    got = lax.ppermute(send, "z", [(i, i ^ 1) for i in range(8)])
    blocks = list(quad(z, keep, got))
    for k in range(1, 4):
        blocks[k] = further(blocks[k], "z", 2 * k, 8)
    up_gradient = up_gradient_of(small, scale, given)
    grad_tokens, down_gradient = finish(z, tokens_full, blocks)
    output, grad_magnitude = output_of(scale, parts)
    return (output, grad_tokens, grad_magnitude.reshape(-1), up_gradient, down_gradient.T)


def solution(mesh):
    split = Mesh(mesh.devices.reshape(4, 4, 8, 2), ROW + COL)
    return jax.shard_map(
        on_device,
        mesh=split,
        in_specs=(P(COL, ROW), P(ROW, COL), P(ROW, None), P(None, COL), P(COL), P(ROW, COL)),
        out_specs=(P(ROW, COL), P(COL, ROW), P(COL), P(None, COL), P(ROW, None)),
        check_vma=False,
    )
```

```python
import jax
import jax.numpy as jnp
from jax import lax
from jax.experimental import pallas as pl
from jax.experimental.pallas import tpu as pltpu
from jax.sharding import Mesh
from jax.sharding import PartitionSpec as P

adapter_scale = 2.0
epsilon = 1e-06
bf16 = jnp.bfloat16
f32 = jnp.float32
ROW = ("x", "y")
COL = ("z", "c")
CHUNK = 512
RANK = 16
LANES = 128
MIB = 1024 * 1024
LIMIT = 63 * MIB + 768 * 1024
ANY = pl.BlockSpec(memory_space=pl.ANY)
SMEM = pl.BlockSpec(memory_space=pltpu.SMEM)


def pieces(value):
    high = value.astype(bf16)
    rest = value - high.astype(f32)
    mid = rest.astype(bf16)
    low = (rest - mid.astype(f32)).astype(bf16)
    return high, mid, low


def dot(left, right, left_dim, right_dim):
    return lax.dot_general(
        left, right, (((left_dim,), (right_dim,)), ((), ())), preferred_element_type=f32
    )


def three(left, right, left_dim, right_dim):
    out = dot(jnp.concatenate(pieces(left), axis=0), right, left_dim, right_dim)
    return out[:RANK] + out[RANK : 2 * RANK] + out[2 * RANK :]


def chunks_of(width):
    return [(at, min(CHUNK, width - at)) for at in range(0, width, CHUNK)]


def call(body, flops, moved, **options):
    return pl.pallas_call(
        body,
        compiler_params=pltpu.CompilerParams(vmem_limit_bytes=LIMIT),
        cost_estimate=pl.CostEstimate(flops=flops, bytes_accessed=moved, transcendentals=0),
        **options,
    )


def begin(source, target, sem):
    copy = pltpu.make_async_copy(source, target, sem)
    copy.start()
    return copy


def stream(pairs, sem, chunks, depth=2):
    def copies(j):
        for i, (source, target) in enumerate(pairs):
            index = (slice(None),) * (len(target.shape) - 1) + (pl.ds(*chunks[j]),)
            yield pltpu.make_async_copy(source.at[index], target.at[index], sem.at[i, j])

    def start(j):
        if j < len(chunks):
            for copy in copies(j):
                copy.start()

    def ready(j):
        for copy in copies(j):
            copy.wait()
        start(j + depth)

    for j in range(depth):
        start(j)
    return ready


def in_rows(row):
    return [row[:, at : at + LANES] for at in range(0, row.shape[1], LANES)]


def in_line(rows, at, size):
    return jnp.concatenate(
        [rows[k : k + 1, :] for k in range(at // LANES, (at + size) // LANES)], axis=1
    )


def merge_kernel(
    after_hbm, down_hbm, up_hbm, weight_hbm, merged_hbm, sums_hbm,
    down, up, weight, merged, sums, up_cat, totals, small_sem, in_sem, out_sem,
):
    depth, width = weight.shape
    rows, tile = 256, 256
    steps = [slice(at, at + rows) for at in range(0, depth, rows)]
    first = begin(up_hbm, up, small_sem.at[0]), begin(down_hbm, down, small_sem.at[1])
    fetches = [begin(weight_hbm.at[p], weight.at[p], in_sem.at[j]) for j, p in enumerate(steps)]
    totals[...] = jnp.zeros_like(totals)
    for copy in first:
        copy.wait()
    for at in range(0, width, tile):
        cols = slice(at, at + tile)
        u1, u2, u3 = pieces(up[:, cols])
        up_cat[:, cols] = jnp.concatenate([u1, u2, u1, u3, u1, u2], axis=0)
    d1, d2, d3 = pieces(down[...] * adapter_scale)
    down_cat = jnp.concatenate([d1, d1, d2, d1, d3, d2], axis=0)
    stores = []
    for j, part in enumerate(steps):
        fetches[j].wait()
        for at in range(0, width, tile):
            cols = slice(at, at + tile)
            value = weight[part, cols].astype(f32) + dot(down_cat[:, part], up_cat[:, cols], 0, 0)
            merged[part, cols] = value.astype(bf16)
            totals[:, cols] += jnp.sum((value * value).reshape(rows // 8, 8, tile), axis=0)
        stores.append(begin(merged.at[part], merged_hbm.at[part], out_sem.at[j]))
    lines = in_rows(jnp.sum(totals[...], axis=0, keepdims=True))
    sums[...] = jnp.concatenate(lines + [jnp.zeros((32 - len(lines), LANES), f32)], axis=0)
    stores.append(begin(sums, sums_hbm, small_sem.at[0]))
    for copy in stores:
        copy.wait()


def merge(after, down_t, up, weight):
    depth, width = weight.shape
    return call(
        merge_kernel,
        12 * depth * width,
        4 * depth * width,
        in_specs=[ANY] * 4,
        out_specs=[ANY] * 2,
        out_shape=[
            jax.ShapeDtypeStruct((depth, width), bf16),
            jax.ShapeDtypeStruct((32, LANES), f32),
        ],
        scratch_shapes=[
            pltpu.VMEM((RANK, depth), f32),
            pltpu.VMEM((RANK, width), f32),
            pltpu.VMEM((depth, width), bf16),
            pltpu.VMEM((depth, width), bf16),
            pltpu.VMEM((32, LANES), f32),
            pltpu.VMEM((6 * RANK, width), bf16),
            pltpu.VMEM((8, width), f32),
            pltpu.SemaphoreType.DMA((2,)),
            pltpu.SemaphoreType.DMA((4,)),
            pltpu.SemaphoreType.DMA((4,)),
        ],
        name="merge",
    )(after, down_t, up, weight)


def spread_kernel(cot_hbm, out_hbm, cot, in_sem, out_sem):
    begin(cot_hbm, cot, in_sem.at[0]).wait()
    copies = [begin(cot, out_hbm.at[r], out_sem.at[r]) for r in range(16)]
    for copy in copies:
        copy.wait()


def spread(cot):
    return call(
        spread_kernel,
        cot.size,
        4 * MIB,
        in_specs=[ANY],
        out_specs=ANY,
        out_shape=jax.ShapeDtypeStruct((16,) + cot.shape, bf16),
        scratch_shapes=[
            pltpu.VMEM(cot.shape, bf16),
            pltpu.SemaphoreType.DMA((1,)),
            pltpu.SemaphoreType.DMA((16,)),
        ],
        name="spread",
    )(cot)


def project_kernel(
    place_ref, own_hbm, other_hbm, down_hbm, sums_hbm, small_hbm, tokens_hbm,
    tokens, down, small, first_sem, sem,
):
    z, core = place_ref[0], place_ref[1]
    copies = [
        begin(down_hbm, down, first_sem.at[0]),
        begin(sums_hbm, small.at[64:], first_sem.at[1]),
    ]
    for k in range(8):
        back = lax.rem(z + 8 - (k - k % 2), 8)
        if k % 2:
            back = back + 1 - 2 * lax.rem(back, 2)
        rows = slice(32 * k, 32 * k + 32)
        copies.append(begin(own_hbm.at[rows], tokens.at[back, core], sem.at[0, k]))
        copies.append(begin(other_hbm.at[rows], tokens.at[back, 1 - core], sem.at[1, k]))
    for copy in copies:
        copy.wait()
    stores = [begin(tokens, tokens_hbm, first_sem.at[0])]
    proj = three(down[...], tokens[...].reshape(512, down.shape[1]), 1, 1)
    for k in range(4):
        small[RANK * k : RANK * k + RANK, :] = proj[:, LANES * k : LANES * k + LANES]
    stores.append(begin(small, small_hbm, first_sem.at[1]))
    for copy in stores:
        copy.wait()


def project(place, own, other, down_t, sums):
    depth = down_t.shape[1]
    return call(
        project_kernel,
        2 * 512 * 256 * depth,
        3 * MIB,
        in_specs=[SMEM] + [ANY] * 4,
        out_specs=[ANY] * 2,
        out_shape=[
            jax.ShapeDtypeStruct((96, LANES), f32),
            jax.ShapeDtypeStruct((8, 2, 32, depth), bf16),
        ],
        scratch_shapes=[
            pltpu.VMEM((8, 2, 32, depth), bf16),
            pltpu.VMEM((RANK, depth), f32),
            pltpu.VMEM((96, LANES), f32),
            pltpu.SemaphoreType.DMA((2,)),
            pltpu.SemaphoreType.DMA((2, 8)),
        ],
        name="project",
    )(place, own, other, down_t, sums)


def forward_kernel(tokens_hbm, merged_hbm, part_hbm, tokens, merged, part, first_sem, sem, out_sem):
    depth, width = merged.shape
    chunks = chunks_of(width)
    first = begin(tokens_hbm, tokens, first_sem.at[0])
    ready = stream([(merged_hbm, merged)], sem, chunks)
    first.wait()
    stores = []
    for j, (at, size) in enumerate(chunks):
        ready(j)
        cols = slice(at, at + size)
        product = dot(tokens[...], merged[:, cols], 1, 0).astype(bf16)
        part[:, :, cols] = product.reshape(16, 32, size)
        stores.append(begin(part.at[:, :, cols], part_hbm.at[:, :, cols], out_sem.at[j]))
    for copy in stores:
        copy.wait()


def forward(tokens, merged_low):
    depth, width = merged_low.shape
    count = len(chunks_of(width))
    return call(
        forward_kernel,
        2 * 512 * depth * width,
        12 * MIB,
        in_specs=[ANY] * 2,
        out_specs=ANY,
        out_shape=jax.ShapeDtypeStruct((16, 32, width + LANES), bf16),
        scratch_shapes=[
            pltpu.VMEM((512, depth), bf16),
            pltpu.VMEM((depth, width), bf16),
            pltpu.VMEM((16, 32, width), bf16),
            pltpu.SemaphoreType.DMA((1,)),
            pltpu.SemaphoreType.DMA((1, count)),
            pltpu.SemaphoreType.DMA((count,)),
        ],
        name="forward",
    )(tokens, merged_low)


def magnitude_kernel(given_hbm, part_hbm, out_hbm, cot, part, extra, sem, out_sem):
    width = cot.shape[2]
    chunks = chunks_of(width)
    ready = stream([(given_hbm, cot), (part_hbm, part)], sem, chunks, len(chunks))
    rows = []
    for j, (at, size) in enumerate(chunks):
        ready(j)
        cols = slice(at, at + size)
        product = cot[:, :, cols].astype(f32) * part[:, :, cols].astype(f32)
        total = jnp.sum(product.reshape(64, 8, size), axis=0)
        rows += in_rows(jnp.sum(total, axis=0, keepdims=True))
    rows.append(jnp.zeros((32 - len(rows), LANES), f32))
    sums = jnp.concatenate(rows, axis=0).astype(bf16)
    extra[...] = jnp.broadcast_to(sums[None], extra.shape)
    begin(extra, out_hbm.at[:, :, width:], out_sem.at[0]).wait()


def add_magnitude(given, part):
    blocks, rows, width = given.shape
    return call(
        magnitude_kernel,
        4 * 512 * width,
        7 * MIB,
        in_specs=[ANY, ANY],
        out_specs=ANY,
        out_shape=jax.ShapeDtypeStruct(part.shape, bf16),
        scratch_shapes=[
            pltpu.VMEM((blocks, rows, width), bf16),
            pltpu.VMEM((blocks, rows, width), bf16),
            pltpu.VMEM((blocks, rows, LANES), bf16),
            pltpu.SemaphoreType.DMA((2, len(chunks_of(width)))),
            pltpu.SemaphoreType.DMA((1,)),
        ],
        input_output_aliases={1: 0},
        name="magnitude",
    )(given, part)


def pack(low, out):
    high = low.astype(bf16)
    rest = (low - high.astype(f32)).astype(bf16)
    out[:, :CHUNK] = high
    out[:, CHUNK:] = rest
    return high.astype(f32) + rest.astype(f32)


def unpack(got):
    got = got.astype(f32)
    return got[:, :CHUNK] + got[:, CHUNK:]


def backward_kernel(
    core_ref, small_hbm, magnitude_hbm, up_hbm, given_hbm, merged_hbm, own_hbm, send_hbm, scale_hbm,
    squares, magnitude, up, cot, merged, total, own, send, scale, first_sem, sem,
):
    core = core_ref[0]
    depth, width = merged.shape
    chunks = chunks_of(width)
    count = width // LANES
    first = (
        begin(small_hbm.at[64:], squares, first_sem.at[0]),
        begin(up_hbm, up, first_sem.at[1]),
        begin(magnitude_hbm, magnitude, first_sem.at[2]),
    )
    ready = stream([(given_hbm, cot), (merged_hbm, merged)], sem, chunks)
    for copy in first:
        copy.wait()
    norm = jnp.sqrt(squares[...] + epsilon)
    factors = magnitude[...] / norm[:count]
    scale[...] = jnp.zeros_like(scale)
    scale[:count, :] = factors
    scale[32:, :] = norm
    last = begin(scale, scale_hbm, first_sem.at[0])
    low = jnp.zeros((RANK, CHUNK), f32)
    for j, (at, size) in enumerate(chunks):
        ready(j)
        cols = slice(at, at + size)
        value = cot[:, :, cols].reshape(512, size).astype(f32)
        grad = (value * in_line(factors, at, size)).astype(bf16)
        product = dot(grad, merged[:, cols], 1, 1)
        if j == 0:
            total[...] = product
        else:
            total[...] += product
        low += three(up[:, cols], grad, 1, 1)
    for z in range(8):
        theirs = pl.ds(pl.multiple_of((2 * z + 1 - core) * 32, 32), 32)
        send[32 * z : 32 * z + 32, :] = total[theirs, :].astype(bf16)
    pack(low, send.at[256:272, :])
    first = begin(send, send_hbm, first_sem.at[1])
    for z in range(8):
        mine = pl.ds(pl.multiple_of((2 * z + core) * 32, 32), 32)
        own[32 * z : 32 * z + 32, :] = total[mine, :].astype(bf16)
    own[256:272, :] = send[256:272, :]
    begin(own, own_hbm, first_sem.at[2]).wait()
    first.wait()
    last.wait()


def backward(core, small, magnitude, up, given, merged_low):
    depth, width = merged_low.shape
    count = len(chunks_of(width))
    return call(
        backward_kernel,
        2 * 512 * depth * width,
        12 * MIB,
        in_specs=[SMEM] + [ANY] * 5,
        out_specs=[ANY] * 3,
        out_shape=[jax.ShapeDtypeStruct((272, depth), bf16)] * 2
        + [jax.ShapeDtypeStruct((64, LANES), f32)],
        scratch_shapes=[
            pltpu.VMEM((32, LANES), f32),
            pltpu.VMEM(magnitude.shape, f32),
            pltpu.VMEM((RANK, width), f32),
            pltpu.VMEM((16, 32, width), bf16),
            pltpu.VMEM((depth, width), bf16),
            pltpu.VMEM((512, depth), f32),
            pltpu.VMEM((272, depth), bf16),
            pltpu.VMEM((272, depth), bf16),
            pltpu.VMEM((64, LANES), f32),
            pltpu.SemaphoreType.DMA((3,)),
            pltpu.SemaphoreType.DMA((2, count)),
        ],
        name="backward",
    )(core, small, magnitude, up, given, merged_low)


def pair_kernel(z_ref, own_hbm, got_hbm, keep_hbm, send_hbm, own, got, keep, send, sem, out_sem):
    bit = lax.rem(z_ref[0], 2)
    copies = begin(own_hbm, own, sem.at[0]), begin(got_hbm, got, sem.at[1])
    for copy in copies:
        copy.wait()
    low = unpack(own[256:272, :]) + unpack(got[256:272, :])
    pack(low, send.at[128:144, :])
    keep[128:144, :] = send[128:144, :]
    stores = []
    for target, other, out in ((send, 1 - bit, send_hbm), (keep, bit, keep_hbm)):
        for i in range(4):
            block = pl.ds(pl.multiple_of((2 * i + other) * 32, 32), 32)
            value = own[block, :].astype(f32) + got[block, :].astype(f32)
            target[32 * i : 32 * i + 32, :] = value.astype(bf16)
        stores.append(begin(target, out, out_sem.at[len(stores)]))
    for copy in stores:
        copy.wait()


def pair(z, own, got):
    rows, depth = own.shape
    return call(
        pair_kernel,
        4 * rows * depth,
        6 * rows * depth,
        in_specs=[SMEM, ANY, ANY],
        out_specs=[ANY] * 2,
        out_shape=[jax.ShapeDtypeStruct((144, depth), bf16)] * 2,
        scratch_shapes=[pltpu.VMEM((rows, depth), bf16)] * 2
        + [pltpu.VMEM((144, depth), bf16)] * 2
        + [pltpu.SemaphoreType.DMA((2,))] * 2,
        name="pair",
    )(z, own, got)


def quad_kernel(z_ref, after_hbm, keep_hbm, got_hbm, *refs):
    out_hbm = refs[:4]
    keep, got, send, sem, out_sem = refs[4:]
    half = z_ref[0] // 2
    copies = begin(keep_hbm, keep, sem.at[0]), begin(got_hbm, got, sem.at[1])
    for copy in copies:
        copy.wait()
    low = unpack(keep[128:144, :]) + unpack(got[128:144, :])
    pack(low, send.at[0, 32:48, :])
    stores = []
    for k in [2, 1, 3, 0]:
        block = pl.ds(pl.multiple_of(lax.rem(half + k, 4) * 32, 32), 32)
        send[k, :32, :] = (keep[block, :].astype(f32) + got[block, :].astype(f32)).astype(bf16)
        if k:
            send[k, 32:48, :] = send[0, 32:48, :]
        stores.append(begin(send.at[k], out_hbm[k], out_sem.at[k]))
    for copy in stores:
        copy.wait()


def quad(z, after, keep, got):
    rows, depth = keep.shape
    return call(
        quad_kernel,
        4 * rows * depth,
        6 * rows * depth,
        in_specs=[SMEM, ANY, ANY, ANY],
        out_specs=[ANY] * 4,
        out_shape=[jax.ShapeDtypeStruct((48, depth), bf16)] * 4,
        scratch_shapes=[pltpu.VMEM((rows, depth), bf16)] * 2
        + [pltpu.VMEM((4, 48, depth), bf16)]
        + [pltpu.SemaphoreType.DMA((2,)), pltpu.SemaphoreType.DMA((4,))],
        name="quad",
    )(z, after, keep, got)


def up_kernel(
    small_hbm, scale_hbm, given_hbm, out_hbm, small, scale, cot, out, first_sem, sem, out_sem
):
    width = cot.shape[2]
    chunks = chunks_of(width)
    first = begin(small_hbm, small, first_sem.at[0]), begin(scale_hbm, scale, first_sem.at[1])
    ready = stream([(given_hbm, cot)], sem, chunks, 3)
    for copy in first:
        copy.wait()
    proj = [small[RANK * k : RANK * k + RANK, :] for k in range(4)]
    proj = jnp.concatenate(proj, axis=1) * adapter_scale
    factors = scale[:32, :]
    stores = []
    for j, (at, size) in enumerate(chunks):
        ready(j)
        cols = slice(at, at + size)
        value = cot[:, :, cols].reshape(512, size).astype(f32)
        grad = (value * in_line(factors, at, size)).astype(bf16)
        out[:, cols] = three(proj, grad, 1, 0)
        stores.append(begin(out.at[:, cols], out_hbm.at[:, cols], out_sem.at[j]))
    for copy in stores:
        copy.wait()


def up_gradient_of(small, scale, given):
    width = given.shape[2]
    count = len(chunks_of(width))
    return call(
        up_kernel,
        2 * 512 * 256 * width,
        4 * MIB,
        in_specs=[ANY] * 3,
        out_specs=ANY,
        out_shape=jax.ShapeDtypeStruct((RANK, width), f32),
        scratch_shapes=[
            pltpu.VMEM(small.shape, f32),
            pltpu.VMEM(scale.shape, f32),
            pltpu.VMEM(given.shape, bf16),
            pltpu.VMEM((RANK, width), f32),
            pltpu.SemaphoreType.DMA((2,)),
            pltpu.SemaphoreType.DMA((1, count)),
            pltpu.SemaphoreType.DMA((count,)),
        ],
        name="up_gradient",
    )(small, scale, given)


def finish_kernel(z_ref, tokens_hbm, scale_hbm, parts_hbm, *refs):
    blocks_hbm, (grad_hbm, down_hbm, out_hbm, mag_hbm) = refs[:4], refs[4:8]
    blocks, tokens, lows, grad, down, scale, parts, out, mag = refs[8:17]
    block_sem, first_sem, sem, out_sem = refs[17:]
    half = z_ref[0] // 2
    width = out.shape[1]
    chunks = chunks_of(width)
    count = width // LANES
    copies = [begin(blocks_hbm[k], blocks.at[k], block_sem.at[k]) for k in range(4)]
    later = (
        begin(tokens_hbm, tokens, first_sem.at[0]),
        begin(scale_hbm, scale, first_sem.at[1]),
        begin(parts_hbm.at[:, :, width:], parts.at[:, :, width:], first_sem.at[2]),
    )
    ready = stream([(parts_hbm, parts.at[:, :, :width])], sem, chunks, len(chunks))
    for copy in copies:
        copy.wait()
    total = blocks[0, :32, :].astype(f32)
    for k in range(1, 4):
        total += blocks[k, :32, :].astype(f32)
    grad[...] = total.astype(bf16)
    stores = [begin(grad, grad_hbm, block_sem.at[0])]
    for k in range(4):
        lows[lax.rem(half + 4 - k, 4)] = unpack(blocks[k, 32:48, :])
    low = (lows[0] + lows[1]) + (lows[2] + lows[3])
    for copy in later:
        copy.wait()
    down[...] = three(low * adapter_scale, tokens[...], 1, 0)
    stores.append(begin(down, down_hbm, block_sem.at[1]))

    def summed(cols):
        total = parts[0, :, cols].astype(f32)
        for r in range(1, 16):
            total += parts[r, :, cols].astype(f32)
        return total

    mag[...] = summed(slice(width, width + LANES))[:count] / scale[32 : 32 + count, :]
    stores.append(begin(mag, mag_hbm, block_sem.at[2]))
    factors = scale[:32, :]
    for j, (at, size) in enumerate(chunks):
        ready(j)
        cols = slice(at, at + size)
        out[:, cols] = (summed(cols) * in_line(factors, at, size)).astype(bf16)
        stores.append(begin(out.at[:, cols], out_hbm.at[:, cols], out_sem.at[j]))
    for copy in stores:
        copy.wait()


def finish(z, tokens, scale, parts, blocks):
    depth = tokens.shape[1]
    width = parts.shape[2] - LANES
    count = len(chunks_of(width))
    return call(
        finish_kernel,
        2 * 512 * 256 * depth,
        6 * MIB,
        in_specs=[SMEM] + [ANY] * 7,
        out_specs=[ANY] * 4,
        out_shape=[
            jax.ShapeDtypeStruct((32, depth), bf16),
            jax.ShapeDtypeStruct((RANK, depth), f32),
            jax.ShapeDtypeStruct((32, width), bf16),
            jax.ShapeDtypeStruct((width // LANES, LANES), f32),
        ],
        scratch_shapes=[
            pltpu.VMEM((4, 48, depth), bf16),
            pltpu.VMEM(tokens.shape, bf16),
            pltpu.VMEM((4, RANK, CHUNK), f32),
            pltpu.VMEM((32, depth), bf16),
            pltpu.VMEM((RANK, depth), f32),
            pltpu.VMEM(scale.shape, f32),
            pltpu.VMEM(parts.shape, bf16),
            pltpu.VMEM((32, width), bf16),
            pltpu.VMEM((width // LANES, LANES), f32),
            pltpu.SemaphoreType.DMA((4,)),
            pltpu.SemaphoreType.DMA((3,)),
            pltpu.SemaphoreType.DMA((1, count)),
            pltpu.SemaphoreType.DMA((count,)),
        ],
        name="finish",
    )(z, tokens, scale, parts, *blocks)


def exchange(blocks):
    return lax.all_to_all(blocks, ROW, 0, 0, tiled=False)


def further(value, axis, k, size):
    return lax.ppermute(value, axis, [(i, (i + k) % size) for i in range(size)])


def shifted(value, axis):
    return [further(value, axis, k, 4) for k in (1, 2, 3)]


def added(value, arrived):
    one, two, other = arrived
    return (value + two) + (one + other)


def on_device(tokens, weight, down_adapter, up_adapter, magnitude, out_cotangent):
    z, core = [lax.axis_index(name).astype(jnp.int32).reshape(1) for name in COL]
    swap = [(0, 1), (1, 0)]
    down_t = down_adapter.T
    magnitude = magnitude.reshape(-1, LANES)
    given = exchange(spread(out_cotangent))
    beside = [(i, i ^ 1) for i in range(8)]
    two = jnp.concatenate([tokens, lax.ppermute(tokens, "z", beside)], axis=0)
    own = [two] + [further(two, "z", 2 * k, 8) for k in (1, 2, 3)]
    merged_low, sums = merge(two, down_t, up_adapter, weight)
    own = jnp.concatenate(own, axis=0)
    other = lax.ppermute(own, "c", swap)
    place = jnp.concatenate([z, core])
    small, tokens_full = project(place, own, other, down_t, sums)
    tokens_full = tokens_full.reshape(512, -1)
    part = forward(tokens_full, merged_low)
    arrived = shifted(small, "x")
    arrived, part = lax.optimization_barrier((arrived, part))
    small = added(small, arrived)
    part = add_magnitude(given, part)
    arrived = shifted(small, "y")
    arrived, part = lax.optimization_barrier((arrived, part))
    parts = exchange(part)
    small = added(small, arrived)
    own, send, scale = backward(core, small, magnitude, up_adapter, given, merged_low)
    got = lax.ppermute(send, "c", swap)
    keep, send = pair(z, own, got)
    got = lax.ppermute(send, "z", beside)
    up_gradient = up_gradient_of(small, scale, given)
    blocks = list(quad(z, up_gradient, keep, got))
    for k in range(1, 4):
        blocks[k] = further(blocks[k], "z", 2 * k, 8)
    grad_tokens, down_gradient, output, grad_magnitude = finish(
        z, tokens_full, scale, parts, blocks
    )
    return (output, grad_tokens, grad_magnitude.reshape(-1), up_gradient, down_gradient.T)


def solution(mesh):
    split = Mesh(mesh.devices.reshape(4, 4, 8, 2), ROW + COL)
    return jax.shard_map(
        on_device,
        mesh=split,
        in_specs=(P(COL, ROW), P(ROW, COL), P(ROW, None), P(None, COL), P(COL), P(ROW, COL)),
        out_specs=(P(ROW, COL), P(COL, ROW), P(COL), P(None, COL), P(ROW, None)),
        check_vma=False,
    )
```

```python
import jax
import jax.numpy as jnp
from jax import lax
from jax.experimental import pallas as pl
from jax.experimental.pallas import tpu as pltpu
from jax.sharding import Mesh
from jax.sharding import PartitionSpec as P

adapter_scale = 2.0
epsilon = 1e-06
bf16 = jnp.bfloat16
f32 = jnp.float32
ROW = ("x", "y")
COL = ("z", "c")
CHUNK = 512
RANK = 16
LANES = 128
MIB = 1024 * 1024
LIMIT = 63 * MIB + 768 * 1024
ANY = pl.BlockSpec(memory_space=pl.ANY)
SMEM = pl.BlockSpec(memory_space=pltpu.SMEM)


def pieces(value):
    high = value.astype(bf16)
    rest = value - high.astype(f32)
    mid = rest.astype(bf16)
    low = (rest - mid.astype(f32)).astype(bf16)
    return high, mid, low


def dot(left, right, left_dim, right_dim):
    return lax.dot_general(
        left, right, (((left_dim,), (right_dim,)), ((), ())), preferred_element_type=f32
    )


def three(left, right, left_dim, right_dim):
    out = dot(jnp.concatenate(pieces(left), axis=0), right, left_dim, right_dim)
    return out[:RANK] + out[RANK : 2 * RANK] + out[2 * RANK :]


def chunks_of(width):
    return [(at, min(CHUNK, width - at)) for at in range(0, width, CHUNK)]


def call(body, flops, moved, **options):
    return pl.pallas_call(
        body,
        compiler_params=pltpu.CompilerParams(vmem_limit_bytes=LIMIT),
        cost_estimate=pl.CostEstimate(flops=flops, bytes_accessed=moved, transcendentals=0),
        **options,
    )


def begin(source, target, sem):
    copy = pltpu.make_async_copy(source, target, sem)
    copy.start()
    return copy


def stream(pairs, sem, chunks, depth=2):
    def copies(j):
        for i, (source, target) in enumerate(pairs):
            index = (slice(None),) * (len(target.shape) - 1) + (pl.ds(*chunks[j]),)
            yield pltpu.make_async_copy(source.at[index], target.at[index], sem.at[i, j])

    def start(j):
        if j < len(chunks):
            for copy in copies(j):
                copy.start()

    def ready(j):
        for copy in copies(j):
            copy.wait()
        start(j + depth)

    for j in range(depth):
        start(j)
    return ready


def in_rows(row):
    return [row[:, at : at + LANES] for at in range(0, row.shape[1], LANES)]


def in_line(rows, at, size):
    return jnp.concatenate(
        [rows[k : k + 1, :] for k in range(at // LANES, (at + size) // LANES)], axis=1
    )


def merge_kernel(
    after_hbm, down_hbm, up_hbm, weight_hbm, merged_hbm, sums_hbm,
    down, up, weight, merged, sums, up_cat, totals, small_sem, in_sem, out_sem,
):
    depth, width = weight.shape
    rows, tile = 256, 256
    steps = [slice(at, at + rows) for at in range(0, depth, rows)]
    first = begin(up_hbm, up, small_sem.at[0]), begin(down_hbm, down, small_sem.at[1])
    fetches = [begin(weight_hbm.at[p], weight.at[p], in_sem.at[j]) for j, p in enumerate(steps)]
    totals[...] = jnp.zeros_like(totals)
    for copy in first:
        copy.wait()
    for at in range(0, width, tile):
        cols = slice(at, at + tile)
        u1, u2, u3 = pieces(up[:, cols])
        up_cat[:, cols] = jnp.concatenate([u1, u2, u1, u3, u1, u2], axis=0)
    d1, d2, d3 = pieces(down[...] * adapter_scale)
    down_cat = jnp.concatenate([d1, d1, d2, d1, d3, d2], axis=0)
    stores = []
    for j, part in enumerate(steps):
        fetches[j].wait()
        for at in range(0, width, tile):
            cols = slice(at, at + tile)
            value = weight[part, cols].astype(f32) + dot(down_cat[:, part], up_cat[:, cols], 0, 0)
            merged[part, cols] = value.astype(bf16)
            totals[:, cols] += jnp.sum((value * value).reshape(rows // 8, 8, tile), axis=0)
        stores.append(begin(merged.at[part], merged_hbm.at[part], out_sem.at[j]))
    lines = in_rows(jnp.sum(totals[...], axis=0, keepdims=True))
    sums[...] = jnp.concatenate(lines + [jnp.zeros((32 - len(lines), LANES), f32)], axis=0)
    stores.append(begin(sums, sums_hbm, small_sem.at[0]))
    for copy in stores:
        copy.wait()


def merge(after, down_t, up, weight):
    depth, width = weight.shape
    return call(
        merge_kernel,
        12 * depth * width,
        4 * depth * width,
        in_specs=[ANY] * 4,
        out_specs=[ANY] * 2,
        out_shape=[
            jax.ShapeDtypeStruct((depth, width), bf16),
            jax.ShapeDtypeStruct((32, LANES), f32),
        ],
        scratch_shapes=[
            pltpu.VMEM((RANK, depth), f32),
            pltpu.VMEM((RANK, width), f32),
            pltpu.VMEM((depth, width), bf16),
            pltpu.VMEM((depth, width), bf16),
            pltpu.VMEM((32, LANES), f32),
            pltpu.VMEM((6 * RANK, width), bf16),
            pltpu.VMEM((8, width), f32),
            pltpu.SemaphoreType.DMA((2,)),
            pltpu.SemaphoreType.DMA((4,)),
            pltpu.SemaphoreType.DMA((4,)),
        ],
        name="merge",
    )(after, down_t, up, weight)


def spread_kernel(cot_hbm, out_hbm, cot, in_sem, out_sem):
    begin(cot_hbm, cot, in_sem.at[0]).wait()
    copies = [begin(cot, out_hbm.at[r], out_sem.at[r]) for r in range(16)]
    for copy in copies:
        copy.wait()


def spread(cot):
    return call(
        spread_kernel,
        cot.size,
        4 * MIB,
        in_specs=[ANY],
        out_specs=ANY,
        out_shape=jax.ShapeDtypeStruct((16,) + cot.shape, bf16),
        scratch_shapes=[
            pltpu.VMEM(cot.shape, bf16),
            pltpu.SemaphoreType.DMA((1,)),
            pltpu.SemaphoreType.DMA((16,)),
        ],
        name="spread",
    )(cot)


def project_kernel(
    place_ref, own_hbm, other_hbm, down_hbm, sums_hbm, small_hbm, tokens_hbm,
    tokens, down, small, first_sem, sem,
):
    z, core = place_ref[0], place_ref[1]
    copies = [
        begin(down_hbm, down, first_sem.at[0]),
        begin(sums_hbm, small.at[64:], first_sem.at[1]),
    ]
    for k in range(8):
        back = lax.rem(z + 8 - (k - k % 2), 8)
        if k % 2:
            back = back + 1 - 2 * lax.rem(back, 2)
        rows = slice(32 * k, 32 * k + 32)
        copies.append(begin(own_hbm.at[rows], tokens.at[back, core], sem.at[0, k]))
        copies.append(begin(other_hbm.at[rows], tokens.at[back, 1 - core], sem.at[1, k]))
    for copy in copies:
        copy.wait()
    stores = [begin(tokens, tokens_hbm, first_sem.at[0])]
    proj = three(down[...], tokens[...].reshape(512, down.shape[1]), 1, 1)
    for k in range(4):
        small[RANK * k : RANK * k + RANK, :] = proj[:, LANES * k : LANES * k + LANES]
    stores.append(begin(small, small_hbm, first_sem.at[1]))
    for copy in stores:
        copy.wait()


def project(place, own, other, down_t, sums):
    depth = down_t.shape[1]
    return call(
        project_kernel,
        2 * 512 * 256 * depth,
        3 * MIB,
        in_specs=[SMEM] + [ANY] * 4,
        out_specs=[ANY] * 2,
        out_shape=[
            jax.ShapeDtypeStruct((96, LANES), f32),
            jax.ShapeDtypeStruct((8, 2, 32, depth), bf16),
        ],
        scratch_shapes=[
            pltpu.VMEM((8, 2, 32, depth), bf16),
            pltpu.VMEM((RANK, depth), f32),
            pltpu.VMEM((96, LANES), f32),
            pltpu.SemaphoreType.DMA((2,)),
            pltpu.SemaphoreType.DMA((2, 8)),
        ],
        name="project",
    )(place, own, other, down_t, sums)


def forward_kernel(tokens_hbm, merged_hbm, part_hbm, tokens, merged, part, first_sem, sem, out_sem):
    depth, width = merged.shape
    chunks = chunks_of(width)
    first = begin(tokens_hbm, tokens, first_sem.at[0])
    ready = stream([(merged_hbm, merged)], sem, chunks)
    first.wait()
    stores = []
    for j, (at, size) in enumerate(chunks):
        ready(j)
        cols = slice(at, at + size)
        product = dot(tokens[...], merged[:, cols], 1, 0).astype(bf16)
        part[:, :, cols] = product.reshape(16, 32, size)
        stores.append(begin(part.at[:, :, cols], part_hbm.at[:, :, cols], out_sem.at[j]))
    for copy in stores:
        copy.wait()


def forward(tokens, merged_low):
    depth, width = merged_low.shape
    count = len(chunks_of(width))
    return call(
        forward_kernel,
        2 * 512 * depth * width,
        12 * MIB,
        in_specs=[ANY] * 2,
        out_specs=ANY,
        out_shape=jax.ShapeDtypeStruct((16, 32, width + LANES), bf16),
        scratch_shapes=[
            pltpu.VMEM((512, depth), bf16),
            pltpu.VMEM((depth, width), bf16),
            pltpu.VMEM((16, 32, width), bf16),
            pltpu.SemaphoreType.DMA((1,)),
            pltpu.SemaphoreType.DMA((1, count)),
            pltpu.SemaphoreType.DMA((count,)),
        ],
        name="forward",
    )(tokens, merged_low)


def magnitude_kernel(given_hbm, part_hbm, out_hbm, cot, part, extra, sem, out_sem):
    width = cot.shape[2]
    chunks = chunks_of(width)
    ready = stream([(given_hbm, cot), (part_hbm, part)], sem, chunks, len(chunks))
    rows = []
    for j, (at, size) in enumerate(chunks):
        ready(j)
        cols = slice(at, at + size)
        product = cot[:, :, cols].astype(f32) * part[:, :, cols].astype(f32)
        total = jnp.sum(product.reshape(64, 8, size), axis=0)
        rows += in_rows(jnp.sum(total, axis=0, keepdims=True))
    rows.append(jnp.zeros((32 - len(rows), LANES), f32))
    sums = jnp.concatenate(rows, axis=0).astype(bf16)
    extra[...] = jnp.broadcast_to(sums[None], extra.shape)
    begin(extra, out_hbm.at[:, :, width:], out_sem.at[0]).wait()


def add_magnitude(given, part):
    blocks, rows, width = given.shape
    return call(
        magnitude_kernel,
        4 * 512 * width,
        7 * MIB,
        in_specs=[ANY, ANY],
        out_specs=ANY,
        out_shape=jax.ShapeDtypeStruct(part.shape, bf16),
        scratch_shapes=[
            pltpu.VMEM((blocks, rows, width), bf16),
            pltpu.VMEM((blocks, rows, width), bf16),
            pltpu.VMEM((blocks, rows, LANES), bf16),
            pltpu.SemaphoreType.DMA((2, len(chunks_of(width)))),
            pltpu.SemaphoreType.DMA((1,)),
        ],
        input_output_aliases={1: 0},
        name="magnitude",
    )(given, part)


def pack(low, out):
    high = low.astype(bf16)
    rest = (low - high.astype(f32)).astype(bf16)
    out[:, :CHUNK] = high
    out[:, CHUNK:] = rest
    return high.astype(f32) + rest.astype(f32)


def unpack(got):
    got = got.astype(f32)
    return got[:, :CHUNK] + got[:, CHUNK:]


def backward_kernel(
    core_ref, small_hbm, magnitude_hbm, up_hbm, given_hbm, merged_hbm, own_hbm, send_hbm, scale_hbm,
    squares, magnitude, up, cot, merged, total, own, send, scale, first_sem, sem,
):
    core = core_ref[0]
    depth, width = merged.shape
    chunks = chunks_of(width)
    count = width // LANES
    first = (
        begin(small_hbm.at[64:], squares, first_sem.at[0]),
        begin(up_hbm, up, first_sem.at[1]),
        begin(magnitude_hbm, magnitude, first_sem.at[2]),
    )
    ready = stream([(given_hbm, cot), (merged_hbm, merged)], sem, chunks)
    for copy in first:
        copy.wait()
    norm = jnp.sqrt(squares[...] + epsilon)
    factors = magnitude[...] / norm[:count]
    scale[...] = jnp.zeros_like(scale)
    scale[:count, :] = factors
    scale[32:, :] = norm
    last = begin(scale, scale_hbm, first_sem.at[0])
    low = jnp.zeros((RANK, CHUNK), f32)
    for j, (at, size) in enumerate(chunks):
        ready(j)
        cols = slice(at, at + size)
        value = cot[:, :, cols].reshape(512, size).astype(f32)
        grad = (value * in_line(factors, at, size)).astype(bf16)
        product = dot(grad, merged[:, cols], 1, 1)
        if j == 0:
            total[...] = product
        else:
            total[...] += product
        low += three(up[:, cols], grad, 1, 1)
    for z in range(8):
        theirs = pl.ds(pl.multiple_of((2 * z + 1 - core) * 32, 32), 32)
        send[32 * z : 32 * z + 32, :] = total[theirs, :].astype(bf16)
    pack(low, send.at[256:272, :])
    first = begin(send, send_hbm, first_sem.at[1])
    for z in range(8):
        mine = pl.ds(pl.multiple_of((2 * z + core) * 32, 32), 32)
        own[32 * z : 32 * z + 32, :] = total[mine, :].astype(bf16)
    own[256:272, :] = send[256:272, :]
    begin(own, own_hbm, first_sem.at[2]).wait()
    first.wait()
    last.wait()


def backward(core, small, magnitude, up, given, merged_low):
    depth, width = merged_low.shape
    count = len(chunks_of(width))
    return call(
        backward_kernel,
        2 * 512 * depth * width,
        12 * MIB,
        in_specs=[SMEM] + [ANY] * 5,
        out_specs=[ANY] * 3,
        out_shape=[jax.ShapeDtypeStruct((272, depth), bf16)] * 2
        + [jax.ShapeDtypeStruct((64, LANES), f32)],
        scratch_shapes=[
            pltpu.VMEM((32, LANES), f32),
            pltpu.VMEM(magnitude.shape, f32),
            pltpu.VMEM((RANK, width), f32),
            pltpu.VMEM((16, 32, width), bf16),
            pltpu.VMEM((depth, width), bf16),
            pltpu.VMEM((512, depth), f32),
            pltpu.VMEM((272, depth), bf16),
            pltpu.VMEM((272, depth), bf16),
            pltpu.VMEM((64, LANES), f32),
            pltpu.SemaphoreType.DMA((3,)),
            pltpu.SemaphoreType.DMA((2, count)),
        ],
        name="backward",
    )(core, small, magnitude, up, given, merged_low)


def pair_kernel(z_ref, own_hbm, got_hbm, keep_hbm, send_hbm, own, got, keep, send, sem, out_sem):
    bit = lax.rem(z_ref[0], 2)
    copies = begin(own_hbm, own, sem.at[0]), begin(got_hbm, got, sem.at[1])
    for copy in copies:
        copy.wait()
    low = unpack(own[256:272, :]) + unpack(got[256:272, :])
    pack(low, send.at[128:144, :])
    keep[128:144, :] = send[128:144, :]
    stores = []
    for target, other, out in ((send, 1 - bit, send_hbm), (keep, bit, keep_hbm)):
        for i in range(4):
            block = pl.ds(pl.multiple_of((2 * i + other) * 32, 32), 32)
            value = own[block, :].astype(f32) + got[block, :].astype(f32)
            target[32 * i : 32 * i + 32, :] = value.astype(bf16)
        stores.append(begin(target, out, out_sem.at[len(stores)]))
    for copy in stores:
        copy.wait()


def pair(z, own, got):
    rows, depth = own.shape
    return call(
        pair_kernel,
        4 * rows * depth,
        6 * rows * depth,
        in_specs=[SMEM, ANY, ANY],
        out_specs=[ANY] * 2,
        out_shape=[jax.ShapeDtypeStruct((144, depth), bf16)] * 2,
        scratch_shapes=[pltpu.VMEM((rows, depth), bf16)] * 2
        + [pltpu.VMEM((144, depth), bf16)] * 2
        + [pltpu.SemaphoreType.DMA((2,))] * 2,
        name="pair",
    )(z, own, got)


def quad_kernel(z_ref, after_hbm, keep_hbm, got_hbm, *refs):
    out_hbm = refs[:4]
    keep, got, send, sem, out_sem = refs[4:]
    half = z_ref[0] // 2
    copies = begin(keep_hbm, keep, sem.at[0]), begin(got_hbm, got, sem.at[1])
    for copy in copies:
        copy.wait()
    low = unpack(keep[128:144, :]) + unpack(got[128:144, :])
    pack(low, send.at[0, 32:48, :])
    stores = []
    for k in [2, 1, 3, 0]:
        block = pl.ds(pl.multiple_of(lax.rem(half + k, 4) * 32, 32), 32)
        send[k, :32, :] = (keep[block, :].astype(f32) + got[block, :].astype(f32)).astype(bf16)
        if k:
            send[k, 32:48, :] = send[0, 32:48, :]
        stores.append(begin(send.at[k], out_hbm[k], out_sem.at[k]))
    for copy in stores:
        copy.wait()


def quad(z, after, keep, got):
    rows, depth = keep.shape
    return call(
        quad_kernel,
        4 * rows * depth,
        6 * rows * depth,
        in_specs=[SMEM, ANY, ANY, ANY],
        out_specs=[ANY] * 4,
        out_shape=[jax.ShapeDtypeStruct((48, depth), bf16)] * 4,
        scratch_shapes=[pltpu.VMEM((rows, depth), bf16)] * 2
        + [pltpu.VMEM((4, 48, depth), bf16)]
        + [pltpu.SemaphoreType.DMA((2,)), pltpu.SemaphoreType.DMA((4,))],
        name="quad",
    )(z, after, keep, got)


def finish_kernel(z_ref, tokens_hbm, *refs):
    parts_hbm = refs[:4]
    grad_hbm, down_hbm, parts, tokens, lows, grad, down, sem, out_sem = refs[4:]
    half = z_ref[0] // 2
    copies = [begin(parts_hbm[k], parts.at[k], sem.at[k]) for k in range(4)]
    later = begin(tokens_hbm, tokens, sem.at[4])
    for copy in copies:
        copy.wait()
    total = parts[0, :32, :].astype(f32)
    for k in range(1, 4):
        total += parts[k, :32, :].astype(f32)
    grad[...] = total.astype(bf16)
    first = begin(grad, grad_hbm, out_sem.at[0])
    for k in range(4):
        lows[lax.rem(half + 4 - k, 4)] = unpack(parts[k, 32:48, :])
    low = (lows[0] + lows[1]) + (lows[2] + lows[3])
    later.wait()
    down[...] = three(low * adapter_scale, tokens[...], 1, 0)
    begin(down, down_hbm, out_sem.at[1]).wait()
    first.wait()


def finish(z, tokens, parts):
    depth = tokens.shape[1]
    return call(
        finish_kernel,
        2 * 512 * 256 * depth,
        2 * MIB,
        in_specs=[SMEM] + [ANY] * 5,
        out_specs=[ANY, ANY],
        out_shape=[
            jax.ShapeDtypeStruct((32, depth), bf16),
            jax.ShapeDtypeStruct((RANK, depth), f32),
        ],
        scratch_shapes=[
            pltpu.VMEM((4, 48, depth), bf16),
            pltpu.VMEM(tokens.shape, bf16),
            pltpu.VMEM((4, RANK, CHUNK), f32),
            pltpu.VMEM((32, depth), bf16),
            pltpu.VMEM((RANK, depth), f32),
            pltpu.SemaphoreType.DMA((5,)),
            pltpu.SemaphoreType.DMA((2,)),
        ],
        name="finish",
    )(z, tokens, *parts)


def up_kernel(
    small_hbm, scale_hbm, given_hbm, out_hbm, small, scale, cot, out, first_sem, sem, out_sem
):
    width = cot.shape[2]
    chunks = chunks_of(width)
    first = begin(small_hbm, small, first_sem.at[0]), begin(scale_hbm, scale, first_sem.at[1])
    ready = stream([(given_hbm, cot)], sem, chunks, 3)
    for copy in first:
        copy.wait()
    proj = [small[RANK * k : RANK * k + RANK, :] for k in range(4)]
    proj = jnp.concatenate(proj, axis=1) * adapter_scale
    factors = scale[:32, :]
    stores = []
    for j, (at, size) in enumerate(chunks):
        ready(j)
        cols = slice(at, at + size)
        value = cot[:, :, cols].reshape(512, size).astype(f32)
        grad = (value * in_line(factors, at, size)).astype(bf16)
        out[:, cols] = three(proj, grad, 1, 0)
        stores.append(begin(out.at[:, cols], out_hbm.at[:, cols], out_sem.at[j]))
    for copy in stores:
        copy.wait()


def up_gradient_of(small, scale, given):
    width = given.shape[2]
    count = len(chunks_of(width))
    return call(
        up_kernel,
        2 * 512 * 256 * width,
        4 * MIB,
        in_specs=[ANY] * 3,
        out_specs=ANY,
        out_shape=jax.ShapeDtypeStruct((RANK, width), f32),
        scratch_shapes=[
            pltpu.VMEM(small.shape, f32),
            pltpu.VMEM(scale.shape, f32),
            pltpu.VMEM(given.shape, bf16),
            pltpu.VMEM((RANK, width), f32),
            pltpu.SemaphoreType.DMA((2,)),
            pltpu.SemaphoreType.DMA((1, count)),
            pltpu.SemaphoreType.DMA((count,)),
        ],
        name="up_gradient",
    )(small, scale, given)


def output_kernel(
    after_hbm, scale_hbm, parts_hbm, out_hbm, mag_hbm, scale, parts, out, mag, first_sem, sem, out_sem
):
    width = out.shape[1]
    chunks = chunks_of(width)
    count = width // LANES
    first = (
        begin(scale_hbm, scale, first_sem.at[0]),
        begin(parts_hbm.at[:, :, width:], parts.at[:, :, width:], first_sem.at[1]),
    )
    ready = stream([(parts_hbm, parts.at[:, :, :width])], sem, chunks, len(chunks))
    for copy in first:
        copy.wait()

    def added(cols):
        total = parts[0, :, cols].astype(f32)
        for r in range(1, 16):
            total += parts[r, :, cols].astype(f32)
        return total

    mag[...] = added(slice(width, width + LANES))[:count] / scale[32 : 32 + count, :]
    stores = [begin(mag, mag_hbm, first_sem.at[0])]
    factors = scale[:32, :]
    for j, (at, size) in enumerate(chunks):
        ready(j)
        cols = slice(at, at + size)
        out[:, cols] = (added(cols) * in_line(factors, at, size)).astype(bf16)
        stores.append(begin(out.at[:, cols], out_hbm.at[:, cols], out_sem.at[j]))
    for copy in stores:
        copy.wait()


def output_of(after, scale, parts):
    width = parts.shape[2] - LANES
    count = len(chunks_of(width))
    return call(
        output_kernel,
        16 * 32 * width,
        4 * MIB,
        in_specs=[ANY] * 3,
        out_specs=[ANY] * 2,
        out_shape=[
            jax.ShapeDtypeStruct((32, width), bf16),
            jax.ShapeDtypeStruct((width // LANES, LANES), f32),
        ],
        scratch_shapes=[
            pltpu.VMEM(scale.shape, f32),
            pltpu.VMEM(parts.shape, bf16),
            pltpu.VMEM((32, width), bf16),
            pltpu.VMEM((width // LANES, LANES), f32),
            pltpu.SemaphoreType.DMA((2,)),
            pltpu.SemaphoreType.DMA((1, count)),
            pltpu.SemaphoreType.DMA((count,)),
        ],
        name="output",
    )(after, scale, parts)


def exchange(blocks):
    return lax.all_to_all(blocks, ROW, 0, 0, tiled=False)


def further(value, axis, k, size):
    return lax.ppermute(value, axis, [(i, (i + k) % size) for i in range(size)])


def shifted(value, axis):
    return [further(value, axis, k, 4) for k in (1, 2, 3)]


def added(value, arrived):
    one, two, other = arrived
    return (value + two) + (one + other)


def on_device(tokens, weight, down_adapter, up_adapter, magnitude, out_cotangent):
    z, core = [lax.axis_index(name).astype(jnp.int32).reshape(1) for name in COL]
    swap = [(0, 1), (1, 0)]
    down_t = down_adapter.T
    magnitude = magnitude.reshape(-1, LANES)
    given = exchange(spread(out_cotangent))
    beside = [(i, i ^ 1) for i in range(8)]
    two = jnp.concatenate([tokens, lax.ppermute(tokens, "z", beside)], axis=0)
    own = [two] + [further(two, "z", 2 * k, 8) for k in (1, 2, 3)]
    merged_low, sums = merge(two, down_t, up_adapter, weight)
    own = jnp.concatenate(own, axis=0)
    other = lax.ppermute(own, "c", swap)
    place = jnp.concatenate([z, core])
    small, tokens_full = project(place, own, other, down_t, sums)
    tokens_full = tokens_full.reshape(512, -1)
    part = forward(tokens_full, merged_low)
    arrived = shifted(small, "x")
    arrived, part = lax.optimization_barrier((arrived, part))
    small = added(small, arrived)
    part = add_magnitude(given, part)
    arrived = shifted(small, "y")
    arrived, part = lax.optimization_barrier((arrived, part))
    parts = exchange(part)
    small = added(small, arrived)
    own, send, scale = backward(core, small, magnitude, up_adapter, given, merged_low)
    got = lax.ppermute(send, "c", swap)
    keep, send = pair(z, own, got)
    got = lax.ppermute(send, "z", beside)
    up_gradient = up_gradient_of(small, scale, given)
    blocks = list(quad(z, up_gradient, keep, got))
    for k in range(1, 4):
        blocks[k] = further(blocks[k], "z", 2 * k, 8)
    grad_tokens, down_gradient = finish(z, tokens_full, blocks)
    output, grad_magnitude = output_of(grad_tokens, scale, parts)
    return (output, grad_tokens, grad_magnitude.reshape(-1), up_gradient, down_gradient.T)


def solution(mesh):
    split = Mesh(mesh.devices.reshape(4, 4, 8, 2), ROW + COL)
    return jax.shard_map(
        on_device,
        mesh=split,
        in_specs=(P(COL, ROW), P(ROW, COL), P(ROW, None), P(None, COL), P(COL), P(ROW, COL)),
        out_specs=(P(ROW, COL), P(COL, ROW), P(COL), P(None, COL), P(ROW, None)),
        check_vma=False,
    )
```

```python
import jax
import jax.numpy as jnp
from jax import lax
from jax.experimental import pallas as pl
from jax.experimental.pallas import tpu as pltpu
from jax.sharding import Mesh
from jax.sharding import PartitionSpec as P

adapter_scale = 2.0
epsilon = 1e-06
bf16 = jnp.bfloat16
f32 = jnp.float32
ROW = ("x", "y")
COL = ("z", "c")
CHUNK = 512
RANK = 16
LANES = 128
MIB = 1024 * 1024
LIMIT = 63 * MIB + 768 * 1024
ANY = pl.BlockSpec(memory_space=pl.ANY)
SMEM = pl.BlockSpec(memory_space=pltpu.SMEM)


def pieces(value):
    high = value.astype(bf16)
    rest = value - high.astype(f32)
    mid = rest.astype(bf16)
    low = (rest - mid.astype(f32)).astype(bf16)
    return high, mid, low


def dot(left, right, left_dim, right_dim):
    return lax.dot_general(
        left, right, (((left_dim,), (right_dim,)), ((), ())), preferred_element_type=f32
    )


def three(left, right, left_dim, right_dim):
    out = dot(jnp.concatenate(pieces(left), axis=0), right, left_dim, right_dim)
    return out[:RANK] + out[RANK : 2 * RANK] + out[2 * RANK :]


def chunks_of(width):
    return [(at, min(CHUNK, width - at)) for at in range(0, width, CHUNK)]


def call(body, flops, moved, **options):
    return pl.pallas_call(
        body,
        compiler_params=pltpu.CompilerParams(vmem_limit_bytes=LIMIT),
        cost_estimate=pl.CostEstimate(flops=flops, bytes_accessed=moved, transcendentals=0),
        **options,
    )


def begin(source, target, sem):
    copy = pltpu.make_async_copy(source, target, sem)
    copy.start()
    return copy


def stream(pairs, sem, chunks, depth=2):
    def copies(j):
        for i, (source, target) in enumerate(pairs):
            index = (slice(None),) * (len(target.shape) - 1) + (pl.ds(*chunks[j]),)
            yield pltpu.make_async_copy(source.at[index], target.at[index], sem.at[i, j])

    def start(j):
        if j < len(chunks):
            for copy in copies(j):
                copy.start()

    def ready(j):
        for copy in copies(j):
            copy.wait()
        start(j + depth)

    for j in range(depth):
        start(j)
    return ready


def in_rows(row):
    return [row[:, at : at + LANES] for at in range(0, row.shape[1], LANES)]


def in_line(rows, at, size):
    return jnp.concatenate(
        [rows[k : k + 1, :] for k in range(at // LANES, (at + size) // LANES)], axis=1
    )


def merge_kernel(
    after_hbm, down_hbm, up_hbm, weight_hbm, merged_hbm, sums_hbm,
    down, up, weight, merged, sums, up_cat, totals, small_sem, in_sem, out_sem,
):
    depth, width = weight.shape
    rows, tile = 256, 256
    steps = [slice(at, at + rows) for at in range(0, depth, rows)]
    first = begin(up_hbm, up, small_sem.at[0]), begin(down_hbm, down, small_sem.at[1])
    fetches = [begin(weight_hbm.at[p], weight.at[p], in_sem.at[j]) for j, p in enumerate(steps)]
    totals[...] = jnp.zeros_like(totals)
    for copy in first:
        copy.wait()
    for at in range(0, width, tile):
        cols = slice(at, at + tile)
        u1, u2, u3 = pieces(up[:, cols])
        up_cat[:, cols] = jnp.concatenate([u1, u2, u1, u3, u1, u2], axis=0)
    d1, d2, d3 = pieces(down[...] * adapter_scale)
    down_cat = jnp.concatenate([d1, d1, d2, d1, d3, d2], axis=0)
    stores = []
    for j, part in enumerate(steps):
        fetches[j].wait()
        for at in range(0, width, tile):
            cols = slice(at, at + tile)
            value = weight[part, cols].astype(f32) + dot(down_cat[:, part], up_cat[:, cols], 0, 0)
            merged[part, cols] = value.astype(bf16)
            totals[:, cols] += jnp.sum((value * value).reshape(rows // 8, 8, tile), axis=0)
        stores.append(begin(merged.at[part], merged_hbm.at[part], out_sem.at[j]))
    lines = in_rows(jnp.sum(totals[...], axis=0, keepdims=True))
    sums[...] = jnp.concatenate(lines + [jnp.zeros((32 - len(lines), LANES), f32)], axis=0)
    stores.append(begin(sums, sums_hbm, small_sem.at[0]))
    for copy in stores:
        copy.wait()


def merge(after, down_t, up, weight):
    depth, width = weight.shape
    return call(
        merge_kernel,
        12 * depth * width,
        4 * depth * width,
        in_specs=[ANY] * 4,
        out_specs=[ANY] * 2,
        out_shape=[
            jax.ShapeDtypeStruct((depth, width), bf16),
            jax.ShapeDtypeStruct((32, LANES), f32),
        ],
        scratch_shapes=[
            pltpu.VMEM((RANK, depth), f32),
            pltpu.VMEM((RANK, width), f32),
            pltpu.VMEM((depth, width), bf16),
            pltpu.VMEM((depth, width), bf16),
            pltpu.VMEM((32, LANES), f32),
            pltpu.VMEM((6 * RANK, width), bf16),
            pltpu.VMEM((8, width), f32),
            pltpu.SemaphoreType.DMA((2,)),
            pltpu.SemaphoreType.DMA((4,)),
            pltpu.SemaphoreType.DMA((4,)),
        ],
        name="merge",
    )(after, down_t, up, weight)


def spread_kernel(cot_hbm, out_hbm, cot, in_sem, out_sem):
    begin(cot_hbm, cot, in_sem.at[0]).wait()
    copies = [begin(cot, out_hbm.at[r], out_sem.at[r]) for r in range(16)]
    for copy in copies:
        copy.wait()


def spread(cot):
    return call(
        spread_kernel,
        cot.size,
        4 * MIB,
        in_specs=[ANY],
        out_specs=ANY,
        out_shape=jax.ShapeDtypeStruct((16,) + cot.shape, bf16),
        scratch_shapes=[
            pltpu.VMEM(cot.shape, bf16),
            pltpu.SemaphoreType.DMA((1,)),
            pltpu.SemaphoreType.DMA((16,)),
        ],
        name="spread",
    )(cot)


def project_kernel(
    place_ref, own_hbm, other_hbm, down_hbm, sums_hbm, small_hbm, tokens_hbm,
    tokens, down, small, first_sem, sem,
):
    z, core = place_ref[0], place_ref[1]
    copies = [
        begin(down_hbm, down, first_sem.at[0]),
        begin(sums_hbm, small.at[64:], first_sem.at[1]),
    ]
    for k in range(8):
        back = lax.rem(z + 8 - (k - k % 2), 8)
        if k % 2:
            back = back + 1 - 2 * lax.rem(back, 2)
        rows = slice(32 * k, 32 * k + 32)
        copies.append(begin(own_hbm.at[rows], tokens.at[back, core], sem.at[0, k]))
        copies.append(begin(other_hbm.at[rows], tokens.at[back, 1 - core], sem.at[1, k]))
    for copy in copies:
        copy.wait()
    stores = [begin(tokens, tokens_hbm, first_sem.at[0])]
    proj = three(down[...], tokens[...].reshape(512, down.shape[1]), 1, 1)
    for k in range(4):
        small[RANK * k : RANK * k + RANK, :] = proj[:, LANES * k : LANES * k + LANES]
    stores.append(begin(small, small_hbm, first_sem.at[1]))
    for copy in stores:
        copy.wait()


def project(place, own, other, down_t, sums):
    depth = down_t.shape[1]
    return call(
        project_kernel,
        2 * 512 * 256 * depth,
        3 * MIB,
        in_specs=[SMEM] + [ANY] * 4,
        out_specs=[ANY] * 2,
        out_shape=[
            jax.ShapeDtypeStruct((96, LANES), f32),
            jax.ShapeDtypeStruct((8, 2, 32, depth), bf16),
        ],
        scratch_shapes=[
            pltpu.VMEM((8, 2, 32, depth), bf16),
            pltpu.VMEM((RANK, depth), f32),
            pltpu.VMEM((96, LANES), f32),
            pltpu.SemaphoreType.DMA((2,)),
            pltpu.SemaphoreType.DMA((2, 8)),
        ],
        name="project",
    )(place, own, other, down_t, sums)


def forward_kernel(tokens_hbm, merged_hbm, part_hbm, tokens, merged, part, first_sem, sem, out_sem):
    depth, width = merged.shape
    chunks = chunks_of(width)
    first = begin(tokens_hbm, tokens, first_sem.at[0])
    ready = stream([(merged_hbm, merged)], sem, chunks)
    first.wait()
    stores = []
    for j, (at, size) in enumerate(chunks):
        ready(j)
        cols = slice(at, at + size)
        product = dot(tokens[...], merged[:, cols], 1, 0).astype(bf16)
        part[:, :, cols] = product.reshape(16, 32, size)
        stores.append(begin(part.at[:, :, cols], part_hbm.at[:, :, cols], out_sem.at[j]))
    for copy in stores:
        copy.wait()


def forward(tokens, merged_low):
    depth, width = merged_low.shape
    count = len(chunks_of(width))
    return call(
        forward_kernel,
        2 * 512 * depth * width,
        12 * MIB,
        in_specs=[ANY] * 2,
        out_specs=ANY,
        out_shape=jax.ShapeDtypeStruct((16, 32, width + LANES), bf16),
        scratch_shapes=[
            pltpu.VMEM((512, depth), bf16),
            pltpu.VMEM((depth, width), bf16),
            pltpu.VMEM((16, 32, width), bf16),
            pltpu.SemaphoreType.DMA((1,)),
            pltpu.SemaphoreType.DMA((1, count)),
            pltpu.SemaphoreType.DMA((count,)),
        ],
        name="forward",
    )(tokens, merged_low)


def magnitude_kernel(given_hbm, part_hbm, out_hbm, cot, part, extra, sem, out_sem):
    width = cot.shape[2]
    chunks = chunks_of(width)
    ready = stream([(given_hbm, cot), (part_hbm, part)], sem, chunks, len(chunks))
    rows = []
    for j, (at, size) in enumerate(chunks):
        ready(j)
        cols = slice(at, at + size)
        product = cot[:, :, cols].astype(f32) * part[:, :, cols].astype(f32)
        total = jnp.sum(product.reshape(64, 8, size), axis=0)
        rows += in_rows(jnp.sum(total, axis=0, keepdims=True))
    rows.append(jnp.zeros((32 - len(rows), LANES), f32))
    sums = jnp.concatenate(rows, axis=0).astype(bf16)
    extra[...] = jnp.broadcast_to(sums[None], extra.shape)
    begin(extra, out_hbm.at[:, :, width:], out_sem.at[0]).wait()


def add_magnitude(given, part):
    blocks, rows, width = given.shape
    return call(
        magnitude_kernel,
        4 * 512 * width,
        7 * MIB,
        in_specs=[ANY, ANY],
        out_specs=ANY,
        out_shape=jax.ShapeDtypeStruct(part.shape, bf16),
        scratch_shapes=[
            pltpu.VMEM((blocks, rows, width), bf16),
            pltpu.VMEM((blocks, rows, width), bf16),
            pltpu.VMEM((blocks, rows, LANES), bf16),
            pltpu.SemaphoreType.DMA((2, len(chunks_of(width)))),
            pltpu.SemaphoreType.DMA((1,)),
        ],
        input_output_aliases={1: 0},
        name="magnitude",
    )(given, part)


def pack(low, out):
    high = low.astype(bf16)
    rest = (low - high.astype(f32)).astype(bf16)
    out[:, :CHUNK] = high
    out[:, CHUNK:] = rest
    return high.astype(f32) + rest.astype(f32)


def unpack(got):
    got = got.astype(f32)
    return got[:, :CHUNK] + got[:, CHUNK:]


def backward_kernel(
    core_ref, small_hbm, magnitude_hbm, up_hbm, given_hbm, merged_hbm, own_hbm, send_hbm, scale_hbm,
    squares, magnitude, up, cot, merged, total, own, send, scale, first_sem, sem,
):
    core = core_ref[0]
    depth, width = merged.shape
    chunks = chunks_of(width)
    count = width // LANES
    first = (
        begin(small_hbm.at[64:], squares, first_sem.at[0]),
        begin(up_hbm, up, first_sem.at[1]),
        begin(magnitude_hbm, magnitude, first_sem.at[2]),
    )
    ready = stream([(given_hbm, cot), (merged_hbm, merged)], sem, chunks)
    for copy in first:
        copy.wait()
    norm = jnp.sqrt(squares[...] + epsilon)
    factors = magnitude[...] / norm[:count]
    scale[...] = jnp.zeros_like(scale)
    scale[:count, :] = factors
    scale[32:, :] = norm
    last = begin(scale, scale_hbm, first_sem.at[0])
    low = jnp.zeros((RANK, CHUNK), f32)
    for j, (at, size) in enumerate(chunks):
        ready(j)
        cols = slice(at, at + size)
        value = cot[:, :, cols].reshape(512, size).astype(f32)
        grad = (value * in_line(factors, at, size)).astype(bf16)
        product = dot(grad, merged[:, cols], 1, 1)
        if j == 0:
            total[...] = product
        else:
            total[...] += product
        low += three(up[:, cols], grad, 1, 1)
    for z in range(8):
        theirs = pl.ds(pl.multiple_of((2 * z + 1 - core) * 32, 32), 32)
        send[32 * z : 32 * z + 32, :] = total[theirs, :].astype(bf16)
    pack(low, send.at[256:272, :])
    first = begin(send, send_hbm, first_sem.at[1])
    for z in range(8):
        mine = pl.ds(pl.multiple_of((2 * z + core) * 32, 32), 32)
        own[32 * z : 32 * z + 32, :] = total[mine, :].astype(bf16)
    own[256:272, :] = send[256:272, :]
    begin(own, own_hbm, first_sem.at[2]).wait()
    first.wait()
    last.wait()


def backward(core, small, magnitude, up, given, merged_low):
    depth, width = merged_low.shape
    count = len(chunks_of(width))
    return call(
        backward_kernel,
        2 * 512 * depth * width,
        12 * MIB,
        in_specs=[SMEM] + [ANY] * 5,
        out_specs=[ANY] * 3,
        out_shape=[jax.ShapeDtypeStruct((272, depth), bf16)] * 2
        + [jax.ShapeDtypeStruct((64, LANES), f32)],
        scratch_shapes=[
            pltpu.VMEM((32, LANES), f32),
            pltpu.VMEM(magnitude.shape, f32),
            pltpu.VMEM((RANK, width), f32),
            pltpu.VMEM((16, 32, width), bf16),
            pltpu.VMEM((depth, width), bf16),
            pltpu.VMEM((512, depth), f32),
            pltpu.VMEM((272, depth), bf16),
            pltpu.VMEM((272, depth), bf16),
            pltpu.VMEM((64, LANES), f32),
            pltpu.SemaphoreType.DMA((3,)),
            pltpu.SemaphoreType.DMA((2, count)),
        ],
        name="backward",
    )(core, small, magnitude, up, given, merged_low)


def pair_kernel(z_ref, own_hbm, got_hbm, keep_hbm, send_hbm, own, got, keep, send, sem, out_sem):
    bit = lax.rem(z_ref[0], 2)
    copies = begin(own_hbm, own, sem.at[0]), begin(got_hbm, got, sem.at[1])
    for copy in copies:
        copy.wait()
    low = unpack(own[256:272, :]) + unpack(got[256:272, :])
    pack(low, send.at[128:144, :])
    keep[128:144, :] = send[128:144, :]
    stores = []
    for target, other, out in ((send, 1 - bit, send_hbm), (keep, bit, keep_hbm)):
        for i in range(4):
            block = pl.ds(pl.multiple_of((2 * i + other) * 32, 32), 32)
            value = own[block, :].astype(f32) + got[block, :].astype(f32)
            target[32 * i : 32 * i + 32, :] = value.astype(bf16)
        stores.append(begin(target, out, out_sem.at[len(stores)]))
    for copy in stores:
        copy.wait()


def pair(z, own, got):
    rows, depth = own.shape
    return call(
        pair_kernel,
        4 * rows * depth,
        6 * rows * depth,
        in_specs=[SMEM, ANY, ANY],
        out_specs=[ANY] * 2,
        out_shape=[jax.ShapeDtypeStruct((144, depth), bf16)] * 2,
        scratch_shapes=[pltpu.VMEM((rows, depth), bf16)] * 2
        + [pltpu.VMEM((144, depth), bf16)] * 2
        + [pltpu.SemaphoreType.DMA((2,))] * 2,
        name="pair",
    )(z, own, got)


def quad_kernel(z_ref, after_hbm, keep_hbm, got_hbm, *refs):
    out_hbm = refs[:4]
    keep, got, send, sem, out_sem = refs[4:]
    half = z_ref[0] // 2
    copies = begin(keep_hbm, keep, sem.at[0]), begin(got_hbm, got, sem.at[1])
    for copy in copies:
        copy.wait()
    low = unpack(keep[128:144, :]) + unpack(got[128:144, :])
    pack(low, send.at[0, 32:48, :])
    stores = []
    for k in [2, 1, 3, 0]:
        block = pl.ds(pl.multiple_of(lax.rem(half + k, 4) * 32, 32), 32)
        send[k, :32, :] = (keep[block, :].astype(f32) + got[block, :].astype(f32)).astype(bf16)
        if k:
            send[k, 32:48, :] = send[0, 32:48, :]
        stores.append(begin(send.at[k], out_hbm[k], out_sem.at[k]))
    for copy in stores:
        copy.wait()


def quad(z, after, keep, got):
    rows, depth = keep.shape
    return call(
        quad_kernel,
        4 * rows * depth,
        6 * rows * depth,
        in_specs=[SMEM, ANY, ANY, ANY],
        out_specs=[ANY] * 4,
        out_shape=[jax.ShapeDtypeStruct((48, depth), bf16)] * 4,
        scratch_shapes=[pltpu.VMEM((rows, depth), bf16)] * 2
        + [pltpu.VMEM((4, 48, depth), bf16)]
        + [pltpu.SemaphoreType.DMA((2,)), pltpu.SemaphoreType.DMA((4,))],
        name="quad",
    )(z, after, keep, got)


def up_kernel(
    small_hbm, scale_hbm, given_hbm, out_hbm, small, scale, cot, out, first_sem, sem, out_sem
):
    width = cot.shape[2]
    chunks = chunks_of(width)
    first = begin(small_hbm, small, first_sem.at[0]), begin(scale_hbm, scale, first_sem.at[1])
    ready = stream([(given_hbm, cot)], sem, chunks, 3)
    for copy in first:
        copy.wait()
    proj = [small[RANK * k : RANK * k + RANK, :] for k in range(4)]
    proj = jnp.concatenate(proj, axis=1) * adapter_scale
    factors = scale[:32, :]
    stores = []
    for j, (at, size) in enumerate(chunks):
        ready(j)
        cols = slice(at, at + size)
        value = cot[:, :, cols].reshape(512, size).astype(f32)
        grad = (value * in_line(factors, at, size)).astype(bf16)
        out[:, cols] = three(proj, grad, 1, 0)
        stores.append(begin(out.at[:, cols], out_hbm.at[:, cols], out_sem.at[j]))
    for copy in stores:
        copy.wait()


def up_gradient_of(small, scale, given):
    width = given.shape[2]
    count = len(chunks_of(width))
    return call(
        up_kernel,
        2 * 512 * 256 * width,
        4 * MIB,
        in_specs=[ANY] * 3,
        out_specs=ANY,
        out_shape=jax.ShapeDtypeStruct((RANK, width), f32),
        scratch_shapes=[
            pltpu.VMEM(small.shape, f32),
            pltpu.VMEM(scale.shape, f32),
            pltpu.VMEM(given.shape, bf16),
            pltpu.VMEM((RANK, width), f32),
            pltpu.SemaphoreType.DMA((2,)),
            pltpu.SemaphoreType.DMA((1, count)),
            pltpu.SemaphoreType.DMA((count,)),
        ],
        name="up_gradient",
    )(small, scale, given)


def finish_kernel(z_ref, tokens_hbm, scale_hbm, parts_hbm, *refs):
    blocks_hbm, (grad_hbm, down_hbm, out_hbm, mag_hbm) = refs[:4], refs[4:8]
    blocks, tokens, lows, grad, down, scale, parts, out, mag = refs[8:17]
    block_sem, first_sem, sem, out_sem = refs[17:]
    half = z_ref[0] // 2
    width = out.shape[1]
    chunks = chunks_of(width)
    count = width // LANES
    copies = [begin(blocks_hbm[k], blocks.at[k], block_sem.at[k]) for k in range(4)]
    later = (
        begin(tokens_hbm, tokens, first_sem.at[0]),
        begin(scale_hbm, scale, first_sem.at[1]),
        begin(parts_hbm.at[:, :, width:], parts.at[:, :, width:], first_sem.at[2]),
    )
    ready = stream([(parts_hbm, parts.at[:, :, :width])], sem, chunks, len(chunks))
    for copy in copies:
        copy.wait()
    total = blocks[0, :32, :].astype(f32)
    for k in range(1, 4):
        total += blocks[k, :32, :].astype(f32)
    grad[...] = total.astype(bf16)
    stores = [begin(grad, grad_hbm, block_sem.at[0])]
    for k in range(4):
        lows[lax.rem(half + 4 - k, 4)] = unpack(blocks[k, 32:48, :])
    low = (lows[0] + lows[1]) + (lows[2] + lows[3])
    for copy in later:
        copy.wait()
    down[...] = three(low * adapter_scale, tokens[...], 1, 0)
    stores.append(begin(down, down_hbm, block_sem.at[1]))

    def summed(cols):
        total = parts[0, :, cols].astype(f32)
        for r in range(1, 16):
            total += parts[r, :, cols].astype(f32)
        return total

    mag[...] = summed(slice(width, width + LANES))[:count] / scale[32 : 32 + count, :]
    stores.append(begin(mag, mag_hbm, block_sem.at[2]))
    factors = scale[:32, :]
    for j, (at, size) in enumerate(chunks):
        ready(j)
        cols = slice(at, at + size)
        out[:, cols] = (summed(cols) * in_line(factors, at, size)).astype(bf16)
        stores.append(begin(out.at[:, cols], out_hbm.at[:, cols], out_sem.at[j]))
    for copy in stores:
        copy.wait()


def finish(z, tokens, scale, parts, blocks):
    depth = tokens.shape[1]
    width = parts.shape[2] - LANES
    count = len(chunks_of(width))
    return call(
        finish_kernel,
        2 * 512 * 256 * depth,
        6 * MIB,
        in_specs=[SMEM] + [ANY] * 7,
        out_specs=[ANY] * 4,
        out_shape=[
            jax.ShapeDtypeStruct((32, depth), bf16),
            jax.ShapeDtypeStruct((RANK, depth), f32),
            jax.ShapeDtypeStruct((32, width), bf16),
            jax.ShapeDtypeStruct((width // LANES, LANES), f32),
        ],
        scratch_shapes=[
            pltpu.VMEM((4, 48, depth), bf16),
            pltpu.VMEM(tokens.shape, bf16),
            pltpu.VMEM((4, RANK, CHUNK), f32),
            pltpu.VMEM((32, depth), bf16),
            pltpu.VMEM((RANK, depth), f32),
            pltpu.VMEM(scale.shape, f32),
            pltpu.VMEM(parts.shape, bf16),
            pltpu.VMEM((32, width), bf16),
            pltpu.VMEM((width // LANES, LANES), f32),
            pltpu.SemaphoreType.DMA((4,)),
            pltpu.SemaphoreType.DMA((3,)),
            pltpu.SemaphoreType.DMA((1, count)),
            pltpu.SemaphoreType.DMA((count,)),
        ],
        name="finish",
    )(z, tokens, scale, parts, *blocks)


def exchange(blocks):
    return lax.all_to_all(blocks, ROW, 0, 0, tiled=False)


def further(value, axis, k, size):
    return lax.ppermute(value, axis, [(i, (i + k) % size) for i in range(size)])


def shifted(value, axis):
    return [further(value, axis, k, 4) for k in (1, 2, 3)]


def added(value, arrived):
    one, two, other = arrived
    return (value + two) + (one + other)


def on_device(tokens, weight, down_adapter, up_adapter, magnitude, out_cotangent):
    z, core = [lax.axis_index(name).astype(jnp.int32).reshape(1) for name in COL]
    swap = [(0, 1), (1, 0)]
    down_t = down_adapter.T
    magnitude = magnitude.reshape(-1, LANES)
    given = exchange(spread(out_cotangent))
    beside = [(i, i ^ 1) for i in range(8)]
    two = jnp.concatenate([tokens, lax.ppermute(tokens, "z", beside)], axis=0)
    own = [two] + [further(two, "z", 2 * k, 8) for k in (1, 2, 3)]
    merged_low, sums = merge(two, down_t, up_adapter, weight)
    own = jnp.concatenate(own, axis=0)
    other = lax.ppermute(own, "c", swap)
    place = jnp.concatenate([z, core])
    small, tokens_full = project(place, own, other, down_t, sums)
    tokens_full = tokens_full.reshape(512, -1)
    part = forward(tokens_full, merged_low)
    arrived = shifted(small, "x")
    arrived, part = lax.optimization_barrier((arrived, part))
    small = added(small, arrived)
    part = add_magnitude(given, part)
    arrived = shifted(small, "y")
    arrived, part = lax.optimization_barrier((arrived, part))
    parts = exchange(part)
    small = added(small, arrived)
    own, send, scale = backward(core, small, magnitude, up_adapter, given, merged_low)
    got = lax.ppermute(send, "c", swap)
    keep, send = pair(z, own, got)
    got = lax.ppermute(send, "z", beside)
    up_gradient = up_gradient_of(small, scale, given)
    blocks = list(quad(z, up_gradient, keep, got))
    for k in (2, 1, 3):
        blocks[k] = further(blocks[k], "z", 2 * k, 8)
    grad_tokens, down_gradient, output, grad_magnitude = finish(
        z, tokens_full, scale, parts, blocks
    )
    return (output, grad_tokens, grad_magnitude.reshape(-1), up_gradient, down_gradient.T)


def solution(mesh):
    split = Mesh(mesh.devices.reshape(4, 4, 8, 2), ROW + COL)
    return jax.shard_map(
        on_device,
        mesh=split,
        in_specs=(P(COL, ROW), P(ROW, COL), P(ROW, None), P(None, COL), P(COL), P(ROW, COL)),
        out_specs=(P(ROW, COL), P(COL, ROW), P(COL), P(None, COL), P(ROW, None)),
        check_vma=False,
    )
```
